128 devices in a mesh: lon: 16 (over y, z_lo, core), lat: 2 (over z_hi), dp: 4 (over x).
Axes of the slice: x: 4, y: 4, z: 4 (z_hi: 2, z_lo: 2; z = z_hi * 2 + z_lo), core: 2. Of those that a mesh axis runs over, the one named last changes fastest.
Arguments:
- inputs: bfloat16 [4, 24, 576, 1024], P('dp', 'lat', 'lon'), may hold values from -6 to 6
- cotangent: bfloat16 [4, 24, 576, 1024], P('dp', 'lat', 'lon'), may hold values from -0.59765625 to 0.59765625
- qkv_weight: bfloat16 [2, 1024, 3072], replicated, may hold values from -0.1875 to 0.1875
- out_weight: bfloat16 [2, 1024, 1024], replicated, may hold values from -0.1875 to 0.1875
- norm_gain: float32 [2, 1024], replicated, may hold values from 0.5 to 1.5
- position_bias: float32 [2, 16, 144, 144], replicated, may hold values from -4 to 302
- region_ids: int32 [24, 576], P('lat', 'lon'), may hold values from 0 to 8, as said below
Outputs:
- grad_inputs: bfloat16 [4, 24, 576, 1024], P('dp', 'lat', 'lon')
- grad_out_weight: float32 [2, 1024, 1024], P(None, ('lon', 'lat', 'dp'))
- grad_gain: float32 [2, 1024], P(None, ('lon', 'lat', 'dp'))
The draws below stay inside these ranges and needn't reach their ends.
Inputs may be any that keep to these rules, and one draw needn't show every extreme that they name: `region_ids`: the shifted frame is cut into 3 x 3 regions by the latitude rows 12 and 18 and the longitude columns 564 and 570; all tokens of one region carry one label, and two regions may carry the same label.
All inputs are finite; a program needn't handle non-finite values.
Results may differ from the reference program's by a relative error of at most 0.019.
Values may be sent and summed in bfloat16 or wider, within the bound.
No kernel may reach another device: no remote copies, remote signals or barrier semaphores. Data moves between devices by JAX's collectives and lax.ppermute only.
A program may use at most 192 MiB of HBM per device.

```python
import jax
import jax.numpy as jnp
from jax import lax

D = 1024
HEADS = 16
WIN = 12
REGIONS = 9
LAYERS = 2
BATCH = 4
NLAT = 24
NLON = 576


def draw_position_bias(key, part):
    key = jax.random.fold_in(key, 11)
    shape = (LAYERS, HEADS, WIN * WIN, WIN * WIN)
    return jnp.clip(jax.random.normal(key, shape, jnp.float32), -4.0, 4.0)


def draw_region_ids(key, part):
    key = jax.random.fold_in(key, 13)
    order = jax.random.permutation(jax.random.fold_in(key, 1), 9).astype(jnp.int32)
    loose = jax.random.randint(jax.random.fold_in(key, 2), (9,), 0, REGIONS).astype(jnp.int32)
    table = jnp.where(order == 0, 0, jnp.where(order == 8, REGIONS - 1, loose)).astype(jnp.int32)
    lat_index = lax.broadcasted_iota(jnp.int32, (NLAT, NLON), 0)
    lon_index = lax.broadcasted_iota(jnp.int32, (NLAT, NLON), 1)
    lat_band = (lat_index >= NLAT - WIN).astype(jnp.int32) + (lat_index >= NLAT - WIN // 2).astype(jnp.int32)
    lon_band = (lon_index >= NLON - WIN).astype(jnp.int32) + (lon_index >= NLON - WIN // 2).astype(jnp.int32)
    region = 3 * lat_band + lon_band
    slots = lax.broadcasted_iota(jnp.int32, (NLAT, NLON, 9), 2)
    return jnp.sum(jnp.where(region[:, :, None] == slots, table[None, None, :], 0), -1).astype(jnp.int32)


def shard_levels(stream_key, dims, cuts, low, top_value):
    loudness = 1.0
    for position, shards_of in cuts:
        steps = jax.random.uniform(jax.random.fold_in(jax.random.fold_in(stream_key, 6), position), (shards_of,), jnp.float32, low / len(cuts), top_value / len(cuts))
        loudness = loudness * jnp.repeat(jnp.exp(steps), dims[position] // shards_of).reshape((-1,) + (1,) * (len(dims) - 1 - position))
    return loudness


def gaussian(own_key, extent, spread, most, pieces=(), kind=jnp.bfloat16):
    entries = spread * jax.random.normal(own_key, extent, jnp.float32)
    if pieces:
        entries = entries * shard_levels(own_key, extent, pieces, -0.22, 0.18)
    return jnp.clip(entries, -most, most).astype(kind)


def setup_inputs(seed: int = 0) -> dict:
    arg_keys = jax.random.split(jax.random.key(seed), 8)
    inputs = gaussian(arg_keys[0], (BATCH, NLAT, NLON, D), 1.0, 6.0, ((0, 4), (1, 2), (2, 16)))
    cotangent = gaussian(arg_keys[1], (BATCH, NLAT, NLON, D), 0.1, 0.59765625, ((0, 4), (1, 2), (2, 16)))
    qkv_weight = gaussian(arg_keys[2], (LAYERS, D, 3 * D), D ** -0.5, 0.1875)
    out_weight = gaussian(arg_keys[3], (LAYERS, D, D), D ** -0.5, 0.1875)
    norm_gain = jnp.clip(1.0 + 0.1 * jax.random.normal(arg_keys[4], (LAYERS, D), jnp.float32), 0.5, 1.5)
    position_bias = draw_position_bias(jax.random.fold_in(arg_keys[7], 71), 0)
    region_ids = draw_region_ids(jax.random.fold_in(arg_keys[7], 71), 0)
    return dict(inputs=inputs, cotangent=cotangent, qkv_weight=qkv_weight, out_weight=out_weight, norm_gain=norm_gain, position_bias=position_bias, region_ids=region_ids)


def widen(array):
    return lax.optimization_barrier(array).astype(jnp.float32)

def windows(tokens, window):
    samples, lat_rows, lon_cols, width = tokens.shape
    tokens = tokens.reshape(samples, lat_rows // window, window, lon_cols // window, window, width)
    tokens = tokens.transpose(0, 1, 3, 2, 4, 5)
    return tokens.reshape(samples, lat_rows // window * (lon_cols // window), window * window, width)

def tokens_back(blocks, lat_rows, lon_cols, window):
    samples, number, window_area, width = blocks.shape
    blocks = blocks.reshape(samples, lat_rows // window, lon_cols // window, window, window, width)
    blocks = blocks.transpose(0, 1, 3, 2, 4, 5)
    return blocks.reshape(samples, lat_rows, lon_cols, width)

def normalize(tokens, scale_gain):
    widened = tokens.astype(jnp.float32)
    average = lax.optimization_barrier(jnp.mean(widened, -1, keepdims=True))
    centred = widened - average
    inv_std = lax.rsqrt(lax.optimization_barrier(jnp.mean(centred * centred, -1, keepdims=True)) + 1e-05)
    standard = centred * inv_std
    return (standard, inv_std, (standard * scale_gain).astype(jnp.bfloat16))

def probabilities(queries, key_vecs, rel_bias, allowed, factor):
    scores = jnp.einsum('bnqhd,bnkhd->bnhqk', widen(queries), widen(key_vecs)) * factor + rel_bias
    if allowed is not None:
        scores = jnp.where(allowed[:, :, None], scores, -1000000000.0)
    row_max = lax.optimization_barrier(jnp.max(scores, -1, keepdims=True))
    expo = jnp.exp(scores - row_max)
    return expo / lax.optimization_barrier(jnp.sum(expo, -1, keepdims=True))

def forward(tokens, proj_in, proj_out, scale_gain, rel_bias, allowed, window):
    samples, lat_rows, lon_cols, width = tokens.shape
    head_count = rel_bias.shape[0]
    head_size = width // head_count
    standard, inv_std, normed = normalize(tokens, scale_gain)
    packed = jnp.dot(normed.reshape(-1, width), proj_in, preferred_element_type=jnp.float32).astype(jnp.bfloat16)
    packed = windows(packed.reshape(samples, lat_rows, lon_cols, 3 * width), window)
    number = packed.shape[1]
    window_area = window * window
    queries = packed[..., :width].reshape(samples, number, window_area, head_count, head_size)
    key_vecs = packed[..., width:2 * width].reshape(samples, number, window_area, head_count, head_size)
    values = packed[..., 2 * width:].reshape(samples, number, window_area, head_count, head_size)
    attn_probs = probabilities(queries, key_vecs, rel_bias, allowed, head_size ** (-0.5))
    rounded = attn_probs.astype(jnp.bfloat16)
    blended = jnp.einsum('bnhqk,bnkhd->bnqhd', widen(rounded), widen(values)).astype(jnp.bfloat16)
    attended = tokens_back(blended.reshape(samples, number, window_area, width), lat_rows, lon_cols, window)
    flat_att = attended.reshape(-1, width)
    projected = jnp.dot(flat_att, proj_out, preferred_element_type=jnp.float32).reshape(samples, lat_rows, lon_cols, width)
    block_out = (tokens.astype(jnp.float32) + projected).astype(jnp.bfloat16)
    return (block_out, (standard, inv_std, queries, key_vecs, values, attn_probs, rounded, flat_att))

def backward(saved, grad, proj_in, proj_out, scale_gain, window):
    standard, inv_std, queries, key_vecs, values, attn_probs, rounded, flat_att = saved
    samples, lat_rows, lon_cols, width = grad.shape
    number, window_area, head_count, head_size = queries.shape[1:]
    grad_rows = grad.reshape(-1, width)
    out_grad = lax.dot_general(flat_att, grad_rows, (((0,), (0,)), ((), ())), preferred_element_type=jnp.float32)
    d_att = lax.dot_general(grad_rows, proj_out, (((1,), (1,)), ((), ())), preferred_element_type=jnp.float32).astype(jnp.bfloat16)
    d_att = windows(d_att.reshape(samples, lat_rows, lon_cols, width), window)
    d_att = d_att.reshape(samples, number, window_area, head_count, head_size)
    d_values = jnp.einsum('bnhqk,bnqhd->bnkhd', widen(rounded), widen(d_att)).astype(jnp.bfloat16)
    d_probs = jnp.einsum('bnqhd,bnkhd->bnhqk', widen(d_att), widen(values))
    d_scores = attn_probs * (d_probs - lax.optimization_barrier(jnp.sum(d_probs * attn_probs, -1, keepdims=True)))
    d_scaled = (d_scores * head_size ** (-0.5)).astype(jnp.bfloat16)
    d_query = jnp.einsum('bnhqk,bnkhd->bnqhd', widen(d_scaled), widen(key_vecs)).astype(jnp.bfloat16)
    d_keys = jnp.einsum('bnhqk,bnqhd->bnkhd', widen(d_scaled), widen(queries)).astype(jnp.bfloat16)
    d_packed = jnp.concatenate([d_query.reshape(samples, number, window_area, width), d_keys.reshape(samples, number, window_area, width), d_values.reshape(samples, number, window_area, width)], -1)
    d_packed = tokens_back(d_packed, lat_rows, lon_cols, window).reshape(-1, 3 * width)
    d_norm = lax.dot_general(d_packed, proj_in, (((1,), (1,)), ((), ())), preferred_element_type=jnp.float32)
    d_norm = d_norm.reshape(samples, lat_rows, lon_cols, width)
    gain_grad = lax.optimization_barrier(jnp.sum(d_norm * standard, axis=(0, 1, 2)))
    d_hat = d_norm * scale_gain
    d_x = inv_std * (d_hat - lax.optimization_barrier(jnp.mean(d_hat, -1, keepdims=True)) - standard * lax.optimization_barrier(jnp.mean(d_hat * standard, -1, keepdims=True)))
    d_in = (grad.astype(jnp.float32) + d_x).astype(jnp.bfloat16)
    return (d_in, out_grad, gain_grad)

def reference(inputs, cotangent, qkv_weight, out_weight, norm_gain, position_bias, region_ids):
    offset = WIN // 2
    labels = windows(region_ids[None, :, :, None], WIN)[..., 0]
    allowed = labels[:, :, :, None] == labels[:, :, None, :]

    def per_sample(totals, sample_pair):
        sample_in = sample_pair[0][None]
        sample_grad = sample_pair[1][None]
        first_out, saved_first = forward(sample_in, qkv_weight[0], out_weight[0], norm_gain[0], position_bias[0], None, WIN)
        shifted = jnp.roll(first_out, (-offset, -offset), (1, 2))
        unused, saved_second = forward(shifted, qkv_weight[1], out_weight[1], norm_gain[1], position_bias[1], allowed, WIN)
        shifted_grad = jnp.roll(sample_grad, (-offset, -offset), (1, 2))
        back_second, out_second, gain_second = backward(saved_second, shifted_grad, qkv_weight[1], out_weight[1], norm_gain[1], WIN)
        back_first = jnp.roll(back_second, (offset, offset), (1, 2))
        result, out_first, gain_first = backward(saved_first, back_first, qkv_weight[0], out_weight[0], norm_gain[0], WIN)
        new_totals = (totals[0] + jnp.stack([out_first, out_second]), totals[1] + jnp.stack([gain_first, gain_second]))
        return (new_totals, result[0])
    zero_sums = (jnp.zeros((LAYERS, D, D), jnp.float32), jnp.zeros((LAYERS, D), jnp.float32))
    sums, grad_inputs = lax.scan(per_sample, zero_sums, (inputs, cotangent))
    return (grad_inputs, sums[0], sums[1])
```

```python
import jax
import jax.numpy as jnp
from jax import lax
from jax.sharding import PartitionSpec as P

WIN = 12


def passed_along(value, axis, steps):
    count = lax.axis_size(axis)
    pairs = [(source, (source + steps) % count) for source in range(count)]
    return lax.ppermute(value, axis, pairs)


def windows(tokens, window):
    samples, lat_rows, lon_cols, width = tokens.shape
    tokens = tokens.reshape(samples, lat_rows // window, window, lon_cols // window, window, width)
    tokens = tokens.transpose(0, 1, 3, 2, 4, 5)
    return tokens.reshape(
        samples, lat_rows // window * (lon_cols // window), window * window, width
    )


def tokens_back(blocks, lat_rows, lon_cols, window):
    samples, number, window_area, width = blocks.shape
    blocks = blocks.reshape(samples, lat_rows // window, lon_cols // window, window, window, width)
    blocks = blocks.transpose(0, 1, 3, 2, 4, 5)
    return blocks.reshape(samples, lat_rows, lon_cols, width)


def normalize(tokens, scale_gain):
    widened = tokens.astype(jnp.float32)
    average = jnp.mean(widened, -1, keepdims=True)
    centred = widened - average
    inv_std = lax.rsqrt(jnp.mean(centred * centred, -1, keepdims=True) + 1e-05)
    standard = centred * inv_std
    return (standard, inv_std, (standard * scale_gain).astype(jnp.bfloat16))


def probabilities(queries, key_vecs, rel_bias, allowed, factor):
    scores = (
        jnp.einsum("bnqhd,bnkhd->bnhqk", queries, key_vecs, preferred_element_type=jnp.float32)
        * factor
        + rel_bias
    )
    if allowed is not None:
        scores = jnp.where(allowed[:, :, None], scores, -1000000000.0)
    row_max = jnp.max(scores, -1, keepdims=True)
    expo = jnp.exp(scores - row_max)
    return expo / jnp.sum(expo, -1, keepdims=True)


def forward(tokens, proj_in, proj_out, scale_gain, rel_bias, allowed, window):
    samples, lat_rows, lon_cols, width = tokens.shape
    head_count = rel_bias.shape[0]
    head_size = width // head_count
    standard, inv_std, normed = normalize(tokens, scale_gain)
    packed = jnp.dot(normed.reshape(-1, width), proj_in, preferred_element_type=jnp.float32).astype(
        jnp.bfloat16
    )
    packed = windows(packed.reshape(samples, lat_rows, lon_cols, 3 * width), window)
    number = packed.shape[1]
    window_area = window * window
    queries = packed[..., :width].reshape(samples, number, window_area, head_count, head_size)
    key_vecs = packed[..., width : 2 * width].reshape(
        samples, number, window_area, head_count, head_size
    )
    values = packed[..., 2 * width :].reshape(samples, number, window_area, head_count, head_size)
    attn_probs = probabilities(queries, key_vecs, rel_bias, allowed, head_size ** (-0.5))
    rounded = attn_probs.astype(jnp.bfloat16)
    blended = jnp.einsum(
        "bnhqk,bnkhd->bnqhd", rounded, values, preferred_element_type=jnp.float32
    ).astype(jnp.bfloat16)
    attended = tokens_back(
        blended.reshape(samples, number, window_area, width), lat_rows, lon_cols, window
    )
    flat_att = attended.reshape(-1, width)
    projected = jnp.dot(flat_att, proj_out, preferred_element_type=jnp.float32).reshape(
        samples, lat_rows, lon_cols, width
    )
    block_out = (tokens.astype(jnp.float32) + projected).astype(jnp.bfloat16)
    return (
        block_out,
        (standard, inv_std, queries, key_vecs, values, attn_probs, rounded, flat_att),
    )


def backward(saved, grad, proj_in, proj_out, scale_gain, window):
    standard, inv_std, queries, key_vecs, values, attn_probs, rounded, flat_att = saved
    samples, lat_rows, lon_cols, width = grad.shape
    number, window_area, head_count, head_size = queries.shape[1:]
    grad_rows = grad.reshape(-1, width)
    out_grad = lax.dot_general(
        flat_att, grad_rows, (((0,), (0,)), ((), ())), preferred_element_type=jnp.float32
    )
    d_att = lax.dot_general(
        grad_rows, proj_out, (((1,), (1,)), ((), ())), preferred_element_type=jnp.float32
    ).astype(jnp.bfloat16)
    d_att = windows(d_att.reshape(samples, lat_rows, lon_cols, width), window)
    d_att = d_att.reshape(samples, number, window_area, head_count, head_size)
    d_values = jnp.einsum(
        "bnhqk,bnqhd->bnkhd", rounded, d_att, preferred_element_type=jnp.float32
    ).astype(jnp.bfloat16)
    d_probs = jnp.einsum("bnqhd,bnkhd->bnhqk", d_att, values, preferred_element_type=jnp.float32)
    d_scores = attn_probs * (d_probs - jnp.sum(d_probs * attn_probs, -1, keepdims=True))
    d_scaled = (d_scores * head_size ** (-0.5)).astype(jnp.bfloat16)
    d_query = jnp.einsum(
        "bnhqk,bnkhd->bnqhd", d_scaled, key_vecs, preferred_element_type=jnp.float32
    ).astype(jnp.bfloat16)
    d_keys = jnp.einsum(
        "bnhqk,bnqhd->bnkhd", d_scaled, queries, preferred_element_type=jnp.float32
    ).astype(jnp.bfloat16)
    d_packed = jnp.concatenate(
        [
            d_query.reshape(samples, number, window_area, width),
            d_keys.reshape(samples, number, window_area, width),
            d_values.reshape(samples, number, window_area, width),
        ],
        -1,
    )
    d_packed = tokens_back(d_packed, lat_rows, lon_cols, window).reshape(-1, 3 * width)
    d_norm = lax.dot_general(
        d_packed, proj_in, (((1,), (1,)), ((), ())), preferred_element_type=jnp.float32
    )
    d_norm = d_norm.reshape(samples, lat_rows, lon_cols, width)
    gain_grad = jnp.sum(d_norm * standard, axis=(0, 1, 2))
    d_hat = d_norm * scale_gain
    d_x = inv_std * (
        d_hat
        - jnp.mean(d_hat, -1, keepdims=True)
        - standard * jnp.mean(d_hat * standard, -1, keepdims=True)
    )
    d_in = (grad.astype(jnp.float32) + d_x).astype(jnp.bfloat16)
    return (d_in, out_grad, gain_grad)


def roll_ahead(tokens):
    offset = WIN // 2
    border = passed_along(tokens[:, :, :offset], "lon", -1)
    tokens = jnp.concatenate([tokens[:, :, offset:], border], 2)
    border = passed_along(tokens[:, :offset], "lat", -1)
    return jnp.concatenate([tokens[:, offset:], border], 1)


def roll_behind(tokens):
    offset = WIN // 2
    border = passed_along(tokens[:, :, -offset:], "lon", 1)
    tokens = jnp.concatenate([border, tokens[:, :, :-offset]], 2)
    border = passed_along(tokens[:, -offset:], "lat", 1)
    return jnp.concatenate([border, tokens[:, :-offset]], 1)


def to_core(value):
    return lax.ppermute(value, "lon", [(i, i ^ 1) for i in range(16)])


def along_x(value, step):
    return lax.ppermute(value, "dp", [(i, (i + step) % 4) for i in range(4)])


def along_y(value, step):
    return lax.ppermute(value, "lon", [(i, (i + 4 * step) % 16) for i in range(16)])


def along_z(value, step):
    near, far = step % 2, step // 2
    pairs = [
        (i * 2 + j, (i ^ (2 * near)) * 2 + (j ^ far)) for i in range(16) for j in range(2)
    ]
    return lax.ppermute(value, ("lon", "lat"), pairs)


def places():
    lon = lax.axis_index("lon")
    return lon // 4, (lon // 2) % 2, lon % 2, lax.axis_index("lat"), lax.axis_index("dp")


def chosen(value, index, axis):
    return lax.dynamic_index_in_dim(value, index, axis, keepdims=False)


def row_share(terms):
    y, near, core, far, x = places()
    layers, rows, width = terms.shape
    parts = terms.reshape(layers, 4, 2, 2, 2, 4, rows // 128, width)
    sent = chosen(parts, 1 - core, 3).astype(jnp.bfloat16)
    parts = chosen(parts, core, 3) + to_core(sent).astype(jnp.float32)
    kept = chosen(parts, x, 4)
    for step in range(1, 4):
        sent = chosen(parts, (x + step) % 4, 4).astype(jnp.bfloat16)
        kept = kept + along_x(sent, step).astype(jnp.float32)
    parts, kept = kept, chosen(kept, y, 1)
    for step in range(1, 4):
        sent = chosen(parts, (y + step) % 4, 1).astype(jnp.bfloat16)
        kept = kept + along_y(sent, step).astype(jnp.float32)
    parts, kept = kept, chosen(chosen(kept, near, 1), far, 1)
    for step in range(1, 4):
        sent = chosen(chosen(parts, near ^ (step % 2), 1), far ^ (step // 2), 1)
        kept = kept + along_z(sent.astype(jnp.bfloat16), step).astype(jnp.float32)
    return kept


def feature_share(terms):
    total = terms + to_core(terms)
    total = total + along_x(total, 1) + along_x(total, 2) + along_x(total, 3)
    total = total + along_y(total, 1) + along_y(total, 2) + along_y(total, 3)
    total = total + along_z(total, 1) + along_z(total, 2) + along_z(total, 3)
    place = (lax.axis_index("lon") * 2 + lax.axis_index("lat")) * 4 + lax.axis_index("dp")
    return lax.dynamic_slice_in_dim(total, place * 8, 8, 1)


def per_device(inputs, cotangent, qkv_weight, out_weight, norm_gain, position_bias, region_ids):
    labels = windows(region_ids[None, :, :, None], WIN)[..., 0]
    allowed = labels[:, :, :, None] == labels[:, :, None, :]
    shifted_grad = roll_ahead(cotangent)
    first_out, saved_first = forward(
        inputs, qkv_weight[0], out_weight[0], norm_gain[0], position_bias[0], None, WIN
    )
    shifted = roll_ahead(first_out)
    unused, saved_second = forward(
        shifted, qkv_weight[1], out_weight[1], norm_gain[1], position_bias[1], allowed, WIN
    )
    back_second, out_second, gain_second = backward(
        saved_second, shifted_grad, qkv_weight[1], out_weight[1], norm_gain[1], WIN
    )
    back_first = roll_behind(back_second)
    result, out_first, gain_first = backward(
        saved_first, back_first, qkv_weight[0], out_weight[0], norm_gain[0], WIN
    )
    out_share = row_share(jnp.stack([out_first, out_second]))
    gain_share = feature_share(jnp.stack([gain_first, gain_second]))
    return (result, out_share, gain_share)


def solution(mesh):
    in_specs = (
        P("dp", "lat", "lon", None),
        P("dp", "lat", "lon", None),
        P(),
        P(),
        P(),
        P(),
        P("lat", "lon"),
    )
    out_specs = (
        P("dp", "lat", "lon", None),
        P(None, ("lon", "lat", "dp"), None),
        P(None, ("lon", "lat", "dp")),
    )
    return jax.shard_map(
        per_device, mesh=mesh, in_specs=in_specs, out_specs=out_specs, check_vma=False
    )
```

```python
import numpy as np

import jax
import jax.numpy as jnp
from jax import lax
from jax.experimental import pallas as pl
from jax.experimental.pallas import tpu as pltpu
from jax.sharding import PartitionSpec as P

WIN = 12
ROWS = 12
COLS = 36
TOKENS = 432
AREA = 144
WINDOWS = 3
WIDTH = 1024
HEADS = 16
PAIRS = 8
LAT, DIAG, LON, EDGES = 192, 48, 48, 288
F32 = jnp.float32
BF16 = jnp.bfloat16
VMEM_LIMIT = 50 * 2**20


def tables():
    win = np.zeros((TOKENS, TOKENS), np.float32)
    local = np.zeros((TOKENS, TOKENS), np.float32)
    edge = np.zeros((TOKENS, EDGES), np.float32)
    send = np.zeros((EDGES, TOKENS), np.float32)
    for row in range(ROWS):
        for col in range(COLS):
            grid = row * COLS + col
            place = col // WIN * AREA + row * WIN + col % WIN
            win[place, grid] = 1
            if row + 6 < ROWS and col + 6 < COLS:
                local[place, grid + 6 * COLS + 6] = 1
            elif row + 6 < ROWS:
                edge[place, LAT + DIAG + row * 6 + col - 30] = 1
            elif col + 6 < COLS:
                edge[place, (row - 6) * 30 + col] = 1
            else:
                edge[place, LAT + (row - 6) * 6 + col - 30] = 1
            if row < 6 and col >= 6:
                send[row * 30 + col - 6, grid] = 1
            elif row < 6:
                send[LAT + row * 6 + col, grid] = 1
            elif col < 6:
                send[LAT + DIAG + (row - 6) * 6 + col, grid] = 1
    return win, local, edge, send


WIN_OF_GRID, LOCAL_OF_GRID, AHEAD_EDGE, SEND_OF_GRID = tables()
LOCAL_OF_WIN = LOCAL_OF_GRID @ WIN_OF_GRID.T
SEND_OF_WIN = SEND_OF_GRID @ WIN_OF_GRID.T


def table(values):
    return jnp.asarray(values, BF16)


def mm(a, b):
    return lax.dot_general(a, b, (((1,), (0,)), ((), ())), preferred_element_type=F32)


def mm_nt(a, b):
    return lax.dot_general(a, b, (((1,), (1,)), ((), ())), preferred_element_type=F32)


def mm_tn(a, b):
    return lax.dot_general(a, b, (((0,), (0,)), ((), ())), preferred_element_type=F32)


def call(kernel, outs, scratch, *args):
    return pl.pallas_call(
        kernel,
        out_shape=[jax.ShapeDtypeStruct(shape, dtype) for shape, dtype in outs],
        in_specs=[pl.BlockSpec(memory_space=pltpu.VMEM)] * len(args),
        out_specs=[pl.BlockSpec(memory_space=pltpu.VMEM)] * len(outs),
        scratch_shapes=scratch,
        compiler_params=pltpu.CompilerParams(vmem_limit_bytes=VMEM_LIMIT),
    )(*args)


def grid_rows(source, flat):
    for row in range(ROWS):
        flat[row * COLS : (row + 1) * COLS, :] = source[0, row].astype(F32)
    return flat[...].astype(BF16)


def standardized(tokens):
    centred = tokens - jnp.mean(tokens, -1, keepdims=True)
    inv_std = lax.rsqrt(jnp.mean(centred * centred, -1, keepdims=True) + 1e-05)
    return centred * inv_std, inv_std


def first_half():
    return lax.broadcasted_iota(jnp.int32, (1, 128), 1) < 64


def halves(pair_values, scale):
    low = first_half()
    low_scale = jnp.where(low, scale, 0.0).astype(BF16)
    high_scale = jnp.where(low, 0.0, scale).astype(BF16)
    return pair_values * low_scale, pair_values * high_scale


def softmax(scores):
    expo = jnp.exp(scores - jnp.max(scores, -1, keepdims=True))
    return expo / jnp.sum(expo, -1, keepdims=True)


def send_edges(send, tokens, lat, diag, lon):
    edges = mm(send, tokens).astype(BF16)
    lat[...] = edges[:LAT]
    diag[...] = edges[LAT : LAT + DIAG]
    lon[...] = edges[LAT + DIAG :]


def joined(local_table, edge_table, local, lat, diag, lon):
    edges = jnp.concatenate([lat[...], diag[...], lon[...]], 0)
    return mm(local_table, local) + mm(edge_table, edges)


def cotangent_kernel(cotangent, send, flat_out, lat, diag, lon, flat):
    tokens = grid_rows(cotangent, flat)
    flat_out[...] = tokens
    send_edges(send[...], tokens, lat, diag, lon)


def first_forward_kernel(
    inputs, to_win, send, proj_in, proj_out, gain, bias,
    out, lat, diag, lon, attended, packed, probs, flat,
):
    tokens = mm(to_win[...], grid_rows(inputs, flat))
    standard, _ = standardized(tokens)
    normed = (standard * gain[0:1, :]).astype(BF16)
    packed[...] = mm(normed, proj_in[0]).astype(BF16)

    def pair_step(pair, carry):
        for window in range(WINDOWS):
            rows = slice(window * AREA, (window + 1) * AREA)
            at = [pl.ds(pl.multiple_of(pair * 128 + WIDTH * n, 128), 128) for n in range(3)]
            query, key, value = (packed[rows, a] for a in at)
            results = []
            for half, key_half in enumerate(halves(key, 0.125)):
                head = 2 * pair + half
                weights = softmax(mm_nt(query, key_half) + bias[0, head]).astype(BF16)
                probs[window, head] = weights
                results.append(mm(weights, value))
            attended[rows, at[0]] = jnp.where(first_half(), *results).astype(BF16)
        return carry

    lax.fori_loop(0, PAIRS, pair_step, 0)
    result = (tokens + mm(attended[...], proj_out[0])).astype(BF16)
    out[...] = result
    send_edges(send[...], result, lat, diag, lon)


def attention_backward(weights, weights_rounded, d_att, query, key, value_half):
    d_probs = mm_nt(d_att, value_half)
    d_scaled = weights * (d_probs - jnp.sum(d_probs * weights, -1, keepdims=True))
    d_scaled = d_scaled.astype(BF16)
    return mm(d_scaled, key), mm_tn(d_scaled, query), mm_tn(weights_rounded, d_att)


def norm_backward(d_norm, standard, inv_std, gain, gain_grad, grad):
    gain_grad[...] = jnp.sum(d_norm * standard, 0, keepdims=True)
    d_hat = d_norm * gain
    d_x = inv_std * (
        d_hat
        - jnp.mean(d_hat, -1, keepdims=True)
        - standard * jnp.mean(d_hat * standard, -1, keepdims=True)
    )
    return (grad + d_x).astype(BF16)


def write_out_grad(attended, grad, kept, sent):
    core = lax.axis_index("lon") % 2
    for pair in range(PAIRS):
        both = mm_tn(attended[:, pair * 128 : (pair + 1) * 128], grad)
        kept[pair] = jnp.where(core == 0, both[:64], both[64:])
        sent[pair] = jnp.where(core == 0, both[64:], both[:64]).astype(BF16)


def second_kernel(
    tokens_in, lat_in, diag_in, lon_in, cot, cot_lat, cot_diag, cot_lon,
    local_win, local_grid, edge, send, proj_in, proj_out, gain, bias, region,
    out, lat, diag, lon, kept, sent, gain_grad,
    packed, d_att, attended, standard, grad, allowed,
):
    tokens = joined(local_win[...], edge[...], tokens_in[...], lat_in, diag_in, lon_in)
    hat, inv_std = standardized(tokens)
    standard[...] = hat
    normed = (hat * gain[1:2, :]).astype(BF16)
    packed[...] = mm(normed, proj_in[1]).astype(BF16)
    grad[...] = joined(local_grid[...], edge[...], cot[...], cot_lat, cot_diag, cot_lon).astype(BF16)
    d_att[...] = mm_nt(grad[...], proj_out[1]).astype(BF16)

    token = lax.broadcasted_iota(jnp.int32, (AREA, 1), 0)
    row_of = (token * 171) >> 11
    col_of = token - 12 * row_of
    pick_row = (row_of == lax.broadcasted_iota(jnp.int32, (AREA, ROWS), 1)).astype(BF16)
    by_row = mm(pick_row, region[...].astype(F32).astype(BF16))
    for window in range(WINDOWS):
        column = lax.broadcasted_iota(jnp.int32, (AREA, COLS), 1)
        picked = jnp.where(column == col_of + 12 * window, by_row, 0.0)
        own = jnp.sum(picked, -1, keepdims=True)
        other = mm_nt(jnp.ones((AREA, COLS), BF16), picked.astype(BF16))
        allowed[window] = (own == other).astype(F32)

    def pair_step(pair, carry):
        for window in range(WINDOWS):
            rows = slice(window * AREA, (window + 1) * AREA)
            at = [pl.ds(pl.multiple_of(pair * 128 + WIDTH * n, 128), 128) for n in range(3)]
            query, key, value = (packed[rows, a] for a in at)
            d_out = d_att[rows, at[0]]
            keys, values = halves(key, 0.125), halves(value, 0.125)
            results = []
            for half in range(2):
                scores = mm_nt(query, keys[half]) + bias[1, 2 * pair + half]
                weights = softmax(jnp.where(allowed[window] > 0.5, scores, -1e9))
                rounded = weights.astype(BF16)
                result = mm(rounded, value)
                back = attention_backward(weights, rounded, d_out, query, key, values[half])
                results.append((result,) + back)
            merged = [jnp.where(first_half(), a, b).astype(BF16) for a, b in zip(*results)]
            attended[rows, at[0]] = merged[0]
            for n in range(3):
                packed[rows, at[n]] = merged[1 + n]
        return carry

    lax.fori_loop(0, PAIRS, pair_step, 0)
    write_out_grad(attended, grad[...], kept, sent)
    d_norm = mm_nt(packed[...], proj_in[1])
    result = norm_backward(
        d_norm, standard[...], inv_std, gain[1:2, :], gain_grad, grad[...].astype(F32)
    )
    out[...] = result
    send_edges(send[...], result, lat, diag, lon)


def first_grad_kernel(
    back, lat_in, diag_in, lon_in, local, edge, proj_out, attended,
    grad, d_att, kept, sent,
):
    grad[...] = joined(local[...], edge[...], back[...], lat_in, diag_in, lon_in).astype(BF16)
    write_out_grad(attended, grad[...], kept, sent)
    d_att[...] = mm_nt(grad[...], proj_out[0]).astype(BF16)


def first_backward_kernel(
    inputs, to_win, to_grid, grad, d_att, packed_in, probs, proj_in, gain,
    out, gain_grad, flat, packed,
):
    def pair_step(pair, carry):
        for window in range(WINDOWS):
            rows = slice(window * AREA, (window + 1) * AREA)
            at = [pl.ds(pl.multiple_of(pair * 128 + WIDTH * n, 128), 128) for n in range(3)]
            query, key, value = (packed_in[rows, a] for a in at)
            d_out = d_att[rows, at[0]]
            results = []
            for half, value_half in enumerate(halves(value, 0.125)):
                rounded = probs[window, 2 * pair + half]
                results.append(
                    attention_backward(rounded.astype(F32), rounded, d_out, query, key, value_half)
                )
            merged = [jnp.where(first_half(), a, b).astype(BF16) for a, b in zip(*results)]
            for n in range(3):
                packed[rows, at[n]] = merged[n]
        return carry

    lax.fori_loop(0, PAIRS, pair_step, 0)
    d_norm = mm_nt(packed[...], proj_in[0])
    standard, inv_std = standardized(mm(to_win[...], grid_rows(inputs, flat)))
    result = norm_backward(
        d_norm, standard, inv_std, gain[0:1, :], gain_grad, grad[...].astype(F32)
    )
    flat[...] = mm(to_grid[...], result)
    for row in range(ROWS):
        out[0, row] = flat[row * COLS : (row + 1) * COLS, :].astype(BF16)


def over_lat(value):
    return lax.ppermute(value, "lat", [(0, 1), (1, 0)])


def over_lon(value, step):
    return lax.ppermute(value, "lon", [(i, (i + step) % 16) for i in range(16)])


def over_both(value, step):
    pairs = [(i * 2 + j, (i + step) % 16 * 2 + 1 - j) for i in range(16) for j in range(2)]
    return lax.ppermute(value, ("lon", "lat"), pairs)


def exchanged(lat, diag, lon, step):
    return over_lat(lat), over_both(diag, step), over_lon(lon, step)


def to_core(value):
    return lax.ppermute(value, "lon", [(i, i ^ 1) for i in range(16)])


def along_x(value, step):
    return lax.ppermute(value, "dp", [(i, (i + step) % 4) for i in range(4)])


def along_y(value, step):
    return lax.ppermute(value, "lon", [(i, (i + 4 * step) % 16) for i in range(16)])


def along_z(value, step):
    near, far = step % 2, step // 2
    pairs = [
        (i * 2 + j, (i ^ (2 * near)) * 2 + (j ^ far)) for i in range(16) for j in range(2)
    ]
    return lax.ppermute(value, ("lon", "lat"), pairs)


def places():
    lon = lax.axis_index("lon")
    return lon // 4, (lon // 2) % 2, lax.axis_index("lat"), lax.axis_index("dp")


def chosen(value, index, axis):
    return lax.dynamic_index_in_dim(value, index, axis, keepdims=False)


def row_share(kept, sent):
    y, near, far, x = places()
    parts = kept + to_core(sent).astype(F32)
    parts = parts.reshape(4, 2, 2, 4, 8, WIDTH)
    kept = chosen(parts, x, 3)
    for step in range(1, 4):
        sent = chosen(parts, (x + step) % 4, 3).astype(BF16)
        kept = kept + along_x(sent, step).astype(F32)
    parts, kept = kept, chosen(kept, y, 0)
    for step in range(1, 4):
        sent = chosen(parts, (y + step) % 4, 0).astype(BF16)
        kept = kept + along_y(sent, step).astype(F32)
    parts, kept = kept, chosen(chosen(kept, near, 0), far, 0)
    for step in range(1, 4):
        sent = chosen(chosen(parts, near ^ (step % 2), 0), far ^ (step // 2), 0)
        kept = kept + along_z(sent.astype(BF16), step).astype(F32)
    return kept


def feature_share(terms):
    total = terms + to_core(terms)
    total = total + along_x(total, 1) + along_x(total, 2) + along_x(total, 3)
    total = total + along_y(total, 1) + along_y(total, 2) + along_y(total, 3)
    total = total + along_z(total, 1) + along_z(total, 2) + along_z(total, 3)
    place = (lax.axis_index("lon") * 2 + lax.axis_index("lat")) * 4 + lax.axis_index("dp")
    return lax.dynamic_slice_in_dim(total, place * 8, 8, 1)


EDGE_OUTS = [((LAT, WIDTH), BF16), ((DIAG, WIDTH), BF16), ((LON, WIDTH), BF16)]
HALF_OUTS = [((PAIRS, 64, WIDTH), F32), ((PAIRS, 64, WIDTH), BF16)]
FLAT_OUT = ((TOKENS, WIDTH), BF16)
PACKED_OUT = ((TOKENS, 3 * WIDTH), BF16)


def per_device(inputs, cotangent, qkv_weight, out_weight, norm_gain, position_bias, region_ids):
    flat = pltpu.VMEM((TOKENS, WIDTH), F32)
    cot, *cot_edges = call(
        cotangent_kernel, [FLAT_OUT] + EDGE_OUTS, [flat], cotangent, table(SEND_OF_GRID)
    )
    cot_edges = exchanged(*cot_edges, -1)
    first_out, lat, diag, lon, attended, packed, probs = call(
        first_forward_kernel,
        [FLAT_OUT] + EDGE_OUTS + [FLAT_OUT, PACKED_OUT, ((WINDOWS, HEADS, AREA, AREA), BF16)],
        [flat],
        inputs, table(WIN_OF_GRID), table(SEND_OF_WIN), qkv_weight, out_weight, norm_gain,
        position_bias,
    )
    edges = exchanged(lat, diag, lon, -1)
    back, lat, diag, lon, kept_second, sent_second, gain_second = call(
        second_kernel,
        [FLAT_OUT] + EDGE_OUTS + HALF_OUTS + [((1, WIDTH), F32)],
        [
            pltpu.VMEM((TOKENS, 3 * WIDTH), BF16),
            pltpu.VMEM((TOKENS, WIDTH), BF16),
            pltpu.VMEM((TOKENS, WIDTH), BF16),
            flat,
            pltpu.VMEM((TOKENS, WIDTH), BF16),
            pltpu.VMEM((WINDOWS, AREA, AREA), F32),
        ],
        first_out, *edges, cot, *cot_edges, table(LOCAL_OF_WIN), table(LOCAL_OF_GRID),
        table(AHEAD_EDGE), table(AHEAD_EDGE.T), qkv_weight, out_weight, norm_gain, position_bias,
        region_ids,
    )
    edges = exchanged(lat, diag, lon, 1)
    share_second = row_share(kept_second, sent_second)
    grad, d_att, kept_first, sent_first = call(
        first_grad_kernel,
        [FLAT_OUT, FLAT_OUT] + HALF_OUTS,
        [],
        back, *edges, table(LOCAL_OF_WIN.T), table(SEND_OF_WIN.T), out_weight, attended,
    )
    share_first = row_share(kept_first, sent_first)
    result, gain_first = call(
        first_backward_kernel,
        [((1, ROWS, COLS, WIDTH), BF16), ((1, WIDTH), F32)],
        [flat, pltpu.VMEM((TOKENS, 3 * WIDTH), BF16)],
        inputs, table(WIN_OF_GRID), table(WIN_OF_GRID.T), grad, d_att, packed, probs, qkv_weight,
        norm_gain,
    )
    gain_share = feature_share(jnp.concatenate([gain_first, gain_second], 0))
    return result, jnp.stack([share_first, share_second]), gain_share


def solution(mesh):
    in_specs = (
        P("dp", "lat", "lon", None),
        P("dp", "lat", "lon", None),
        P(),
        P(),
        P(),
        P(),
        P("lat", "lon"),
    )
    out_specs = (
        P("dp", "lat", "lon", None),
        P(None, ("lon", "lat", "dp"), None),
        P(None, ("lon", "lat", "dp")),
    )
    return jax.shard_map(
        per_device, mesh=mesh, in_specs=in_specs, out_specs=out_specs, check_vma=False
    )
```

```python
import functools

import numpy as np

import jax
import jax.numpy as jnp
from jax import lax
from jax.experimental import pallas as pl
from jax.experimental.pallas import tpu as pltpu
from jax.sharding import PartitionSpec as P

WIN = 12
ROWS = 12
COLS = 36
TOKENS = 432
AREA = 144
WINDOWS = 3
WIDTH = 1024
HEADS = 16
PAIRS = 8
QUAD = 4
LAT, DIAG, LON, EDGES = 192, 48, 48, 288
F32 = jnp.float32
BF16 = jnp.bfloat16
VMEM_LIMIT = 26 * 2**20


def tables():
    win = np.zeros((TOKENS, TOKENS), np.float32)
    local = np.zeros((TOKENS, TOKENS), np.float32)
    edge = np.zeros((TOKENS, EDGES), np.float32)
    send = np.zeros((EDGES, TOKENS), np.float32)
    for row in range(ROWS):
        for col in range(COLS):
            grid = row * COLS + col
            place = col // WIN * AREA + row * WIN + col % WIN
            win[place, grid] = 1
            if row + 6 < ROWS and col + 6 < COLS:
                local[place, grid + 6 * COLS + 6] = 1
            elif row + 6 < ROWS:
                edge[place, LAT + DIAG + row * 6 + col - 30] = 1
            elif col + 6 < COLS:
                edge[place, (row - 6) * 30 + col] = 1
            else:
                edge[place, LAT + (row - 6) * 6 + col - 30] = 1
            if row < 6 and col >= 6:
                send[row * 30 + col - 6, grid] = 1
            elif row < 6:
                send[LAT + row * 6 + col, grid] = 1
            elif col < 6:
                send[LAT + DIAG + (row - 6) * 6 + col, grid] = 1
    return win, local, edge, send


WIN_OF_GRID, LOCAL_OF_GRID, AHEAD_EDGE, SEND_OF_GRID = tables()
LOCAL_OF_WIN = LOCAL_OF_GRID @ WIN_OF_GRID.T
SEND_OF_WIN = SEND_OF_GRID @ WIN_OF_GRID.T


def table(values):
    return jnp.asarray(values, BF16)


def mm(a, b):
    return lax.dot_general(a, b, (((1,), (0,)), ((), ())), preferred_element_type=F32)


def mm_nt(a, b):
    return lax.dot_general(a, b, (((1,), (1,)), ((), ())), preferred_element_type=F32)


def mm_tn(a, b):
    return lax.dot_general(a, b, (((0,), (0,)), ((), ())), preferred_element_type=F32)


def call(kernel, outs, scratch, args, hbm=(), after=(), micros=10):
    count, last = len(args), len(args) + len(after)
    spaces = [pltpu.HBM if i in hbm else pltpu.VMEM for i in range(count)]
    spaces += [pl.ANY] * len(after)

    args = [
        pltpu.with_memory_space_constraint(arg, pltpu.HBM) if i in hbm else arg
        for i, arg in enumerate(args)
    ]

    def body(*refs):
        kernel(*refs[:count], *refs[last:])

    return pl.pallas_call(
        body,
        out_shape=[jax.ShapeDtypeStruct(shape, dtype) for shape, dtype in outs],
        in_specs=[pl.BlockSpec(memory_space=space) for space in spaces],
        out_specs=[pl.BlockSpec(memory_space=pltpu.VMEM)] * len(outs),
        scratch_shapes=scratch,
        compiler_params=pltpu.CompilerParams(vmem_limit_bytes=VMEM_LIMIT),
        cost_estimate=pl.CostEstimate(
            flops=int(micros * 1.15e9), transcendentals=0, bytes_accessed=2**20
        ),
    )(*args, *after)


def fetch(*copies):
    handles = [pltpu.make_async_copy(*copy) for copy in copies]
    for handle in handles:
        handle.start()
    return handles


def grid_rows(source, flat):
    for row in range(ROWS):
        flat[row * COLS : (row + 1) * COLS, :] = source[0, row].astype(F32)
    return flat[...].astype(BF16)


def standardized(tokens):
    centred = tokens - jnp.mean(tokens, -1, keepdims=True)
    inv_std = lax.rsqrt(jnp.mean(centred * centred, -1, keepdims=True) + 1e-05)
    return centred * inv_std, inv_std


def quarter(width=4 * 64):
    return lax.broadcasted_iota(jnp.int32, (1, width), 1) // 64


def stacked(values):
    parts = [values * jnp.where(quarter() == n, 0.125, 0.0).astype(BF16) for n in range(QUAD)]
    return jnp.concatenate(parts, 0)


def by_head(values):
    return values.reshape(QUAD, AREA, AREA)


def flipped(values):
    return jnp.concatenate([values[n].T for n in range(QUAD)], 0)


def merged(values):
    result = values[:AREA]
    for n in range(1, QUAD):
        result = jnp.where(quarter() == n, values[n * AREA : (n + 1) * AREA], result)
    return result.astype(BF16)


def columns(group, block, width=WIDTH):
    return pl.ds(pl.multiple_of(group * 256 + width * block, 256), 256)


def softmax(scores):
    expo = jnp.exp(scores - jnp.max(scores, 1, keepdims=True))
    return expo * (1.0 / jnp.sum(expo, 1, keepdims=True))


def scores_of(key, query, bias):
    return by_head(mm_nt(stacked(key), query)) + bias


def bias_of(bias, group):
    return jnp.stack([bias[QUAD * group + n].T for n in range(QUAD)], 0)


def send_edges(send, tokens, lat, diag, lon):
    edges = mm(send, tokens).astype(BF16)
    lat[...] = edges[:LAT]
    diag[...] = edges[LAT : LAT + DIAG]
    lon[...] = edges[LAT + DIAG :]


def joined(local_table, edge_table, local, lat, diag, lon):
    edges = jnp.concatenate([lat[...], diag[...], lon[...]], 0)
    return mm(local_table, local) + mm(edge_table, edges)


def cotangent_kernel(
    cotangent_hbm, send_hbm, flat_out, lat, diag, lon, flat, cotangent, send, sems
):
    tokens_in, send_in = fetch(
        (cotangent_hbm, cotangent, sems.at[0]), (send_hbm, send, sems.at[1])
    )
    tokens_in.wait()
    tokens = grid_rows(cotangent, flat)
    flat_out[...] = tokens
    send_in.wait()
    send_edges(send[...], tokens, lat, diag, lon)


def first_forward_kernel(
    inputs_hbm, to_win_hbm, send_hbm, proj_in_hbm, proj_out_hbm, gain_hbm, bias_hbm,
    out, lat, diag, lon, attended, packed, probs, standard, inv_std,
    flat, inputs, to_win, send, proj_in, proj_out, gain, bias, sems,
):
    tokens_in, to_win_in, gain_in, weights_in, bias_in, weights_out, send_in = fetch(
        (inputs_hbm, inputs, sems.at[0]),
        (to_win_hbm, to_win, sems.at[1]),
        (gain_hbm, gain, sems.at[2]),
        (proj_in_hbm.at[0], proj_in, sems.at[3]),
        (bias_hbm.at[0], bias, sems.at[4]),
        (proj_out_hbm.at[0], proj_out, sems.at[5]),
        (send_hbm, send, sems.at[6]),
    )
    tokens_in.wait()
    grid = grid_rows(inputs, flat)
    to_win_in.wait()
    tokens = mm(to_win[...], grid)
    flat[...] = tokens
    hat, inv = standardized(tokens)
    standard[...] = hat
    inv_std[...] = jnp.broadcast_to(inv, (TOKENS, 128))
    gain_in.wait()
    normed = (hat * gain[0:1, :]).astype(BF16)
    weights_in.wait()
    packed[...] = mm(normed, proj_in[...]).astype(BF16)
    bias_in.wait()

    def one(group):
        added = bias_of(bias, group)
        for window in range(WINDOWS):
            rows = slice(window * AREA, (window + 1) * AREA)
            query, key, value = (packed[rows, columns(group, n)] for n in range(3))
            rounded = softmax(scores_of(key, query, added)).astype(BF16)
            probs[window, pl.ds(QUAD * group, QUAD)] = rounded
            attended[rows, columns(group, 0)] = merged(mm(flipped(rounded), value))

    def step(index, carry):
        one(2 * index)
        one(2 * index + 1)
        return carry

    lax.fori_loop(0, 2, step, 0)
    weights_out.wait()
    send_in.wait()
    result = (flat[...] + mm(attended[...], proj_out[...])).astype(BF16)
    out[...] = result
    send_edges(send[...], result, lat, diag, lon)


def score_grad(weights, value, d_att):
    d_probs = by_head(mm_nt(stacked(value), d_att))
    d_scaled = weights * (d_probs - jnp.sum(d_probs * weights, 1, keepdims=True))
    return d_scaled.astype(BF16)


def norm_backward(d_norm, standard, inv_std, gain, gain_grad, grad):
    gain_grad[...] = jnp.sum(d_norm * standard, 0, keepdims=True)
    d_hat = d_norm * gain
    d_x = inv_std * (
        d_hat
        - jnp.mean(d_hat, -1, keepdims=True)
        - standard * jnp.mean(d_hat * standard, -1, keepdims=True)
    )
    return (grad + d_x).astype(BF16)


def write_out_grad(attended, grad, kept, sent):
    core = lax.axis_index("lon") % 2
    for pair in range(PAIRS):
        both = mm_tn(attended[:, pair * 128 : (pair + 1) * 128], grad[...])
        kept[pair] = jnp.where(core == 0, both[:64], both[64:])
        sent[pair] = jnp.where(core == 0, both[64:], both[:64]).astype(BF16)


def second_grad_kernel(
    local, lat, diag, lon, local_table, edge, proj_hbm, grad, d_att, proj, sem
):
    (weights,) = fetch((proj_hbm.at[1], proj, sem))
    grad[...] = joined(local_table[...], edge[...], local[...], lat, diag, lon).astype(BF16)
    weights.wait()
    d_att[...] = mm_nt(grad[...], proj[...]).astype(BF16)


def first_grad_kernel(
    local, lat, diag, lon, local_table, edge, attended, grad, kept, sent
):
    grad[...] = joined(local_table[...], edge[...], local[...], lat, diag, lon).astype(BF16)
    write_out_grad(attended, grad, kept, sent)


def mask_kernel(region, bias_hbm, allowed, bias_out, bias, sem):
    (bias_in,) = fetch((bias_hbm.at[1], bias, sem))
    token = lax.broadcasted_iota(jnp.int32, (AREA, 1), 0)
    row_of = (token * 171) >> 11
    col_of = token - 12 * row_of
    pick_row = (row_of == lax.broadcasted_iota(jnp.int32, (AREA, ROWS), 1)).astype(BF16)
    by_row = mm(pick_row, region[...].astype(F32).astype(BF16))
    for window in range(WINDOWS):
        column = lax.broadcasted_iota(jnp.int32, (AREA, COLS), 1)
        picked = jnp.where(column == col_of + 12 * window, by_row, 0.0)
        own = jnp.sum(picked, -1, keepdims=True)
        other = mm_nt(jnp.ones((AREA, COLS), BF16), picked.astype(BF16))
        allowed[window] = (own == other).astype(F32)
    bias_in.wait()
    for head in range(HEADS):
        bias_out[head] = bias[head].T


def second_kernel(
    tokens_in, lat_in, diag_in, lon_in, grad, d_att, local_win, edge, send,
    proj_in_hbm, gain, bias, allowed,
    out, lat, diag, lon, attended, gain_grad,
    packed, standard, proj_in, sem,
):
    (weights_in,) = fetch((proj_in_hbm.at[1], proj_in, sem))
    tokens = joined(local_win[...], edge[...], tokens_in[...], lat_in, diag_in, lon_in)
    hat, inv_std = standardized(tokens)
    standard[...] = hat
    normed = (hat * gain[1:2, :]).astype(BF16)
    weights_in.wait()
    packed[...] = mm(normed, proj_in[...]).astype(BF16)

    def step(group, carry):
        added = bias[pl.ds(QUAD * group, QUAD)]
        for window in range(WINDOWS):
            rows = slice(window * AREA, (window + 1) * AREA)
            query, key, value = (packed[rows, columns(group, n)] for n in range(3))
            d_out = d_att[rows, columns(group, 0)]
            scores = scores_of(key, query, added)
            weights = softmax(jnp.where(allowed[window] > 0.5, scores, -1e9))
            rounded = weights.astype(BF16)
            d_scaled = score_grad(weights, value, d_out)
            flat_scaled = d_scaled.reshape(QUAD * AREA, AREA)
            flat_rounded = rounded.reshape(QUAD * AREA, AREA)
            packed[rows, columns(group, 1)] = merged(mm(flat_scaled, query))
            packed[rows, columns(group, 2)] = merged(mm(flat_rounded, d_out))
            attended[rows, columns(group, 0)] = merged(mm(flipped(rounded), value))
            packed[rows, columns(group, 0)] = merged(mm(flipped(d_scaled), key))
        return carry

    lax.fori_loop(0, HEADS // QUAD, step, 0)
    d_norm = mm_nt(packed[...], proj_in[...])
    result = norm_backward(
        d_norm, standard[...], inv_std, gain[1:2, :], gain_grad, grad[...].astype(F32)
    )
    out[...] = result
    send_edges(send[...], result, lat, diag, lon)


def attention_kernel(part, grad, packed, probs, proj_hbm, out, d_att, proj, sem):
    (weights,) = fetch((proj_hbm.at[0, part * 512 : (part + 1) * 512], proj, sem))
    weights.wait()
    d_att[...] = mm_nt(grad[...], proj[...]).astype(BF16)

    def step(index, carry):
        group = 2 * part + index
        for window in range(WINDOWS):
            rows = slice(window * AREA, (window + 1) * AREA)
            query, key, value = (packed[rows, columns(group, n)] for n in range(3))
            d_out = d_att[rows, columns(index, 0)]
            rounded = probs[window, pl.ds(QUAD * group, QUAD)]
            d_scaled = score_grad(rounded.astype(F32), value, d_out)
            flat_scaled = d_scaled.reshape(QUAD * AREA, AREA)
            flat_rounded = rounded.reshape(QUAD * AREA, AREA)
            out[rows, columns(index, 1, 512)] = merged(mm(flat_scaled, query))
            out[rows, columns(index, 2, 512)] = merged(mm(flat_rounded, d_out))
            out[rows, columns(index, 0, 512)] = merged(mm(flipped(d_scaled), key))
        return carry

    lax.fori_loop(0, 2, step, 0)


def norm_grad_kernel(part_a, part_b, proj_hbm, out, packed, proj, sem):
    (weights,) = fetch((proj_hbm.at[0], proj, sem))
    for n, part in enumerate((part_a, part_b)):
        for block in range(3):
            start = block * WIDTH + n * 512
            packed[:, start : start + 512] = part[:, block * 512 : (block + 1) * 512]
    weights.wait()
    out[...] = mm_nt(packed[...], proj[...])


def input_grad_kernel(
    d_norm, grad, standard, inv_std, gain, gain_second, to_grid,
    out, gains, flat, gain_first,
):
    result = norm_backward(
        d_norm[...], standard[...], inv_std[:, 0:1], gain[0:1, :], gain_first,
        grad[...].astype(F32),
    )
    place = lax.broadcasted_iota(jnp.int32, (128, WIDTH), 0)
    feature = lax.broadcasted_iota(jnp.int32, (128, WIDTH), 1)
    own = feature // 8 == place
    slot = lax.broadcasted_iota(jnp.int32, (WIDTH, 128), 1)
    offset = lax.broadcasted_iota(jnp.int32, (WIDTH, 128), 0) % 8
    total = jnp.zeros((128, 128), F32)
    for layer, terms in enumerate((gain_first, gain_second)):
        spread = jnp.where(own, terms[...], 0.0)
        pick = (slot == offset + 8 * layer).astype(F32)
        total = total + jnp.dot(
            spread, pick, precision=lax.Precision.HIGHEST, preferred_element_type=F32
        )
    gains[...] = total
    flat[...] = mm(to_grid[...], result)
    for row in range(ROWS):
        out[0, row] = flat[row * COLS : (row + 1) * COLS, :].astype(BF16)


def split_x_kernel(kept, arrived, own, one, two, three, total):
    x = lax.axis_index("dp")
    for n in range(8):
        total[n] = (kept[n] + arrived[n].astype(F32)).reshape(8, 8, WIDTH)
    for n in range(8):
        for step, out in enumerate((own, one, two, three)):
            place = lax.rem(x + step, 4)
            rows = jnp.concatenate([total[n, place], total[n, 4 + place]], 0)
            out[n] = rows.astype(out.dtype)


def split_y_kernel(*refs):
    layers, (own, *outs), total = (refs[:4], refs[4:8]), refs[8:12], refs[12]
    y = lax.axis_index("lon") // 4
    for layer, parts in enumerate(layers):
        sums = parts[0][...]
        for part in parts[1:]:
            sums = sums + part[...].astype(F32)
        total[...] = sums.reshape(4, 2, 16, WIDTH)
        for step, out in enumerate((own, *outs)):
            out[layer] = total[lax.rem(y + step, 4)].astype(out.dtype)


def split_z_kernel(kept, one, two, three, own, *rest):
    outs, total = rest[:3], rest[3]
    near, far = lax.rem(lax.axis_index("lon") // 2, 2), lax.axis_index("lat")
    for layer in range(2):
        sums = kept[layer] + one[layer].astype(F32) + two[layer].astype(F32) + three[layer].astype(F32)
        total[...] = sums.reshape(2, 2, 8, WIDTH)
        for step, out in enumerate((own, *outs)):
            near_at = near if step % 2 == 0 else 1 - near
            far_at = far if step < 2 else 1 - far
            out[layer] = total[near_at, far_at].astype(out.dtype)


def final_kernel(kept, one, two, three, gains, rows, gain_rows):
    rows[...] = kept[...] + one[...].astype(F32) + two[...].astype(F32) + three[...].astype(F32)
    sums = jnp.sum(gains[...], 0, keepdims=True)
    gain_rows[0:1, :] = sums[:, 0:8]
    gain_rows[1:2, :] = sums[:, 8:16]


def over_lat(value):
    return lax.ppermute(value, "lat", [(0, 1), (1, 0)])


def over_lon(value, step):
    return lax.ppermute(value, "lon", [(i, (i + step) % 16) for i in range(16)])


def over_both(value, step):
    pairs = [(i * 2 + j, (i + step) % 16 * 2 + 1 - j) for i in range(16) for j in range(2)]
    return lax.ppermute(value, ("lon", "lat"), pairs)


def exchanged(lat, diag, lon, step):
    return over_lat(lat), over_both(diag, step), over_lon(lon, step)


def to_core(value):
    return lax.ppermute(value, "lon", [(i, i ^ 1) for i in range(16)])


def along_x(value, step):
    return lax.ppermute(value, "dp", [(i, (i + step) % 4) for i in range(4)])


def along_y(value, step):
    return lax.ppermute(value, "lon", [(i, (i + 4 * step) % 16) for i in range(16)])


def along_z(value, step):
    near, far = step % 2, step // 2
    pairs = [
        (i * 2 + j, (i ^ (2 * near)) * 2 + (j ^ far)) for i in range(16) for j in range(2)
    ]
    return lax.ppermute(value, ("lon", "lat"), pairs)


EDGE_OUTS = [((LAT, WIDTH), BF16), ((DIAG, WIDTH), BF16), ((LON, WIDTH), BF16)]
HALF_OUTS = [((PAIRS, 64, WIDTH), F32), ((PAIRS, 64, WIDTH), BF16)]
FLAT_OUT = ((TOKENS, WIDTH), BF16)
PACKED_OUT = ((TOKENS, 3 * WIDTH), BF16)
X_OUTS = [((8, 16, WIDTH), F32)] + [((8, 16, WIDTH), BF16)] * 3
Y_OUTS = [((2, 2, 16, WIDTH), F32)] + [((2, 2, 16, WIDTH), BF16)] * 3
Z_OUTS = [((2, 8, WIDTH), F32)] + [((2, 8, WIDTH), BF16)] * 3


def split_x(kept, sent):
    return call(
        split_x_kernel, X_OUTS, [pltpu.VMEM((8, 8, 8, WIDTH), F32)], (kept, to_core(sent)), micros=1
    )


def per_device(inputs, cotangent, qkv_weight, out_weight, norm_gain, position_bias, region_ids):
    flat = pltpu.VMEM((TOKENS, WIDTH), F32)
    grid = pltpu.VMEM((1, ROWS, COLS, WIDTH), BF16)
    square = pltpu.VMEM((TOKENS, TOKENS), BF16)
    sender = pltpu.VMEM((EDGES, TOKENS), BF16)
    proj_in = pltpu.VMEM((WIDTH, 3 * WIDTH), BF16)
    proj_out = pltpu.VMEM((WIDTH, WIDTH), BF16)
    bias = pltpu.VMEM((HEADS, AREA, AREA), F32)
    wide = pltpu.VMEM((TOKENS, 3 * WIDTH), BF16)
    dma = pltpu.SemaphoreType.DMA
    cot, *cot_edges = call(
        cotangent_kernel,
        [FLAT_OUT] + EDGE_OUTS,
        [flat, grid, sender, dma((2,))],
        (cotangent, table(SEND_OF_GRID)),
        hbm=(0, 1),
        micros=2,
    )
    cot_edges = exchanged(*cot_edges, -1)
    first_out, lat, diag, lon, attended, packed, probs, standard, inv_std = call(
        first_forward_kernel,
        [FLAT_OUT] + EDGE_OUTS
        + [FLAT_OUT, PACKED_OUT, ((WINDOWS, HEADS, AREA, AREA), BF16)]
        + [((TOKENS, WIDTH), F32), ((TOKENS, 128), F32)],
        [
            flat, grid, square, sender, proj_in, proj_out, pltpu.VMEM((2, WIDTH), F32), bias,
            dma((7,)),
        ],
        (
            inputs, table(WIN_OF_GRID), table(SEND_OF_WIN), qkv_weight, out_weight, norm_gain,
            position_bias,
        ),
        hbm=range(7),
        after=(cot,),
        micros=12,
    )
    edges = exchanged(lat, diag, lon, -1)
    grad_second, d_att = call(
        second_grad_kernel,
        [FLAT_OUT, FLAT_OUT],
        [proj_out, dma],
        (cot, *cot_edges, table(LOCAL_OF_GRID), table(AHEAD_EDGE), out_weight),
        hbm=(6,),
        after=(first_out,),
        micros=3,
    )
    allowed, bias_second = call(
        mask_kernel,
        [((WINDOWS, AREA, AREA), F32), ((HEADS, AREA, AREA), F32)],
        [bias, dma],
        (region_ids, position_bias),
        hbm=(1,),
        after=(first_out,),
        micros=2,
    )
    back, lat, diag, lon, attended_second, gain_second = call(
        second_kernel,
        [FLAT_OUT] + EDGE_OUTS + [FLAT_OUT, ((1, WIDTH), F32)],
        [wide, flat, proj_in, dma],
        (
            first_out, *edges, grad_second, d_att, table(LOCAL_OF_WIN), table(AHEAD_EDGE),
            table(AHEAD_EDGE.T), qkv_weight, norm_gain, bias_second, allowed,
        ),
        hbm=(9,),
        micros=19,
    )
    edges = exchanged(lat, diag, lon, 1)
    halves = call(write_out_grad, HALF_OUTS, [], (attended_second, grad_second), micros=2)
    own_second, *outs_second = split_x(*halves)
    shares_second = [along_x(out, step + 1) for step, out in enumerate(outs_second)]
    grad, *halves = call(
        first_grad_kernel,
        [FLAT_OUT] + HALF_OUTS,
        [],
        (back, *edges, table(LOCAL_OF_WIN.T), table(SEND_OF_WIN.T), attended),
        after=outs_second,
        micros=3,
    )

    def attention(part, after):
        return call(
            functools.partial(attention_kernel, part),
            [((TOKENS, 3 * 512), BF16)],
            [pltpu.VMEM((TOKENS, 512), BF16), pltpu.VMEM((512, WIDTH), BF16), dma],
            (grad, packed, probs, out_weight),
            hbm=(3,),
            after=after,
            micros=4,
        )[0]

    part_a = attention(0, ())
    own_first, *outs_first = split_x(*halves)
    shares_first = [along_x(out, step + 1) for step, out in enumerate(outs_first)]
    part_b = attention(1, (part_a, *outs_first))
    (d_norm,) = call(
        norm_grad_kernel,
        [((TOKENS, WIDTH), F32)],
        [wide, proj_in, dma],
        (part_a, part_b, qkv_weight),
        hbm=(2,),
        micros=4,
    )
    own, *outs = call(
        split_y_kernel, Y_OUTS, [pltpu.VMEM((4, 2, 16, WIDTH), F32)],
        (own_first, *shares_first, own_second, *shares_second), after=(d_norm,), micros=1,
    )
    shares = [along_y(out, step + 1) for step, out in enumerate(outs)]
    result, gains = call(
        input_grad_kernel,
        [((1, ROWS, COLS, WIDTH), BF16), ((128, 128), F32)],
        [flat, pltpu.VMEM((1, WIDTH), F32)],
        (d_norm, grad, standard, inv_std, norm_gain, gain_second, table(WIN_OF_GRID.T)),
        after=outs,
        micros=4,
    )
    own, *outs = call(
        split_z_kernel, Z_OUTS, [pltpu.VMEM((2, 2, 8, WIDTH), F32)], (own, *shares),
        after=(gains,), micros=1,
    )
    shares = [along_z(out, step + 1) for step, out in enumerate(outs)]
    gains = lax.all_to_all(gains, ("lon", "lat", "dp"), 0, 0, tiled=True)
    rows, gain_rows = call(
        final_kernel, [((2, 8, WIDTH), F32), ((2, 8), F32)], [], (own, *shares, gains), micros=1
    )
    return result, rows, gain_rows


def solution(mesh):
    in_specs = (
        P("dp", "lat", "lon", None),
        P("dp", "lat", "lon", None),
        P(),
        P(),
        P(),
        P(),
        P("lat", "lon"),
    )
    out_specs = (
        P("dp", "lat", "lon", None),
        P(None, ("lon", "lat", "dp"), None),
        P(None, ("lon", "lat", "dp")),
    )
    return jax.shard_map(
        per_device, mesh=mesh, in_specs=in_specs, out_specs=out_specs, check_vma=False
    )
```

```python
import functools

import numpy as np

import jax
import jax.numpy as jnp
from jax import lax
from jax.experimental import pallas as pl
from jax.experimental.pallas import tpu as pltpu
from jax.sharding import PartitionSpec as P

WIN = 12
ROWS = 12
COLS = 36
TOKENS = 432
AREA = 144
WINDOWS = 3
WIDTH = 1024
HEADS = 16
PAIRS = 8
QUAD = 4
LAT, DIAG, LON, EDGES = 180, 36, 36, 252
EDGES_PADDED = 272
F32 = jnp.float32
BF16 = jnp.bfloat16
VMEM_LIMIT = 26 * 2**20


def tables():
    win = np.zeros((TOKENS, TOKENS), np.float32)
    local = np.zeros((TOKENS, TOKENS), np.float32)
    edge = np.zeros((TOKENS, EDGES), np.float32)
    send = np.zeros((EDGES, TOKENS), np.float32)
    for row in range(ROWS):
        for col in range(COLS):
            grid = row * COLS + col
            place = col // WIN * AREA + row * WIN + col % WIN
            win[place, grid] = 1
            if row + 6 < ROWS and col + 6 < COLS:
                local[place, grid + 6 * COLS + 6] = 1
            elif row + 6 < ROWS:
                edge[place, LAT + DIAG + row * 6 + col - 30] = 1
            elif col + 6 < COLS:
                edge[place, (row - 6) * 30 + col] = 1
            else:
                edge[place, LAT + (row - 6) * 6 + col - 30] = 1
            if row < 6 and col >= 6:
                send[row * 30 + col - 6, grid] = 1
            elif row < 6:
                send[LAT + row * 6 + col, grid] = 1
            elif col < 6:
                send[LAT + DIAG + (row - 6) * 6 + col, grid] = 1
    return win, local, edge, send


WIN_OF_GRID, LOCAL_OF_GRID, AHEAD_EDGE, SEND_OF_GRID = tables()
LOCAL_OF_WIN = LOCAL_OF_GRID @ WIN_OF_GRID.T
SEND_OF_WIN = SEND_OF_GRID @ WIN_OF_GRID.T


EDGE_STARTS = (0, 184, 224)


def sender_table(values):
    rows = np.zeros((EDGES_PADDED, TOKENS), np.float32)
    for start, part in zip(EDGE_STARTS, np.split(values, [LAT, LAT + DIAG])):
        rows[start : start + len(part)] = part
    return table(rows)


def table(values):
    return jnp.asarray(values, BF16)


def edge_tables(values, axis):
    return [table(part) for part in np.split(values, [LAT, LAT + DIAG], axis)]


def mm(a, b):
    return lax.dot_general(a, b, (((1,), (0,)), ((), ())), preferred_element_type=F32)


def mm_nt(a, b):
    return lax.dot_general(a, b, (((1,), (1,)), ((), ())), preferred_element_type=F32)


def mm_tn(a, b):
    return lax.dot_general(a, b, (((0,), (0,)), ((), ())), preferred_element_type=F32)


def call(kernel, outs, scratch, args, hbm=(), after=(), micros=10):
    count, last = len(args), len(args) + len(after)
    spaces = [pltpu.HBM if i in hbm else pltpu.VMEM for i in range(count)]
    spaces += [pl.ANY] * len(after)

    args = [
        pltpu.with_memory_space_constraint(arg, pltpu.HBM) if i in hbm else arg
        for i, arg in enumerate(args)
    ]

    def body(*refs):
        kernel(*refs[:count], *refs[last:])

    return pl.pallas_call(
        body,
        out_shape=[jax.ShapeDtypeStruct(shape, dtype) for shape, dtype in outs],
        in_specs=[pl.BlockSpec(memory_space=space) for space in spaces],
        out_specs=[pl.BlockSpec(memory_space=pltpu.VMEM)] * len(outs),
        scratch_shapes=scratch,
        compiler_params=pltpu.CompilerParams(vmem_limit_bytes=VMEM_LIMIT),
        cost_estimate=pl.CostEstimate(
            flops=int(micros * 1.15e9), transcendentals=0, bytes_accessed=2**20
        ),
    )(*args, *after)


def fetch(*copies):
    handles = [pltpu.make_async_copy(*copy) for copy in copies]
    for handle in handles:
        handle.start()
    return handles


def grid_rows(source, flat):
    for row in range(ROWS):
        flat[row * COLS : (row + 1) * COLS, :] = source[0, row].astype(F32)
    return flat[...].astype(BF16)


def standardized(tokens):
    centred = tokens - jnp.mean(tokens, -1, keepdims=True)
    inv_std = lax.rsqrt(jnp.mean(centred * centred, -1, keepdims=True) + 1e-05)
    return centred * inv_std, inv_std


def quarter(width=4 * 64):
    return lax.broadcasted_iota(jnp.int32, (1, width), 1) // 64


def stacked(values):
    parts = [values * jnp.where(quarter() == n, 0.125, 0.0).astype(BF16) for n in range(QUAD)]
    return jnp.concatenate(parts, 0)


def by_head(values):
    return values.reshape(QUAD, AREA, AREA)


def flipped(values):
    return jnp.concatenate([values[n].T for n in range(QUAD)], 0)


def merged(values):
    result = values[:AREA]
    for n in range(1, QUAD):
        result = jnp.where(quarter() == n, values[n * AREA : (n + 1) * AREA], result)
    return result.astype(BF16)


def columns(group, block, width=WIDTH):
    return pl.ds(pl.multiple_of(group * 256 + width * block, 256), 256)


def softmax(scores):
    expo = jnp.exp(scores - jnp.max(scores, 1, keepdims=True))
    return expo * (1.0 / jnp.sum(expo, 1, keepdims=True))


def scores_of(key, query, bias):
    return by_head(mm_nt(stacked(key), query)) + bias


def bias_of(bias, group):
    return jnp.stack([bias[QUAD * group + n].T for n in range(QUAD)], 0)


def split_edges(values, outs):
    for start, out in zip(EDGE_STARTS, outs):
        out[...] = values[start : start + out.shape[0]].astype(BF16)


def joined(local_table, edge_tables, local, edges):
    total = mm(local_table[...], local[...])
    for edge_table, edge in zip(edge_tables, edges):
        total = total + mm(edge_table[...], edge[...])
    return total


def cotangent_kernel(
    cotangent_hbm, send_hbm, flat_out, lat, diag, lon, flat, cotangent, send, sems
):
    tokens_in, send_in = fetch(
        (cotangent_hbm, cotangent, sems.at[0]), (send_hbm, send, sems.at[1])
    )
    tokens_in.wait()
    tokens = grid_rows(cotangent, flat)
    flat_out[...] = tokens
    send_in.wait()
    split_edges(mm(send[...], tokens), (lat, diag, lon))


def first_forward_kernel(
    inputs_hbm, to_win_hbm, send_hbm, proj_in_hbm, proj_out_hbm, gain_hbm, bias_hbm,
    out, lat, diag, lon, attended, packed, probs, standard, inv_std,
    flat, inputs, to_win, send, proj_in, proj_out, gain, bias, sems,
):
    tokens_in, to_win_in, gain_in, weights_in, bias_in, weights_out, send_in = fetch(
        (inputs_hbm, inputs, sems.at[0]),
        (to_win_hbm, to_win, sems.at[1]),
        (gain_hbm, gain, sems.at[2]),
        (proj_in_hbm.at[0], proj_in, sems.at[3]),
        (bias_hbm.at[0], bias, sems.at[4]),
        (proj_out_hbm.at[0], proj_out, sems.at[5]),
        (send_hbm, send, sems.at[6]),
    )
    tokens_in.wait()
    grid = grid_rows(inputs, flat)
    to_win_in.wait()
    tokens = mm(to_win[...], grid)
    flat[...] = tokens
    hat, inv = standardized(tokens)
    standard[...] = hat
    inv_std[...] = jnp.broadcast_to(inv, (TOKENS, 128))
    gain_in.wait()
    normed = (hat * gain[0:1, :]).astype(BF16)
    weights_in.wait()
    packed[...] = mm(normed, proj_in[...]).astype(BF16)
    bias_in.wait()

    def one(group):
        added = bias_of(bias, group)
        for window in range(WINDOWS):
            rows = slice(window * AREA, (window + 1) * AREA)
            query, key, value = (packed[rows, columns(group, n)] for n in range(3))
            rounded = softmax(scores_of(key, query, added)).astype(BF16)
            probs[window, pl.ds(QUAD * group, QUAD)] = rounded
            attended[rows, columns(group, 0)] = merged(mm(flipped(rounded), value))

    def step(index, carry):
        one(2 * index)
        one(2 * index + 1)
        return carry

    lax.fori_loop(0, 2, step, 0)
    weights_out.wait()
    send_in.wait()
    result = (flat[...] + mm(attended[...], proj_out[...])).astype(BF16)
    out[...] = result
    split_edges(mm(send[...], result), (lat, diag, lon))


def score_grad(weights, value, d_att):
    d_probs = by_head(mm_nt(stacked(value), d_att))
    d_scaled = weights * (d_probs - jnp.sum(d_probs * weights, 1, keepdims=True))
    return d_scaled.astype(BF16)


def norm_backward(d_norm, standard, inv_std, gain, grad):
    d_hat = d_norm * gain
    d_x = inv_std * (
        d_hat
        - jnp.mean(d_hat, -1, keepdims=True)
        - standard * jnp.mean(d_hat * standard, -1, keepdims=True)
    )
    return (grad + d_x).astype(BF16)


def write_out_grad(attended, grad, kept, sent):
    core = lax.axis_index("lon") % 2
    for pair in range(PAIRS):
        both = mm_tn(attended[:, pair * 128 : (pair + 1) * 128], grad[...])
        kept[pair] = jnp.where(core == 0, both[:64], both[64:])
        sent[pair] = jnp.where(core == 0, both[64:], both[:64]).astype(BF16)


def second_grad_kernel(
    local, lat, diag, lon, local_table, to_lat, to_diag, to_lon, proj_hbm,
    grad, d_att, proj, sem,
):
    (weights,) = fetch((proj_hbm.at[1], proj, sem))
    tables = (to_lat, to_diag, to_lon)
    grad[...] = joined(local_table, tables, local, (lat, diag, lon)).astype(BF16)
    weights.wait()
    d_att[...] = mm_nt(grad[...], proj[...]).astype(BF16)


def first_grad_kernel(
    local, lat, diag, lon, local_table, to_lat, to_diag, to_lon, attended, grad, kept, sent
):
    tables = (to_lat, to_diag, to_lon)
    grad[...] = joined(local_table, tables, local, (lat, diag, lon)).astype(BF16)
    write_out_grad(attended, grad, kept, sent)


def mask_kernel(
    region, diag_in, lon_in, bias_hbm, allowed, bias_out, diag, lon, bias, sem
):
    (bias_in,) = fetch((bias_hbm.at[1], bias, sem))
    diag[...] = diag_in[...]
    lon[...] = lon_in[...]
    token = lax.broadcasted_iota(jnp.int32, (AREA, 1), 0)
    row_of = (token * 171) >> 11
    col_of = token - 12 * row_of
    pick_row = (row_of == lax.broadcasted_iota(jnp.int32, (AREA, ROWS), 1)).astype(BF16)
    by_row = mm(pick_row, region[...].astype(F32).astype(BF16))
    for window in range(WINDOWS):
        column = lax.broadcasted_iota(jnp.int32, (AREA, COLS), 1)
        picked = jnp.where(column == col_of + 12 * window, by_row, 0.0)
        own = jnp.sum(picked, -1, keepdims=True)
        other = mm_nt(jnp.ones((AREA, COLS), BF16), picked.astype(BF16))
        allowed[window] = (own == other).astype(F32)
    bias_in.wait()
    for head in range(HEADS):
        bias_out[head] = bias[head].T


def second_kernel(
    tokens_in, lat_in, diag_in, lon_in, grad, d_att,
    local_win, to_lat, to_diag, to_lon, send,
    proj_in_hbm, gain, bias, allowed,
    out, lat, diag, lon, attended, gain_grad,
    packed, standard, proj_in, sem,
):
    (weights_in,) = fetch((proj_in_hbm.at[1], proj_in, sem))
    tables = (to_lat, to_diag, to_lon)
    tokens = joined(local_win, tables, tokens_in, (lat_in, diag_in, lon_in))
    hat, inv_std = standardized(tokens)
    standard[...] = hat
    normed = (hat * gain[1:2, :]).astype(BF16)
    weights_in.wait()
    packed[...] = mm(normed, proj_in[...]).astype(BF16)

    def step(group, carry):
        added = bias[pl.ds(QUAD * group, QUAD)]
        for window in range(WINDOWS):
            rows = slice(window * AREA, (window + 1) * AREA)
            query, key, value = (packed[rows, columns(group, n)] for n in range(3))
            d_out = d_att[rows, columns(group, 0)]
            scores = scores_of(key, query, added)
            weights = softmax(jnp.where(allowed[window] > 0.5, scores, -1e9))
            rounded = weights.astype(BF16)
            d_scaled = score_grad(weights, value, d_out)
            flat_scaled = d_scaled.reshape(QUAD * AREA, AREA)
            flat_rounded = rounded.reshape(QUAD * AREA, AREA)
            packed[rows, columns(group, 1)] = merged(mm(flat_scaled, query))
            packed[rows, columns(group, 2)] = merged(mm(flat_rounded, d_out))
            attended[rows, columns(group, 0)] = merged(mm(flipped(rounded), value))
            packed[rows, columns(group, 0)] = merged(mm(flipped(d_scaled), key))
        return carry

    lax.fori_loop(0, HEADS // QUAD, step, 0)
    d_norm = mm_nt(packed[...], proj_in[...])
    gain_grad[...] = jnp.sum(d_norm * standard[...], 0, keepdims=True)
    result = norm_backward(d_norm, standard[...], inv_std, gain[1:2, :], grad[...].astype(F32))
    out[...] = result
    split_edges(mm(send[...], result), (lat, diag, lon))


def attention_grad(part, grad, packed, probs, proj, d_att, write):
    d_att[...] = mm_nt(grad[...], proj).astype(BF16)

    def step(index, carry):
        group = 2 * part + index
        for window in range(WINDOWS):
            rows = slice(window * AREA, (window + 1) * AREA)
            query, key, value = (packed[rows, columns(group, n)] for n in range(3))
            d_out = d_att[rows, columns(index, 0)]
            rounded = probs[window, pl.ds(QUAD * group, QUAD)]
            d_scaled = score_grad(rounded.astype(F32), value, d_out)
            flat_scaled = d_scaled.reshape(QUAD * AREA, AREA)
            flat_rounded = rounded.reshape(QUAD * AREA, AREA)
            write(index, rows, 1, merged(mm(flat_scaled, query)))
            write(index, rows, 2, merged(mm(flat_rounded, d_out)))
            write(index, rows, 0, merged(mm(flipped(d_scaled), key)))
        return carry

    lax.fori_loop(0, 2, step, 0)


def first_half_kernel(grad, packed, probs, proj, out, d_att):
    def write(index, rows, block, values):
        out[rows, columns(index, block, 512)] = values

    attention_grad(0, grad, packed, probs, proj[0, 0:512], d_att, write)


def second_half_kernel(
    part_a, grad, packed_in, probs, proj, standard, gain_second, proj_in_hbm,
    d_norm, gains, d_att, packed, proj_in, sem,
):
    (weights,) = fetch((proj_in_hbm.at[0], proj_in, sem))
    for block in range(3):
        packed[:, block * WIDTH : block * WIDTH + 512] = part_a[:, block * 512 : (block + 1) * 512]

    def write(index, rows, block, values):
        packed[rows, columns(2 + index, block)] = values

    attention_grad(1, grad, packed_in, probs, proj[0, 512:1024], d_att, write)
    weights.wait()
    result = mm_nt(packed[...], proj_in[...])
    d_norm[...] = result
    gains[0:1, :] = jnp.sum(result * standard[...], 0, keepdims=True)
    gains[1:2, :] = gain_second[...]


def input_grad_kernel(d_norm, grad, standard, inv_std, gain, to_grid, out, done, flat):
    done[...] = inv_std[0:8, :]
    result = norm_backward(
        d_norm[...], standard[...], inv_std[:, 0:1], gain[0:1, :], grad[...].astype(F32)
    )
    flat[...] = mm(to_grid[...], result)
    for row in range(ROWS):
        out[0, row] = flat[row * COLS : (row + 1) * COLS, :].astype(BF16)


def split_x_kernel(kept, arrived, own, one, two, three, total):
    x = lax.axis_index("dp")
    for n in range(8):
        total[n] = (kept[n] + arrived[n].astype(F32)).reshape(8, 8, WIDTH)
    for n in range(8):
        for step, out in enumerate((own, one, two, three)):
            place = lax.rem(x + step, 4)
            rows = jnp.concatenate([total[n, place], total[n, 4 + place]], 0)
            out[n] = rows.astype(out.dtype)


def pair_of(values):
    high = values.astype(BF16)
    return high, (values - high.astype(F32)).astype(BF16)


def put_gains(out, start, values):
    high, low = pair_of(values)
    rows = jnp.concatenate([high.astype(F32), low.astype(F32), jnp.zeros((12, WIDTH), F32)], 0)
    out[start : start + 16] = rows.astype(BF16)


def taken_gains(part, start):
    rows = part[start : start + 16].astype(F32)
    return rows[0:2] + rows[2:4]


def split_y_kernel(kept, arrived, own, one, two, three):
    y = lax.axis_index("lon") // 4
    for step, out in enumerate((own, one, two, three)):
        place = lax.rem(y + step, 4)
        for n in range(2):
            terms = kept[2 * place + n] + arrived[2 * place + n].astype(F32)
            out[n * 64 : n * 64 + 64] = terms.astype(out.dtype)


def middle_y_kernel(
    kept, a, b, c, gains, gains_arrived, own, own_gains, one, two, three, total
):
    y = lax.axis_index("lon") // 4
    sums = gains[...] + gains_arrived[...]
    own_gains[...] = sums
    terms = kept[...] + a[...].astype(F32) + b[...].astype(F32) + c[...].astype(F32)
    total[...] = terms.reshape(4, 32, WIDTH)
    for step, out in enumerate((own, one, two, three)):
        out[0:32] = total[lax.rem(y + step, 4)].astype(out.dtype)
        if step:
            put_gains(out, 32, sums)


def middle_x_kernel(
    kept, a, b, c, second, gains, d, e, f,
    own, own_second, own_gains, one, two, three, total,
):
    x = lax.axis_index("dp")
    sums, others = gains[...], second[...]
    for part in (d, e, f):
        sums = sums + taken_gains(part, 32)
        others = others + part[0:32].astype(F32)
    own_gains[...] = sums
    own_second[...] = others
    terms = kept[...] + a[...].astype(F32) + b[...].astype(F32) + c[...].astype(F32)
    total[...] = terms.reshape(4, 4, 8, WIDTH)
    for step, out in enumerate((own, one, two, three)):
        place = lax.rem(x + step, 4)
        out[0:32] = jnp.concatenate([total[n, place] for n in range(4)], 0).astype(out.dtype)
        if step:
            put_gains(out, 32, sums)


def split_z_kernel(kept, second, gains, one, two, three, own, own_gains, *rest):
    outs, total = rest[:3], rest[3]
    near, far = lax.rem(lax.axis_index("lon") // 2, 2), lax.axis_index("lat")
    sums, terms = gains[...], kept[...]
    for part in (one, two, three):
        sums = sums + taken_gains(part, 32)
        terms = terms + part[0:32].astype(F32)
    own_gains[...] = sums
    total[0] = terms.reshape(2, 2, 8, WIDTH)
    total[1] = second[...].reshape(2, 2, 8, WIDTH)
    own[...] = jnp.concatenate([total[0, near, far], total[1, near, far]], 0)
    for step, out in enumerate(outs):
        near_at = near if step == 1 else 1 - near
        far_at = far if step == 0 else 1 - far
        rows = jnp.concatenate([total[0, near_at, far_at], total[1, near_at, far_at]], 0)
        out[0:16] = rows.astype(BF16)
        put_gains(out, 16, sums)


def final_kernel(kept, gains, one, two, three, rows, gain_rows):
    terms, sums = kept[...], gains[...]
    for part in (one, two, three):
        terms = terms + part[0:16].astype(F32)
        sums = sums + taken_gains(part, 16)
    rows[0] = terms[0:8]
    rows[1] = terms[8:16]
    place = (lax.axis_index("lon") * 2 + lax.axis_index("lat")) * 4 + lax.axis_index("dp")
    padded = jnp.concatenate([sums, jnp.zeros((6, WIDTH), F32)], 0)
    gain_rows[...] = pltpu.roll(padded, WIDTH - 8 * place, 1)[0:2, 0:8]


def over_lat(value):
    return lax.ppermute(value, "lat", [(0, 1), (1, 0)])


def over_lon(value, step):
    return lax.ppermute(value, "lon", [(i, (i + step) % 16) for i in range(16)])


def over_both(value, step):
    pairs = [(i * 2 + j, (i + step) % 16 * 2 + 1 - j) for i in range(16) for j in range(2)]
    return lax.ppermute(value, ("lon", "lat"), pairs)


def exchanged(lat, diag, lon, step):
    return over_lat(lat), over_both(diag, step), over_lon(lon, step)


def to_core(value):
    return lax.ppermute(value, "lon", [(i, i ^ 1) for i in range(16)])


def along_x(value, step):
    return lax.ppermute(value, "dp", [(i, (i + step) % 4) for i in range(4)])


def along_y(value, step):
    return lax.ppermute(value, "lon", [(i, (i + 4 * step) % 16) for i in range(16)])


def along_z(value, step):
    near, far = step % 2, step // 2
    pairs = [
        (i * 2 + j, (i ^ (2 * near)) * 2 + (j ^ far)) for i in range(16) for j in range(2)
    ]
    return lax.ppermute(value, ("lon", "lat"), pairs)


EDGE_OUTS = [((LAT, WIDTH), BF16), ((DIAG, WIDTH), BF16), ((LON, WIDTH), BF16)]
HALF_OUTS = [((PAIRS, 64, WIDTH), F32), ((PAIRS, 64, WIDTH), BF16)]
FLAT_OUT = ((TOKENS, WIDTH), BF16)
PACKED_OUT = ((TOKENS, 3 * WIDTH), BF16)
X_OUTS = [((8, 16, WIDTH), F32)] + [((8, 16, WIDTH), BF16)] * 3
GAINS = ((2, WIDTH), F32)
Y_OUTS = [((128, WIDTH), F32)] + [((128, WIDTH), BF16)] * 3
OWN = ((32, WIDTH), F32)
MIDDLE_OUTS = [((48, WIDTH), BF16)] * 3
Z_OUTS = [((16, WIDTH), F32), GAINS] + [((32, WIDTH), BF16)] * 3


def split_x(kept, sent):
    return call(
        split_x_kernel, X_OUTS, [pltpu.VMEM((8, 8, 8, WIDTH), F32)], (kept, to_core(sent)), micros=1
    )


def per_device(inputs, cotangent, qkv_weight, out_weight, norm_gain, position_bias, region_ids):
    flat = pltpu.VMEM((TOKENS, WIDTH), F32)
    grid = pltpu.VMEM((1, ROWS, COLS, WIDTH), BF16)
    square = pltpu.VMEM((TOKENS, TOKENS), BF16)
    sender = pltpu.VMEM((EDGES_PADDED, TOKENS), BF16)
    proj_in = pltpu.VMEM((WIDTH, 3 * WIDTH), BF16)
    proj_out = pltpu.VMEM((WIDTH, WIDTH), BF16)
    bias = pltpu.VMEM((HEADS, AREA, AREA), F32)
    wide = pltpu.VMEM((TOKENS, 3 * WIDTH), BF16)
    dma = pltpu.SemaphoreType.DMA
    cot, *cot_edges = call(
        cotangent_kernel,
        [FLAT_OUT] + EDGE_OUTS,
        [flat, grid, sender, dma((2,))],
        (cotangent, sender_table(SEND_OF_GRID)),
        hbm=(0, 1),
        micros=2,
    )
    cot_edges = exchanged(*cot_edges, -1)
    first_out, lat, diag, lon, attended, packed, probs, standard, inv_std = call(
        first_forward_kernel,
        [FLAT_OUT] + EDGE_OUTS
        + [FLAT_OUT, PACKED_OUT, ((WINDOWS, HEADS, AREA, AREA), BF16)]
        + [((TOKENS, WIDTH), F32), ((TOKENS, 128), F32)],
        [
            flat, grid, square, sender, proj_in, proj_out, pltpu.VMEM((2, WIDTH), F32), bias,
            dma((7,)),
        ],
        (
            inputs, table(WIN_OF_GRID), sender_table(SEND_OF_WIN), qkv_weight, out_weight, norm_gain,
            position_bias,
        ),
        hbm=range(7),
        after=(cot,),
        micros=12,
    )
    allowed, bias_second, diag, lon = call(
        mask_kernel,
        [((WINDOWS, AREA, AREA), F32), ((HEADS, AREA, AREA), F32)] + EDGE_OUTS[1:],
        [bias, dma],
        (region_ids, diag, lon, position_bias),
        hbm=(3,),
        after=cot_edges,
        micros=2,
    )
    edges = exchanged(lat, diag, lon, -1)
    grad_second, d_att = call(
        second_grad_kernel,
        [FLAT_OUT, FLAT_OUT],
        [proj_out, dma],
        (cot, *cot_edges, table(LOCAL_OF_GRID), *edge_tables(AHEAD_EDGE, 1), out_weight),
        hbm=(8,),
        after=(allowed,),
        micros=3,
    )
    back, lat, diag, lon, attended_second, gain_second = call(
        second_kernel,
        [FLAT_OUT] + EDGE_OUTS + [FLAT_OUT, ((1, WIDTH), F32)],
        [wide, flat, proj_in, dma],
        (
            first_out, *edges, grad_second, d_att, table(LOCAL_OF_WIN),
            *edge_tables(AHEAD_EDGE, 1), sender_table(AHEAD_EDGE.T), qkv_weight, norm_gain,
            bias_second, allowed,
        ),
        hbm=(11,),
        micros=19,
    )
    edges = exchanged(lat, diag, lon, 1)
    halves = call(write_out_grad, HALF_OUTS, [], (attended_second, grad_second), micros=2)
    own_second, *outs_second = split_x(*halves)
    shares_second = [along_x(out, step + 1) for step, out in enumerate(outs_second)]
    grad, *halves = call(
        first_grad_kernel,
        [FLAT_OUT] + HALF_OUTS,
        [],
        (back, *edges, table(LOCAL_OF_WIN.T), *edge_tables(SEND_OF_WIN.T, 1), attended),
        after=(*outs_second, shares_second[0], shares_second[2]),
        micros=3,
    )

    half = pltpu.VMEM((TOKENS, 512), BF16)
    (part_a,) = call(
        first_half_kernel,
        [((TOKENS, 3 * 512), BF16)],
        [half],
        (grad, packed, probs, out_weight),
        micros=4,
    )
    own_first, *outs_first = call(
        split_y_kernel, Y_OUTS, [], (halves[0], to_core(halves[1])), micros=1
    )
    shares_first = [along_y(out, step + 1) for step, out in enumerate(outs_first)]
    d_norm, gains = call(
        second_half_kernel,
        [((TOKENS, WIDTH), F32), GAINS],
        [half, wide, proj_in, dma],
        (part_a, grad, packed, probs, out_weight, standard, gain_second, qkv_weight),
        hbm=(7,),
        after=(*outs_first, shares_second[1]),
        micros=8,
    )
    own_second, own_gains, *outs = call(
        middle_y_kernel,
        [OWN, GAINS] + MIDDLE_OUTS,
        [pltpu.VMEM((4, 32, WIDTH), F32)],
        (own_second, *shares_second, gains, to_core(gains)),
        micros=0.05,
    )
    shares = [along_y(out, step + 1) for step, out in enumerate(outs)]
    result, done = call(
        input_grad_kernel,
        [((1, ROWS, COLS, WIDTH), BF16), ((8, 128), F32)],
        [flat],
        (d_norm, grad, standard, inv_std, norm_gain, table(WIN_OF_GRID.T)),
        after=(*outs, *shares_first),
        micros=1,
    )
    own_first, own_second, own_gains, *outs = call(
        middle_x_kernel,
        [OWN, OWN, GAINS] + MIDDLE_OUTS,
        [pltpu.VMEM((4, 4, 8, WIDTH), F32)],
        (own_first, *shares_first, own_second, own_gains, *shares),
        after=(done,),
        micros=0.05,
    )
    shares = [along_x(out, step + 1) for step, out in enumerate(outs)]
    own, own_gains, *outs = call(
        split_z_kernel,
        Z_OUTS,
        [pltpu.VMEM((2, 2, 2, 8, WIDTH), F32)],
        (own_first, own_second, own_gains, *shares),
        micros=0.05,
    )
    shares = [along_z(out, step + 1) for step, out in enumerate(outs)]
    rows, gain_rows = call(
        final_kernel, [((2, 8, WIDTH), F32), ((2, 8), F32)], [], (own, own_gains, *shares), micros=1
    )
    return result, rows, gain_rows


def solution(mesh):
    in_specs = (
        P("dp", "lat", "lon", None),
        P("dp", "lat", "lon", None),
        P(),
        P(),
        P(),
        P(),
        P("lat", "lon"),
    )
    out_specs = (
        P("dp", "lat", "lon", None),
        P(None, ("lon", "lat", "dp"), None),
        P(None, ("lon", "lat", "dp")),
    )
    return jax.shard_map(
        per_device, mesh=mesh, in_specs=in_specs, out_specs=out_specs, check_vma=False
    )
```

```python
import functools

import numpy as np

import jax
import jax.numpy as jnp
from jax import lax
from jax.experimental import pallas as pl
from jax.experimental.pallas import tpu as pltpu
from jax.sharding import PartitionSpec as P

WIN = 12
ROWS = 12
COLS = 36
TOKENS = 432
AREA = 144
WINDOWS = 3
WIDTH = 1024
HEADS = 16
PAIRS = 8
QUAD = 4
LAT, DIAG, LON, EDGES = 180, 36, 36, 252
EDGES_PADDED = 272
F32 = jnp.float32
BF16 = jnp.bfloat16
VMEM_LIMIT = 26 * 2**20


def tables():
    win = np.zeros((TOKENS, TOKENS), np.float32)
    local = np.zeros((TOKENS, TOKENS), np.float32)
    edge = np.zeros((TOKENS, EDGES), np.float32)
    send = np.zeros((EDGES, TOKENS), np.float32)
    for row in range(ROWS):
        for col in range(COLS):
            grid = row * COLS + col
            place = col // WIN * AREA + row * WIN + col % WIN
            win[place, grid] = 1
            if row + 6 < ROWS and col + 6 < COLS:
                local[place, grid + 6 * COLS + 6] = 1
            elif row + 6 < ROWS:
                edge[place, LAT + DIAG + row * 6 + col - 30] = 1
            elif col + 6 < COLS:
                edge[place, (row - 6) * 30 + col] = 1
            else:
                edge[place, LAT + (row - 6) * 6 + col - 30] = 1
            if row < 6 and col >= 6:
                send[row * 30 + col - 6, grid] = 1
            elif row < 6:
                send[LAT + row * 6 + col, grid] = 1
            elif col < 6:
                send[LAT + DIAG + (row - 6) * 6 + col, grid] = 1
    return win, local, edge, send


WIN_OF_GRID, LOCAL_OF_GRID, AHEAD_EDGE, SEND_OF_GRID = tables()
LOCAL_OF_WIN = LOCAL_OF_GRID @ WIN_OF_GRID.T
SEND_OF_WIN = SEND_OF_GRID @ WIN_OF_GRID.T


EDGE_STARTS = (0, 184, 224)


def sender_table(values):
    rows = np.zeros((EDGES_PADDED, TOKENS), np.float32)
    for start, part in zip(EDGE_STARTS, np.split(values, [LAT, LAT + DIAG])):
        rows[start : start + len(part)] = part
    return table(rows)


def table(values):
    return jnp.asarray(values, BF16)


def edge_tables(values, axis):
    return [table(part) for part in np.split(values, [LAT, LAT + DIAG], axis)]


def mm(a, b):
    return lax.dot_general(a, b, (((1,), (0,)), ((), ())), preferred_element_type=F32)


def mm_nt(a, b):
    return lax.dot_general(a, b, (((1,), (1,)), ((), ())), preferred_element_type=F32)


def mm_tn(a, b):
    return lax.dot_general(a, b, (((0,), (0,)), ((), ())), preferred_element_type=F32)


def call(kernel, outs, scratch, args, hbm=(), after=(), micros=10):
    count, last = len(args), len(args) + len(after)
    spaces = [pltpu.HBM if i in hbm else pltpu.VMEM for i in range(count)]
    spaces += [pl.ANY] * len(after)

    args = [
        pltpu.with_memory_space_constraint(arg, pltpu.HBM) if i in hbm else arg
        for i, arg in enumerate(args)
    ]

    def body(*refs):
        kernel(*refs[:count], *refs[last:])

    return pl.pallas_call(
        body,
        out_shape=[jax.ShapeDtypeStruct(shape, dtype) for shape, dtype in outs],
        in_specs=[pl.BlockSpec(memory_space=space) for space in spaces],
        out_specs=[pl.BlockSpec(memory_space=pltpu.VMEM)] * len(outs),
        scratch_shapes=scratch,
        compiler_params=pltpu.CompilerParams(vmem_limit_bytes=VMEM_LIMIT),
        cost_estimate=pl.CostEstimate(
            flops=int(micros * 1.15e9), transcendentals=0, bytes_accessed=2**20
        ),
    )(*args, *after)


def fetch(*copies):
    handles = [pltpu.make_async_copy(*copy) for copy in copies]
    for handle in handles:
        handle.start()
    return handles


def grid_rows(source, flat):
    for row in range(ROWS):
        flat[row * COLS : (row + 1) * COLS, :] = source[0, row].astype(F32)
    return flat[...].astype(BF16)


def standardized(tokens):
    centred = tokens - jnp.mean(tokens, -1, keepdims=True)
    inv_std = lax.rsqrt(jnp.mean(centred * centred, -1, keepdims=True) + 1e-05)
    return centred * inv_std, inv_std


def quarter(width=4 * 64):
    return lax.broadcasted_iota(jnp.int32, (1, width), 1) // 64


def stacked(values):
    parts = [values * jnp.where(quarter() == n, 0.125, 0.0).astype(BF16) for n in range(QUAD)]
    return jnp.concatenate(parts, 0)


def by_head(values):
    return values.reshape(QUAD, AREA, AREA)


def flipped(values):
    return jnp.concatenate([values[n].T for n in range(QUAD)], 0)


def merged(values):
    result = values[:AREA]
    for n in range(1, QUAD):
        result = jnp.where(quarter() == n, values[n * AREA : (n + 1) * AREA], result)
    return result.astype(BF16)


def columns(group, block=0, width=WIDTH):
    start = group * 256 + width * block
    return slice(start, start + 256)


def project(normed, proj_in, group, out, place=0, width=256):
    for block in range(3):
        values = mm(normed[...], proj_in[:, columns(group, block)])
        out[:, columns(place, block, width)] = values.astype(BF16)


def softmax(scores):
    expo = jnp.exp(scores - jnp.max(scores, 1, keepdims=True))
    return expo * (1.0 / jnp.sum(expo, 1, keepdims=True))


def scores_of(key, query, bias):
    return by_head(mm_nt(stacked(key), query)) + bias


def bias_of(bias, group):
    return jnp.stack([bias[QUAD * group + n].T for n in range(QUAD)], 0)


def split_edges(values, outs):
    for start, out in zip(EDGE_STARTS, outs):
        out[...] = values[start : start + out.shape[0]].astype(BF16)


def joined(local_table, edge_tables, local, edges):
    total = mm(local_table[...], local[...])
    for edge_table, edge in zip(edge_tables, edges):
        total = total + mm(edge_table[...], edge[...])
    return total


def cotangent_kernel(
    cotangent_hbm, send_hbm, flat_out, lat, diag, lon, flat, cotangent, send, sems
):
    tokens_in, send_in = fetch(
        (cotangent_hbm, cotangent, sems.at[0]), (send_hbm, send, sems.at[1])
    )
    tokens_in.wait()
    tokens = grid_rows(cotangent, flat)
    flat_out[...] = tokens
    send_in.wait()
    split_edges(mm(send[...], tokens), (lat, diag, lon))


def first_forward_kernel(
    inputs_hbm, send_hbm, proj_in_hbm, proj_out_hbm, gain_hbm, bias_hbm,
    out, lat, diag, lon, attended, standard, inv_std, *rest,
):
    packed, probs = rest[:2], rest[2:4]
    flat, normed, inputs, send, proj_in, proj_out, gain, bias, sems = rest[4:]
    tokens_in, gain_in, weights_in, bias_in, weights_out, send_in = fetch(
        (inputs_hbm, inputs, sems.at[0]),
        (gain_hbm, gain, sems.at[1]),
        (proj_in_hbm.at[0], proj_in, sems.at[2]),
        (bias_hbm.at[0], bias, sems.at[3]),
        (proj_out_hbm.at[0], proj_out, sems.at[4]),
        (send_hbm, send, sems.at[5]),
    )
    tokens_in.wait()
    for row in range(ROWS):
        values = inputs[0, row].astype(F32)
        for window in range(WINDOWS):
            start = window * AREA + row * WIN
            flat[start : start + WIN, :] = values[window * WIN : (window + 1) * WIN]
    tokens = flat[...]
    hat, inv = standardized(tokens)
    standard[...] = hat
    inv_std[...] = jnp.broadcast_to(inv, (TOKENS, 128))
    gain_in.wait()
    normed[...] = (hat * gain[0:1, :]).astype(BF16)
    weights_in.wait()
    bias_in.wait()
    project(normed, proj_in, 0, packed[0], 0, 512)
    for group in range(4):
        if group < 3:
            half, place = divmod(group + 1, 2)
            project(normed, proj_in, group + 1, packed[half], place, 512)
        added = bias_of(bias, group)
        half, place = divmod(group, 2)
        for window in range(WINDOWS):
            rows = slice(window * AREA, (window + 1) * AREA)
            query, key, value = (packed[half][rows, columns(place, n, 512)] for n in range(3))
            rounded = softmax(scores_of(key, query, added)).astype(BF16)
            probs[half][window, QUAD * place : QUAD * place + QUAD] = rounded
            attended[rows, columns(group)] = merged(mm(flipped(rounded), value))
    weights_out.wait()
    send_in.wait()
    result = (flat[...] + mm(attended[...], proj_out[...])).astype(BF16)
    out[...] = result
    split_edges(mm(send[...], result), (lat, diag, lon))


def score_grad(weights, value, d_att):
    d_probs = by_head(mm_nt(stacked(value), d_att))
    d_scaled = weights * (d_probs - jnp.sum(d_probs * weights, 1, keepdims=True))
    return d_scaled.astype(BF16)


def norm_backward(d_norm, standard, inv_std, gain, grad):
    d_hat = d_norm * gain
    d_x = inv_std * (
        d_hat
        - jnp.mean(d_hat, -1, keepdims=True)
        - standard * jnp.mean(d_hat * standard, -1, keepdims=True)
    )
    return (grad + d_x).astype(BF16)


def write_out_grad(attended, grad, kept, sent):
    core = lax.axis_index("lon") % 2
    for pair in range(PAIRS):
        both = mm_tn(attended[:, pair * 128 : (pair + 1) * 128], grad[...])
        kept[pair] = jnp.where(core == 0, both[:64], both[64:])
        sent[pair] = jnp.where(core == 0, both[64:], both[:64]).astype(BF16)


def second_grad_kernel(
    local, lat, diag, lon, local_table, to_lat, to_diag, to_lon, proj_hbm,
    grad, d_att, proj, sem,
):
    (weights,) = fetch((proj_hbm.at[1], proj, sem))
    tables = (to_lat, to_diag, to_lon)
    grad[...] = joined(local_table, tables, local, (lat, diag, lon)).astype(BF16)
    weights.wait()
    d_att[...] = mm_nt(grad[...], proj[...]).astype(BF16)


def first_grad_kernel(
    local, lat, diag, lon, local_table, to_lat, to_diag, to_lon, attended, grad, kept, sent
):
    tables = (to_lat, to_diag, to_lon)
    grad[...] = joined(local_table, tables, local, (lat, diag, lon)).astype(BF16)
    write_out_grad(attended, grad, kept, sent)


def mask_kernel(
    region, diag_in, lon_in, bias_hbm, allowed, bias_out, diag, lon, bias, sem
):
    (bias_in,) = fetch((bias_hbm.at[1], bias, sem))
    diag[...] = diag_in[...]
    lon[...] = lon_in[...]
    token = lax.broadcasted_iota(jnp.int32, (AREA, 1), 0)
    row_of = (token * 171) >> 11
    col_of = token - 12 * row_of
    pick_row = (row_of == lax.broadcasted_iota(jnp.int32, (AREA, ROWS), 1)).astype(BF16)
    by_row = mm(pick_row, region[...].astype(F32).astype(BF16))
    for window in range(WINDOWS):
        column = lax.broadcasted_iota(jnp.int32, (AREA, COLS), 1)
        picked = jnp.where(column == col_of + 12 * window, by_row, 0.0)
        own = jnp.sum(picked, -1, keepdims=True)
        other = mm_nt(jnp.ones((AREA, COLS), BF16), picked.astype(BF16))
        allowed[window] = jnp.where(own == other, 0.0, -2e9)
    bias_in.wait()
    for head in range(HEADS):
        bias_out[head] = bias[head].T


def second_kernel(
    tokens_in, lat_in, diag_in, lon_in, grad, d_att,
    local_win, to_lat, to_diag, to_lon, send,
    proj_in_hbm, gain, bias, allowed,
    out, lat, diag, lon, attended, gain_grad,
    d_packed, standard, normed, proj_in, sem, *packed,
):
    (weights_in,) = fetch((proj_in_hbm.at[1], proj_in, sem))
    tables = (to_lat, to_diag, to_lon)
    tokens = joined(local_win, tables, tokens_in, (lat_in, diag_in, lon_in))
    hat, inv_std = standardized(tokens)
    standard[...] = hat
    normed[...] = (hat * gain[1:2, :]).astype(BF16)
    weights_in.wait()
    project(normed, proj_in, 0, packed[0])
    for group in range(4):
        if group < 3:
            project(normed, proj_in, group + 1, packed[group + 1])
        added = bias[QUAD * group : QUAD * group + QUAD]
        for window in range(WINDOWS):
            rows = slice(window * AREA, (window + 1) * AREA)
            query, key, value = (packed[group][rows, columns(n)] for n in range(3))
            d_out = d_att[rows, columns(group)]
            weights = softmax(scores_of(key, query, added) + allowed[window])
            rounded = weights.astype(BF16)
            d_scaled = score_grad(weights, value, d_out)
            flat_scaled = d_scaled.reshape(QUAD * AREA, AREA)
            flat_rounded = rounded.reshape(QUAD * AREA, AREA)
            d_packed[rows, columns(group, 1)] = merged(mm(flat_scaled, query))
            d_packed[rows, columns(group, 2)] = merged(mm(flat_rounded, d_out))
            attended[rows, columns(group)] = merged(mm(flipped(rounded), value))
            d_packed[rows, columns(group, 0)] = merged(mm(flipped(d_scaled), key))
    d_norm = mm_nt(d_packed[...], proj_in[...])
    gain_grad[...] = jnp.sum(d_norm * standard[...], 0, keepdims=True)
    result = norm_backward(d_norm, standard[...], inv_std, gain[1:2, :], grad[...].astype(F32))
    out[...] = result
    split_edges(mm(send[...], result), (lat, diag, lon))


def attention_grad(index, d_att, packed, probs, at_in, at_out, out):
    for window in range(WINDOWS):
        rows = slice(window * AREA, (window + 1) * AREA)
        query, key, value = (packed[rows, at] for at in at_in)
        d_out = d_att[rows, at_in[0]]
        rounded = probs[window, pl.ds(QUAD * index, QUAD)]
        d_scaled = score_grad(rounded.astype(F32), value, d_out)
        flat_scaled = d_scaled.reshape(QUAD * AREA, AREA)
        flat_rounded = rounded.reshape(QUAD * AREA, AREA)
        out[rows, at_out[1]] = merged(mm(flat_scaled, query))
        out[rows, at_out[2]] = merged(mm(flat_rounded, d_out))
        out[rows, at_out[0]] = merged(mm(flipped(d_scaled), key))


def first_half_kernel(grad, packed, probs, proj, out, d_att):
    d_att[...] = mm_nt(grad[...], proj[0, 0:512]).astype(BF16)
    for index in range(2):
        at = [columns(index, n, 512) for n in range(3)]
        attention_grad(index, d_att, packed, probs, at, at, out)


def second_half_kernel(
    part_a, grad, packed_in, probs, proj, standard, gain_second, proj_in_hbm,
    d_norm, gains, d_att, packed, proj_in, sem,
):
    (weights,) = fetch((proj_in_hbm.at[0], proj_in, sem))
    for block in range(3):
        packed[:, block * WIDTH : block * WIDTH + 512] = part_a[:, block * 512 : (block + 1) * 512]
    d_att[...] = mm_nt(grad[...], proj[0, 512:1024]).astype(BF16)

    def moving(start):
        return pl.ds(pl.multiple_of(start, 256), 256)

    def step(index, carry):
        at_in = [moving(index * 256 + n * 512) for n in range(3)]
        at_out = [moving(512 + index * 256 + n * WIDTH) for n in range(3)]
        attention_grad(index, d_att, packed_in, probs, at_in, at_out, packed)
        return carry

    lax.fori_loop(0, 2, step, 0)
    weights.wait()
    result = mm_nt(packed[...], proj_in[...])
    d_norm[...] = result
    gains[0:1, :] = jnp.sum(result * standard[...], 0, keepdims=True)
    gains[1:2, :] = gain_second[...]


def input_grad_kernel(d_norm, grad, standard, inv_std, gain, out, done, flat):
    done[...] = inv_std[0:8, :]
    result = norm_backward(
        d_norm[...], standard[...], inv_std[:, 0:1], gain[0:1, :], grad[...].astype(F32)
    )
    flat[...] = result.astype(F32)
    for row in range(ROWS):
        starts = [window * AREA + row * WIN for window in range(WINDOWS)]
        out[0, row] = jnp.concatenate([flat[s : s + WIN, :] for s in starts], 0).astype(BF16)


def split_x_kernel(kept, arrived, own, one, two, three, total):
    x = lax.axis_index("dp")
    for n in range(8):
        total[n] = (kept[n] + arrived[n].astype(F32)).reshape(8, 8, WIDTH)
    for n in range(8):
        for step, out in enumerate((own, one, two, three)):
            place = lax.rem(x + step, 4)
            rows = jnp.concatenate([total[n, place], total[n, 4 + place]], 0)
            out[n] = rows.astype(out.dtype)


def pair_of(values):
    high = values.astype(BF16)
    return high, (values - high.astype(F32)).astype(BF16)


def put_gains(out, start, values):
    high, low = pair_of(values)
    rows = jnp.concatenate([high.astype(F32), low.astype(F32), jnp.zeros((12, WIDTH), F32)], 0)
    out[start : start + 16] = rows.astype(BF16)


def taken_gains(part, start):
    rows = part[start : start + 16].astype(F32)
    return rows[0:2] + rows[2:4]


def split_y_kernel(kept, arrived, own, one, two, three):
    y = lax.axis_index("lon") // 4
    for step, out in enumerate((own, one, two, three)):
        place = lax.rem(y + step, 4)
        for n in range(2):
            terms = kept[2 * place + n] + arrived[2 * place + n].astype(F32)
            out[n * 64 : n * 64 + 64] = terms.astype(out.dtype)


def middle_y_kernel(
    kept, a, b, c, gains, gains_arrived, own, own_gains, one, two, three, total
):
    y = lax.axis_index("lon") // 4
    sums = gains[...] + gains_arrived[...]
    own_gains[...] = sums
    terms = kept[...] + a[...].astype(F32) + b[...].astype(F32) + c[...].astype(F32)
    total[...] = terms.reshape(4, 32, WIDTH)
    for step, out in enumerate((own, one, two, three)):
        out[0:32] = total[lax.rem(y + step, 4)].astype(out.dtype)
        if step:
            put_gains(out, 32, sums)


def middle_x_kernel(
    kept, a, b, c, second, gains, d, e, f,
    own, own_second, own_gains, one, two, three, total,
):
    x = lax.axis_index("dp")
    sums, others = gains[...], second[...]
    for part in (d, e, f):
        sums = sums + taken_gains(part, 32)
        others = others + part[0:32].astype(F32)
    own_gains[...] = sums
    own_second[...] = others
    terms = kept[...] + a[...].astype(F32) + b[...].astype(F32) + c[...].astype(F32)
    total[...] = terms.reshape(4, 4, 8, WIDTH)
    for step, out in enumerate((own, one, two, three)):
        place = lax.rem(x + step, 4)
        out[0:32] = jnp.concatenate([total[n, place] for n in range(4)], 0).astype(out.dtype)
        if step:
            put_gains(out, 32, sums)


def split_z_kernel(kept, second, gains, one, two, three, own, own_gains, *rest):
    outs, total = rest[:3], rest[3]
    near, far = lax.rem(lax.axis_index("lon") // 2, 2), lax.axis_index("lat")
    sums, terms = gains[...], kept[...]
    for part in (one, two, three):
        sums = sums + taken_gains(part, 32)
        terms = terms + part[0:32].astype(F32)
    own_gains[...] = sums
    total[0] = terms.reshape(2, 2, 8, WIDTH)
    total[1] = second[...].reshape(2, 2, 8, WIDTH)
    own[...] = jnp.concatenate([total[0, near, far], total[1, near, far]], 0)
    for step, out in enumerate(outs):
        near_at = near if step == 1 else 1 - near
        far_at = far if step == 0 else 1 - far
        rows = jnp.concatenate([total[0, near_at, far_at], total[1, near_at, far_at]], 0)
        out[0:16] = rows.astype(BF16)
        put_gains(out, 16, sums)


def final_kernel(kept, gains, one, two, three, rows, gain_rows):
    terms, sums = kept[...], gains[...]
    for part in (one, two, three):
        terms = terms + part[0:16].astype(F32)
        sums = sums + taken_gains(part, 16)
    rows[0] = terms[0:8]
    rows[1] = terms[8:16]
    place = (lax.axis_index("lon") * 2 + lax.axis_index("lat")) * 4 + lax.axis_index("dp")
    padded = jnp.concatenate([sums, jnp.zeros((6, WIDTH), F32)], 0)
    gain_rows[...] = pltpu.roll(padded, WIDTH - 8 * place, 1)[0:2, 0:8]


def over_lat(value):
    return lax.ppermute(value, "lat", [(0, 1), (1, 0)])


def over_lon(value, step):
    return lax.ppermute(value, "lon", [(i, (i + step) % 16) for i in range(16)])


def over_both(value, step):
    pairs = [(i * 2 + j, (i + step) % 16 * 2 + 1 - j) for i in range(16) for j in range(2)]
    return lax.ppermute(value, ("lon", "lat"), pairs)


def exchanged(lat, diag, lon, step):
    return over_lat(lat), over_both(diag, step), over_lon(lon, step)


def to_core(value):
    return lax.ppermute(value, "lon", [(i, i ^ 1) for i in range(16)])


def along_x(value, step):
    return lax.ppermute(value, "dp", [(i, (i + step) % 4) for i in range(4)])


def along_y(value, step):
    return lax.ppermute(value, "lon", [(i, (i + 4 * step) % 16) for i in range(16)])


def along_z(value, step):
    near, far = step % 2, step // 2
    pairs = [
        (i * 2 + j, (i ^ (2 * near)) * 2 + (j ^ far)) for i in range(16) for j in range(2)
    ]
    return lax.ppermute(value, ("lon", "lat"), pairs)


EDGE_OUTS = [((LAT, WIDTH), BF16), ((DIAG, WIDTH), BF16), ((LON, WIDTH), BF16)]
HALF_OUTS = [((PAIRS, 64, WIDTH), F32), ((PAIRS, 64, WIDTH), BF16)]
FLAT_OUT = ((TOKENS, WIDTH), BF16)
X_OUTS = [((8, 16, WIDTH), F32)] + [((8, 16, WIDTH), BF16)] * 3
GAINS = ((2, WIDTH), F32)
Y_OUTS = [((128, WIDTH), F32)] + [((128, WIDTH), BF16)] * 3
OWN = ((32, WIDTH), F32)
MIDDLE_OUTS = [((48, WIDTH), BF16)] * 3
Z_OUTS = [((16, WIDTH), F32), GAINS] + [((32, WIDTH), BF16)] * 3


def split_x(kept, sent):
    return call(
        split_x_kernel, X_OUTS, [pltpu.VMEM((8, 8, 8, WIDTH), F32)], (kept, to_core(sent)), micros=1
    )


def per_device(inputs, cotangent, qkv_weight, out_weight, norm_gain, position_bias, region_ids):
    flat = pltpu.VMEM((TOKENS, WIDTH), F32)
    tokens = pltpu.VMEM((TOKENS, WIDTH), BF16)
    grid = pltpu.VMEM((1, ROWS, COLS, WIDTH), BF16)
    sender = pltpu.VMEM((EDGES_PADDED, TOKENS), BF16)
    proj_in = pltpu.VMEM((WIDTH, 3 * WIDTH), BF16)
    proj_out = pltpu.VMEM((WIDTH, WIDTH), BF16)
    bias = pltpu.VMEM((HEADS, AREA, AREA), F32)
    wide = pltpu.VMEM((TOKENS, 3 * WIDTH), BF16)
    dma = pltpu.SemaphoreType.DMA
    cot, *cot_edges = call(
        cotangent_kernel,
        [FLAT_OUT] + EDGE_OUTS,
        [flat, grid, sender, dma((2,))],
        (cotangent, sender_table(SEND_OF_GRID)),
        hbm=(0, 1),
        micros=2,
    )
    cot_edges = exchanged(*cot_edges, -1)
    first_out, lat, diag, lon, attended, standard, inv_std, *saved = call(
        first_forward_kernel,
        [FLAT_OUT] + EDGE_OUTS
        + [FLAT_OUT, ((TOKENS, WIDTH), F32), ((TOKENS, 128), F32)]
        + [((TOKENS, 3 * 512), BF16)] * 2
        + [((WINDOWS, 2 * QUAD, AREA, AREA), BF16)] * 2,
        [
            flat, tokens, grid, sender, proj_in, proj_out, pltpu.VMEM((2, WIDTH), F32), bias,
            dma((6,)),
        ],
        (
            inputs, sender_table(SEND_OF_WIN), qkv_weight, out_weight, norm_gain,
            position_bias,
        ),
        hbm=range(6),
        after=(cot,),
        micros=12,
    )
    allowed, bias_second, diag, lon = call(
        mask_kernel,
        [((WINDOWS, AREA, AREA), F32), ((HEADS, AREA, AREA), F32)] + EDGE_OUTS[1:],
        [bias, dma],
        (region_ids, diag, lon, position_bias),
        hbm=(3,),
        after=cot_edges,
        micros=2,
    )
    edges = exchanged(lat, diag, lon, -1)
    grad_second, d_att = call(
        second_grad_kernel,
        [FLAT_OUT, FLAT_OUT],
        [proj_out, dma],
        (cot, *cot_edges, table(LOCAL_OF_GRID), *edge_tables(AHEAD_EDGE, 1), out_weight),
        hbm=(8,),
        after=(allowed,),
        micros=3,
    )
    back, lat, diag, lon, attended_second, gain_second = call(
        second_kernel,
        [FLAT_OUT] + EDGE_OUTS + [FLAT_OUT, ((1, WIDTH), F32)],
        [wide, flat, tokens, proj_in, dma] + [pltpu.VMEM((TOKENS, 768), BF16)] * 4,
        (
            first_out, *edges, grad_second, d_att, table(LOCAL_OF_WIN),
            *edge_tables(AHEAD_EDGE, 1), sender_table(AHEAD_EDGE.T), qkv_weight, norm_gain,
            bias_second, allowed,
        ),
        hbm=(11,),
        micros=19,
    )
    edges = exchanged(lat, diag, lon, 1)
    halves = call(write_out_grad, HALF_OUTS, [], (attended_second, grad_second), micros=2)
    own_second, *outs_second = split_x(*halves)
    shares_second = [along_x(out, step + 1) for step, out in enumerate(outs_second)]
    grad, *halves = call(
        first_grad_kernel,
        [FLAT_OUT] + HALF_OUTS,
        [],
        (back, *edges, table(LOCAL_OF_WIN.T), *edge_tables(SEND_OF_WIN.T, 1), attended),
        after=(*outs_second, shares_second[0], shares_second[2]),
        micros=3,
    )

    half = pltpu.VMEM((TOKENS, 512), BF16)
    (part_a,) = call(
        first_half_kernel,
        [((TOKENS, 3 * 512), BF16)],
        [half],
        (grad, saved[0], saved[2], out_weight),
        micros=4,
    )
    own_first, *outs_first = call(
        split_y_kernel, Y_OUTS, [], (halves[0], to_core(halves[1])), micros=1
    )
    shares_first = [along_y(out, step + 1) for step, out in enumerate(outs_first)]
    d_norm, gains = call(
        second_half_kernel,
        [((TOKENS, WIDTH), F32), GAINS],
        [half, wide, proj_in, dma],
        (part_a, grad, saved[1], saved[3], out_weight, standard, gain_second, qkv_weight),
        hbm=(7,),
        after=(*outs_first, shares_second[1]),
        micros=8,
    )
    own_second, own_gains, *outs = call(
        middle_y_kernel,
        [OWN, GAINS] + MIDDLE_OUTS,
        [pltpu.VMEM((4, 32, WIDTH), F32)],
        (own_second, *shares_second, gains, to_core(gains)),
        micros=0.05,
    )
    shares = [along_y(out, step + 1) for step, out in enumerate(outs)]
    result, done = call(
        input_grad_kernel,
        [((1, ROWS, COLS, WIDTH), BF16), ((8, 128), F32)],
        [flat],
        (d_norm, grad, standard, inv_std, norm_gain),
        after=(*outs, *shares_first),
        micros=1,
    )
    own_first, own_second, own_gains, *outs = call(
        middle_x_kernel,
        [OWN, OWN, GAINS] + MIDDLE_OUTS,
        [pltpu.VMEM((4, 4, 8, WIDTH), F32)],
        (own_first, *shares_first, own_second, own_gains, *shares),
        after=(done,),
        micros=0.05,
    )
    shares = [along_x(out, step + 1) for step, out in enumerate(outs)]
    own, own_gains, *outs = call(
        split_z_kernel,
        Z_OUTS,
        [pltpu.VMEM((2, 2, 2, 8, WIDTH), F32)],
        (own_first, own_second, own_gains, *shares),
        micros=0.05,
    )
    shares = [along_z(out, step + 1) for step, out in enumerate(outs)]
    rows, gain_rows = call(
        final_kernel, [((2, 8, WIDTH), F32), ((2, 8), F32)], [], (own, own_gains, *shares), micros=1
    )
    return result, rows, gain_rows


def solution(mesh):
    in_specs = (
        P("dp", "lat", "lon", None),
        P("dp", "lat", "lon", None),
        P(),
        P(),
        P(),
        P(),
        P("lat", "lon"),
    )
    out_specs = (
        P("dp", "lat", "lon", None),
        P(None, ("lon", "lat", "dp"), None),
        P(None, ("lon", "lat", "dp")),
    )
    return jax.shard_map(
        per_device, mesh=mesh, in_specs=in_specs, out_specs=out_specs, check_vma=False
    )
```

```python
import functools

import numpy as np

import jax
import jax.numpy as jnp
from jax import lax
from jax.experimental import pallas as pl
from jax.experimental.pallas import tpu as pltpu
from jax.sharding import PartitionSpec as P

WIN = 12
ROWS = 12
COLS = 36
TOKENS = 432
AREA = 144
WINDOWS = 3
WIDTH = 1024
HEADS = 16
PAIRS = 8
QUAD = 4
LAT, DIAG, LON, EDGES = 180, 36, 36, 252
EDGES_PADDED = 272
F32 = jnp.float32
BF16 = jnp.bfloat16
VMEM_LIMIT = 26 * 2**20


def tables():
    win = np.zeros((TOKENS, TOKENS), np.float32)
    local = np.zeros((TOKENS, TOKENS), np.float32)
    edge = np.zeros((TOKENS, EDGES), np.float32)
    send = np.zeros((EDGES, TOKENS), np.float32)
    for row in range(ROWS):
        for col in range(COLS):
            grid = row * COLS + col
            place = col // WIN * AREA + row * WIN + col % WIN
            win[place, grid] = 1
            if row + 6 < ROWS and col + 6 < COLS:
                local[place, grid + 6 * COLS + 6] = 1
            elif row + 6 < ROWS:
                edge[place, LAT + DIAG + row * 6 + col - 30] = 1
            elif col + 6 < COLS:
                edge[place, (row - 6) * 30 + col] = 1
            else:
                edge[place, LAT + (row - 6) * 6 + col - 30] = 1
            if row < 6 and col >= 6:
                send[row * 30 + col - 6, grid] = 1
            elif row < 6:
                send[LAT + row * 6 + col, grid] = 1
            elif col < 6:
                send[LAT + DIAG + (row - 6) * 6 + col, grid] = 1
    return win, local, edge, send


WIN_OF_GRID, LOCAL_OF_GRID, AHEAD_EDGE, SEND_OF_GRID = tables()
LOCAL_OF_WIN = LOCAL_OF_GRID @ WIN_OF_GRID.T
SEND_OF_WIN = SEND_OF_GRID @ WIN_OF_GRID.T


EDGE_STARTS = (0, 184, 224)


def sender_table(values):
    rows = np.zeros((EDGES_PADDED, TOKENS), np.float32)
    for start, part in zip(EDGE_STARTS, np.split(values, [LAT, LAT + DIAG])):
        rows[start : start + len(part)] = part
    return table(rows)


def table(values):
    return jnp.asarray(values, BF16)


def edge_tables(values, axis):
    return [table(part) for part in np.split(values, [LAT, LAT + DIAG], axis)]


def mm(a, b):
    return lax.dot_general(a, b, (((1,), (0,)), ((), ())), preferred_element_type=F32)


def mm_nt(a, b):
    return lax.dot_general(a, b, (((1,), (1,)), ((), ())), preferred_element_type=F32)


def mm_tn(a, b):
    return lax.dot_general(a, b, (((0,), (0,)), ((), ())), preferred_element_type=F32)


def call(kernel, outs, scratch, args, hbm=(), after=(), micros=10):
    count, last = len(args), len(args) + len(after)
    spaces = [pltpu.HBM if i in hbm else pltpu.VMEM for i in range(count)]
    spaces += [pl.ANY] * len(after)

    args = [
        pltpu.with_memory_space_constraint(arg, pltpu.HBM) if i in hbm else arg
        for i, arg in enumerate(args)
    ]

    def body(*refs):
        kernel(*refs[:count], *refs[last:])

    return pl.pallas_call(
        body,
        out_shape=[jax.ShapeDtypeStruct(shape, dtype) for shape, dtype in outs],
        in_specs=[pl.BlockSpec(memory_space=space) for space in spaces],
        out_specs=[pl.BlockSpec(memory_space=pltpu.VMEM)] * len(outs),
        scratch_shapes=scratch,
        compiler_params=pltpu.CompilerParams(vmem_limit_bytes=VMEM_LIMIT),
        cost_estimate=pl.CostEstimate(
            flops=int(micros * 1.15e9), transcendentals=0, bytes_accessed=2**20
        ),
    )(*args, *after)


def fetch(*copies):
    handles = [pltpu.make_async_copy(*copy) for copy in copies]
    for handle in handles:
        handle.start()
    return handles


def grid_rows(source, flat):
    for row in range(ROWS):
        flat[row * COLS : (row + 1) * COLS, :] = source[0, row].astype(F32)
    return flat[...].astype(BF16)


def standardized(tokens):
    centred = tokens - jnp.mean(tokens, -1, keepdims=True)
    inv_std = lax.rsqrt(jnp.mean(centred * centred, -1, keepdims=True) + 1e-05)
    return centred * inv_std, inv_std


def quarter(width=4 * 64):
    return lax.broadcasted_iota(jnp.int32, (1, width), 1) // 64


def stacked(values):
    parts = [values * jnp.where(quarter() == n, 0.125, 0.0).astype(BF16) for n in range(QUAD)]
    return jnp.concatenate(parts, 0)


def by_head(values):
    return values.reshape(QUAD, AREA, AREA)


def flipped(values):
    return jnp.concatenate([values[n].T for n in range(QUAD)], 0)


def merged(values):
    result = values[:AREA]
    for n in range(1, QUAD):
        result = jnp.where(quarter() == n, values[n * AREA : (n + 1) * AREA], result)
    return result.astype(BF16)


def columns(group, block=0, width=WIDTH):
    start = group * 256 + width * block
    return slice(start, start + 256)


def project(normed, proj_in, group, out, place=0, width=256):
    for block in range(3):
        values = mm(normed[...], proj_in[:, columns(group, block)])
        out[:, columns(place, block, width)] = values.astype(BF16)


def softmax(scores):
    expo = jnp.exp(scores - jnp.max(scores, 1, keepdims=True))
    return expo * (1.0 / jnp.sum(expo, 1, keepdims=True))


def scores_of(key, query, bias):
    return by_head(mm_nt(stacked(key), query)) + bias


def bias_of(bias, group):
    return jnp.stack([bias[QUAD * group + n].T for n in range(QUAD)], 0)


def split_edges(values, outs):
    for start, out in zip(EDGE_STARTS, outs):
        out[...] = values[start : start + out.shape[0]].astype(BF16)


def joined(local_table, edge_tables, local, edges):
    total = mm(local_table[...], local[...])
    for edge_table, edge in zip(edge_tables, edges):
        total = total + mm(edge_table[...], edge[...])
    return total


def cotangent_kernel(
    cotangent_hbm, send_hbm, flat_out, lat, diag, lon, flat, cotangent, send, sems
):
    tokens_in, send_in = fetch(
        (cotangent_hbm, cotangent, sems.at[0]), (send_hbm, send, sems.at[1])
    )
    tokens_in.wait()
    tokens = grid_rows(cotangent, flat)
    flat_out[...] = tokens
    send_in.wait()
    split_edges(mm(send[...], tokens), (lat, diag, lon))


def first_forward_kernel(
    inputs_hbm, send_hbm, proj_in_hbm, proj_out_hbm, gain_hbm, bias_hbm,
    out, lat, diag, lon, attended, standard, inv_std, *rest,
):
    packed, probs = rest[:2], rest[2:4]
    flat, normed, inputs, send, proj_in, proj_out, gain, bias, sems = rest[4:]
    tokens_in, gain_in, weights_in, bias_in, weights_out, send_in = fetch(
        (inputs_hbm, inputs, sems.at[0]),
        (gain_hbm, gain, sems.at[1]),
        (proj_in_hbm.at[0], proj_in, sems.at[2]),
        (bias_hbm.at[0], bias, sems.at[3]),
        (proj_out_hbm.at[0], proj_out, sems.at[4]),
        (send_hbm, send, sems.at[5]),
    )
    tokens_in.wait()
    for row in range(ROWS):
        values = inputs[0, row].astype(F32)
        for window in range(WINDOWS):
            start = window * AREA + row * WIN
            flat[start : start + WIN, :] = values[window * WIN : (window + 1) * WIN]
    tokens = flat[...]
    hat, inv = standardized(tokens)
    standard[...] = hat
    inv_std[...] = jnp.broadcast_to(inv, (TOKENS, 128))
    gain_in.wait()
    normed[...] = (hat * gain[0:1, :]).astype(BF16)
    weights_in.wait()
    bias_in.wait()
    project(normed, proj_in, 0, packed[0], 0, 512)
    for group in range(4):
        if group < 3:
            half, place = divmod(group + 1, 2)
            project(normed, proj_in, group + 1, packed[half], place, 512)
        added = bias_of(bias, group)
        half, place = divmod(group, 2)
        for window in range(WINDOWS):
            rows = slice(window * AREA, (window + 1) * AREA)
            query, key, value = (packed[half][rows, columns(place, n, 512)] for n in range(3))
            rounded = softmax(scores_of(key, query, added)).astype(BF16)
            probs[half][window, QUAD * place : QUAD * place + QUAD] = rounded
            attended[rows, columns(group)] = merged(mm(flipped(rounded), value))
    weights_out.wait()
    send_in.wait()
    result = (flat[...] + mm(attended[...], proj_out[...])).astype(BF16)
    out[...] = result
    split_edges(mm(send[...], result), (lat, diag, lon))


def score_grad(weights, value, d_att):
    d_probs = by_head(mm_nt(stacked(value), d_att))
    d_scaled = weights * (d_probs - jnp.sum(d_probs * weights, 1, keepdims=True))
    return d_scaled.astype(BF16)


def norm_backward(d_norm, standard, inv_std, gain, grad):
    d_hat = d_norm * gain
    d_x = inv_std * (
        d_hat
        - jnp.mean(d_hat, -1, keepdims=True)
        - standard * jnp.mean(d_hat * standard, -1, keepdims=True)
    )
    return (grad + d_x).astype(BF16)


def write_out_grad(attended, grad, kept, sent):
    core = lax.axis_index("lon") % 2
    for pair in range(PAIRS):
        both = mm_tn(attended[:, pair * 128 : (pair + 1) * 128], grad[...])
        kept[pair] = jnp.where(core == 0, both[:64], both[64:])
        sent[pair] = jnp.where(core == 0, both[64:], both[:64]).astype(BF16)


def second_grad_kernel(
    local, lat, diag, lon, local_table, to_lat, to_diag, to_lon, proj_hbm,
    grad, d_att, proj, sem,
):
    (weights,) = fetch((proj_hbm.at[1], proj, sem))
    tables = (to_lat, to_diag, to_lon)
    grad[...] = joined(local_table, tables, local, (lat, diag, lon)).astype(BF16)
    weights.wait()
    d_att[...] = mm_nt(grad[...], proj[...]).astype(BF16)


def first_grad_kernel(
    local, lat, diag, lon, local_table, to_lat, to_diag, to_lon, attended, grad, kept, sent
):
    tables = (to_lat, to_diag, to_lon)
    grad[...] = joined(local_table, tables, local, (lat, diag, lon)).astype(BF16)
    write_out_grad(attended, grad, kept, sent)


def mask_kernel(
    region, diag_in, lon_in, bias_hbm, allowed, bias_out, diag, lon, bias, sem
):
    (bias_in,) = fetch((bias_hbm.at[1], bias, sem))
    diag[...] = diag_in[...]
    lon[...] = lon_in[...]
    token = lax.broadcasted_iota(jnp.int32, (AREA, 1), 0)
    row_of = (token * 171) >> 11
    col_of = token - 12 * row_of
    pick_row = (row_of == lax.broadcasted_iota(jnp.int32, (AREA, ROWS), 1)).astype(BF16)
    by_row = mm(pick_row, region[...].astype(F32).astype(BF16))
    for window in range(WINDOWS):
        column = lax.broadcasted_iota(jnp.int32, (AREA, COLS), 1)
        picked = jnp.where(column == col_of + 12 * window, by_row, 0.0)
        own = jnp.sum(picked, -1, keepdims=True)
        other = mm_nt(jnp.ones((AREA, COLS), BF16), picked.astype(BF16))
        allowed[window] = jnp.where(own == other, 0.0, -2e9)
    bias_in.wait()
    for head in range(HEADS):
        bias_out[head] = bias[head].T


def second_kernel(
    tokens_in, lat_in, diag_in, lon_in, grad, d_att,
    local_win, to_lat, to_diag, to_lon, send,
    proj_in_hbm, gain, bias, allowed,
    out, lat, diag, lon, attended, gain_grad,
    d_packed, standard, normed, proj_in, sem, *packed,
):
    (weights_in,) = fetch((proj_in_hbm.at[1], proj_in, sem))
    tables = (to_lat, to_diag, to_lon)
    tokens = joined(local_win, tables, tokens_in, (lat_in, diag_in, lon_in))
    hat, inv_std = standardized(tokens)
    standard[...] = hat
    normed[...] = (hat * gain[1:2, :]).astype(BF16)
    weights_in.wait()
    project(normed, proj_in, 0, packed[0])
    for group in range(4):
        if group < 3:
            project(normed, proj_in, group + 1, packed[group + 1])
        added = bias[QUAD * group : QUAD * group + QUAD]
        for window in range(WINDOWS):
            rows = slice(window * AREA, (window + 1) * AREA)
            query, key, value = (packed[group][rows, columns(n)] for n in range(3))
            d_out = d_att[rows, columns(group)]
            weights = softmax(scores_of(key, query, added) + allowed[window])
            rounded = weights.astype(BF16)
            d_scaled = score_grad(weights, value, d_out)
            flat_scaled = d_scaled.reshape(QUAD * AREA, AREA)
            flat_rounded = rounded.reshape(QUAD * AREA, AREA)
            d_packed[rows, columns(group, 1)] = merged(mm(flat_scaled, query))
            d_packed[rows, columns(group, 2)] = merged(mm(flat_rounded, d_out))
            attended[rows, columns(group)] = merged(mm(flipped(rounded), value))
            d_packed[rows, columns(group, 0)] = merged(mm(flipped(d_scaled), key))
    d_norm = mm_nt(d_packed[...], proj_in[...])
    gain_grad[...] = jnp.sum(d_norm * standard[...], 0, keepdims=True)
    result = norm_backward(d_norm, standard[...], inv_std, gain[1:2, :], grad[...].astype(F32))
    out[...] = result
    split_edges(mm(send[...], result), (lat, diag, lon))


def attention_grad(index, d_att, packed, probs, at_in, at_out, out):
    for window in range(WINDOWS):
        rows = slice(window * AREA, (window + 1) * AREA)
        query, key, value = (packed[rows, at] for at in at_in)
        d_out = d_att[rows, at_in[0]]
        rounded = probs[window, pl.ds(QUAD * index, QUAD)]
        d_scaled = score_grad(rounded.astype(F32), value, d_out)
        flat_scaled = d_scaled.reshape(QUAD * AREA, AREA)
        flat_rounded = rounded.reshape(QUAD * AREA, AREA)
        out[rows, at_out[1]] = merged(mm(flat_scaled, query))
        out[rows, at_out[2]] = merged(mm(flat_rounded, d_out))
        out[rows, at_out[0]] = merged(mm(flipped(d_scaled), key))


def first_half_kernel(grad, packed, probs, proj, out, d_att):
    d_att[...] = mm_nt(grad[...], proj[0, 0:512]).astype(BF16)
    for index in range(2):
        at = [columns(index, n, 512) for n in range(3)]
        attention_grad(index, d_att, packed, probs, at, at, out)


def second_half_kernel(
    part_a, grad, packed_in, probs, proj, standard, gain_second, proj_in_hbm,
    d_norm, gains, d_att, packed, proj_in, sem,
):
    (weights,) = fetch((proj_in_hbm.at[0], proj_in, sem))
    for block in range(3):
        packed[:, block * WIDTH : block * WIDTH + 512] = part_a[:, block * 512 : (block + 1) * 512]
    d_att[...] = mm_nt(grad[...], proj[0, 512:1024]).astype(BF16)

    def moving(start):
        return pl.ds(pl.multiple_of(start, 256), 256)

    def step(index, carry):
        at_in = [moving(index * 256 + n * 512) for n in range(3)]
        at_out = [moving(512 + index * 256 + n * WIDTH) for n in range(3)]
        attention_grad(index, d_att, packed_in, probs, at_in, at_out, packed)
        return carry

    lax.fori_loop(0, 2, step, 0)
    weights.wait()
    result = mm_nt(packed[...], proj_in[...])
    d_norm[...] = result
    gains[0:1, :] = jnp.sum(result * standard[...], 0, keepdims=True)
    gains[1:2, :] = gain_second[...]


def input_grad_kernel(d_norm, grad, standard, inv_std, gain, out, done, flat):
    done[...] = inv_std[0:8, :]
    result = norm_backward(
        d_norm[...], standard[...], inv_std[:, 0:1], gain[0:1, :], grad[...].astype(F32)
    )
    flat[...] = result.astype(F32)
    for row in range(ROWS):
        starts = [window * AREA + row * WIN for window in range(WINDOWS)]
        out[0, row] = jnp.concatenate([flat[s : s + WIN, :] for s in starts], 0).astype(BF16)


def split_x_kernel(kept, arrived, own, one, two, three, total):
    x = lax.axis_index("dp")
    for n in range(8):
        total[n] = (kept[n] + arrived[n].astype(F32)).reshape(8, 8, WIDTH)
    for n in range(8):
        for step, out in enumerate((own, one, two, three)):
            place = lax.rem(x + step, 4)
            rows = jnp.concatenate([total[n, place], total[n, 4 + place]], 0)
            out[n] = rows.astype(out.dtype)


def pair_of(values):
    high = values.astype(BF16)
    return high, (values - high.astype(F32)).astype(BF16)


def put_gains(out, start, values):
    high, low = pair_of(values)
    rows = jnp.concatenate([high.astype(F32), low.astype(F32), jnp.zeros((4, WIDTH), F32)], 0)
    out[start : start + 8] = rows.astype(BF16)


def taken_gains(part, start):
    rows = part[start : start + 8].astype(F32)
    return rows[0:2] + rows[2:4]


def split_y_kernel(kept, arrived, own, one, two, three):
    y = lax.axis_index("lon") // 4
    for step, out in enumerate((own, one, two, three)):
        place = lax.rem(y + step, 4)
        for n in range(2):
            terms = kept[2 * place + n] + arrived[2 * place + n].astype(F32)
            out[n * 64 : n * 64 + 64] = terms.astype(out.dtype)


def middle_y_kernel(
    kept, a, b, c, gains, gains_arrived, own, own_gains, one, two, three, total
):
    y = lax.axis_index("lon") // 4
    sums = gains[...] + gains_arrived[...]
    own_gains[...] = sums
    terms = kept[...] + a[...].astype(F32) + b[...].astype(F32) + c[...].astype(F32)
    total[...] = terms.reshape(4, 32, WIDTH)
    for step, out in enumerate((own, one, two, three)):
        out[0:32] = total[lax.rem(y + step, 4)].astype(out.dtype)
        if step:
            put_gains(out, 32, sums)


def middle_x_kernel(
    kept, a, b, c, second, gains, d, e, f,
    own, own_second, own_gains, one, two, three, total,
):
    x = lax.axis_index("dp")
    sums, others = gains[...], second[...]
    for part in (d, e, f):
        sums = sums + taken_gains(part, 32)
        others = others + part[0:32].astype(F32)
    own_gains[...] = sums
    own_second[...] = others
    terms = kept[...] + a[...].astype(F32) + b[...].astype(F32) + c[...].astype(F32)
    total[...] = terms.reshape(4, 4, 8, WIDTH)
    for step, out in enumerate((own, one, two, three)):
        place = lax.rem(x + step, 4)
        out[0:32] = jnp.concatenate([total[n, place] for n in range(4)], 0).astype(out.dtype)
        if step:
            put_gains(out, 32, sums)


def split_z_kernel(kept, second, gains, one, two, three, own, own_gains, *rest):
    outs, total = rest[:3], rest[3]
    near, far = lax.rem(lax.axis_index("lon") // 2, 2), lax.axis_index("lat")
    sums, terms = gains[...], kept[...]
    for part in (one, two, three):
        sums = sums + taken_gains(part, 32)
        terms = terms + part[0:32].astype(F32)
    own_gains[...] = sums
    total[0] = terms.reshape(2, 2, 8, WIDTH)
    total[1] = second[...].reshape(2, 2, 8, WIDTH)
    own[...] = jnp.concatenate([total[0, near, far], total[1, near, far]], 0)
    for step, out in enumerate(outs):
        near_at = near if step == 1 else 1 - near
        far_at = far if step == 0 else 1 - far
        rows = jnp.concatenate([total[0, near_at, far_at], total[1, near_at, far_at]], 0)
        out[0:16] = rows.astype(BF16)
        put_gains(out, 16, sums)


def final_kernel(kept, gains, one, two, three, rows, gain_rows):
    terms, sums = kept[...], gains[...]
    for part in (one, two, three):
        terms = terms + part[0:16].astype(F32)
        sums = sums + taken_gains(part, 16)
    rows[0] = terms[0:8]
    rows[1] = terms[8:16]
    place = (lax.axis_index("lon") * 2 + lax.axis_index("lat")) * 4 + lax.axis_index("dp")
    padded = jnp.concatenate([sums, jnp.zeros((6, WIDTH), F32)], 0)
    gain_rows[...] = pltpu.roll(padded, WIDTH - 8 * place, 1)[0:2, 0:8]


def over_lat(value):
    return lax.ppermute(value, "lat", [(0, 1), (1, 0)])


def over_lon(value, step):
    return lax.ppermute(value, "lon", [(i, (i + step) % 16) for i in range(16)])


def over_both(value, step):
    pairs = [(i * 2 + j, (i + step) % 16 * 2 + 1 - j) for i in range(16) for j in range(2)]
    return lax.ppermute(value, ("lon", "lat"), pairs)


def exchanged(lat, diag, lon, step):
    return over_lat(lat), over_both(diag, step), over_lon(lon, step)


def to_core(value):
    return lax.ppermute(value, "lon", [(i, i ^ 1) for i in range(16)])


def along_x(value, step):
    return lax.ppermute(value, "dp", [(i, (i + step) % 4) for i in range(4)])


def along_y(value, step):
    return lax.ppermute(value, "lon", [(i, (i + 4 * step) % 16) for i in range(16)])


def along_z(value, step):
    near, far = step % 2, step // 2
    pairs = [
        (i * 2 + j, (i ^ (2 * near)) * 2 + (j ^ far)) for i in range(16) for j in range(2)
    ]
    return lax.ppermute(value, ("lon", "lat"), pairs)


EDGE_OUTS = [((LAT, WIDTH), BF16), ((DIAG, WIDTH), BF16), ((LON, WIDTH), BF16)]
HALF_OUTS = [((PAIRS, 64, WIDTH), F32), ((PAIRS, 64, WIDTH), BF16)]
FLAT_OUT = ((TOKENS, WIDTH), BF16)
X_OUTS = [((8, 16, WIDTH), F32)] + [((8, 16, WIDTH), BF16)] * 3
GAINS = ((2, WIDTH), F32)
Y_OUTS = [((128, WIDTH), F32)] + [((128, WIDTH), BF16)] * 3
OWN = ((32, WIDTH), F32)
MIDDLE_OUTS = [((40, WIDTH), BF16)] * 3
Z_OUTS = [((16, WIDTH), F32), GAINS] + [((24, WIDTH), BF16)] * 3


def split_x(kept, sent):
    return call(
        split_x_kernel, X_OUTS, [pltpu.VMEM((8, 8, 8, WIDTH), F32)], (kept, to_core(sent)), micros=1
    )


def per_device(inputs, cotangent, qkv_weight, out_weight, norm_gain, position_bias, region_ids):
    flat = pltpu.VMEM((TOKENS, WIDTH), F32)
    tokens = pltpu.VMEM((TOKENS, WIDTH), BF16)
    grid = pltpu.VMEM((1, ROWS, COLS, WIDTH), BF16)
    sender = pltpu.VMEM((EDGES_PADDED, TOKENS), BF16)
    proj_in = pltpu.VMEM((WIDTH, 3 * WIDTH), BF16)
    proj_out = pltpu.VMEM((WIDTH, WIDTH), BF16)
    bias = pltpu.VMEM((HEADS, AREA, AREA), F32)
    wide = pltpu.VMEM((TOKENS, 3 * WIDTH), BF16)
    dma = pltpu.SemaphoreType.DMA
    cot, *cot_edges = call(
        cotangent_kernel,
        [FLAT_OUT] + EDGE_OUTS,
        [flat, grid, sender, dma((2,))],
        (cotangent, sender_table(SEND_OF_GRID)),
        hbm=(0, 1),
        micros=2,
    )
    cot_edges = exchanged(*cot_edges, -1)
    first_out, lat, diag, lon, attended, standard, inv_std, *saved = call(
        first_forward_kernel,
        [FLAT_OUT] + EDGE_OUTS
        + [FLAT_OUT, ((TOKENS, WIDTH), F32), ((TOKENS, 128), F32)]
        + [((TOKENS, 3 * 512), BF16)] * 2
        + [((WINDOWS, 2 * QUAD, AREA, AREA), BF16)] * 2,
        [
            flat, tokens, grid, sender, proj_in, proj_out, pltpu.VMEM((2, WIDTH), F32), bias,
            dma((6,)),
        ],
        (
            inputs, sender_table(SEND_OF_WIN), qkv_weight, out_weight, norm_gain,
            position_bias,
        ),
        hbm=range(6),
        after=(cot,),
        micros=12,
    )
    allowed, bias_second, diag, lon = call(
        mask_kernel,
        [((WINDOWS, AREA, AREA), F32), ((HEADS, AREA, AREA), F32)] + EDGE_OUTS[1:],
        [bias, dma],
        (region_ids, diag, lon, position_bias),
        hbm=(3,),
        after=cot_edges,
        micros=2,
    )
    edges = exchanged(lat, diag, lon, -1)
    grad_second, d_att = call(
        second_grad_kernel,
        [FLAT_OUT, FLAT_OUT],
        [proj_out, dma],
        (cot, *cot_edges, table(LOCAL_OF_GRID), *edge_tables(AHEAD_EDGE, 1), out_weight),
        hbm=(8,),
        after=(allowed,),
        micros=3,
    )
    back, lat, diag, lon, attended_second, gain_second = call(
        second_kernel,
        [FLAT_OUT] + EDGE_OUTS + [FLAT_OUT, ((1, WIDTH), F32)],
        [wide, flat, tokens, proj_in, dma] + [pltpu.VMEM((TOKENS, 768), BF16)] * 4,
        (
            first_out, *edges, grad_second, d_att, table(LOCAL_OF_WIN),
            *edge_tables(AHEAD_EDGE, 1), sender_table(AHEAD_EDGE.T), qkv_weight, norm_gain,
            bias_second, allowed,
        ),
        hbm=(11,),
        micros=19,
    )
    edges = exchanged(lat, diag, lon, 1)
    halves = call(write_out_grad, HALF_OUTS, [], (attended_second, grad_second), micros=2)
    own_second, *outs_second = split_x(*halves)
    shares_second = [along_x(out, step + 1) for step, out in enumerate(outs_second)]
    grad, *halves = call(
        first_grad_kernel,
        [FLAT_OUT] + HALF_OUTS,
        [],
        (back, *edges, table(LOCAL_OF_WIN.T), *edge_tables(SEND_OF_WIN.T, 1), attended),
        after=(*outs_second, shares_second[0], shares_second[2]),
        micros=3,
    )

    half = pltpu.VMEM((TOKENS, 512), BF16)
    (part_a,) = call(
        first_half_kernel,
        [((TOKENS, 3 * 512), BF16)],
        [half],
        (grad, saved[0], saved[2], out_weight),
        micros=4,
    )
    own_first, *outs_first = call(
        split_y_kernel, Y_OUTS, [], (halves[0], to_core(halves[1])), micros=1
    )
    shares_first = [along_y(out, step + 1) for step, out in enumerate(outs_first)]
    d_norm, gains = call(
        second_half_kernel,
        [((TOKENS, WIDTH), F32), GAINS],
        [half, wide, proj_in, dma],
        (part_a, grad, saved[1], saved[3], out_weight, standard, gain_second, qkv_weight),
        hbm=(7,),
        after=(*outs_first, shares_second[1]),
        micros=8,
    )
    own_second, own_gains, *outs = call(
        middle_y_kernel,
        [OWN, GAINS] + MIDDLE_OUTS,
        [pltpu.VMEM((4, 32, WIDTH), F32)],
        (own_second, *shares_second, gains, to_core(gains)),
        after=(shares_first[0],),
        micros=0.05,
    )
    shares = [along_y(out, step + 1) for step, out in enumerate(outs)]
    own_first, own_second, own_gains, *outs = call(
        middle_x_kernel,
        [OWN, OWN, GAINS] + MIDDLE_OUTS,
        [pltpu.VMEM((4, 4, 8, WIDTH), F32)],
        (own_first, *shares_first, own_second, own_gains, *shares),
        micros=0.05,
    )
    shares = [along_x(out, step + 1) for step, out in enumerate(outs)]
    own, own_gains, *outs = call(
        split_z_kernel,
        Z_OUTS,
        [pltpu.VMEM((2, 2, 2, 8, WIDTH), F32)],
        (own_first, own_second, own_gains, *shares),
        micros=0.05,
    )
    result, done = call(
        input_grad_kernel,
        [((1, ROWS, COLS, WIDTH), BF16), ((8, 128), F32)],
        [flat],
        (d_norm, grad, standard, inv_std, norm_gain),
        after=outs,
        micros=1,
    )
    shares = [along_z(out, step + 1) for step, out in enumerate(outs)]
    rows, gain_rows = call(
        final_kernel, [((2, 8, WIDTH), F32), ((2, 8), F32)], [], (own, own_gains, *shares),
        after=(done,), micros=1,
    )
    return result, rows, gain_rows


def solution(mesh):
    in_specs = (
        P("dp", "lat", "lon", None),
        P("dp", "lat", "lon", None),
        P(),
        P(),
        P(),
        P(),
        P("lat", "lon"),
    )
    out_specs = (
        P("dp", "lat", "lon", None),
        P(None, ("lon", "lat", "dp"), None),
        P(None, ("lon", "lat", "dp")),
    )
    return jax.shard_map(
        per_device, mesh=mesh, in_specs=in_specs, out_specs=out_specs, check_vma=False
    )
```

```python
import functools

import numpy as np

import jax
import jax.numpy as jnp
from jax import lax
from jax.experimental import pallas as pl
from jax.experimental.pallas import tpu as pltpu
from jax.sharding import PartitionSpec as P

WIN = 12
ROWS = 12
COLS = 36
TOKENS = 432
AREA = 144
WINDOWS = 3
WIDTH = 1024
HEADS = 16
PAIRS = 8
QUAD = 4
LAT, DIAG, LON, EDGES = 180, 36, 36, 252
EDGES_PADDED = 272
F32 = jnp.float32
BF16 = jnp.bfloat16
VMEM_LIMIT = 26 * 2**20


def tables():
    win = np.zeros((TOKENS, TOKENS), np.float32)
    local = np.zeros((TOKENS, TOKENS), np.float32)
    edge = np.zeros((TOKENS, EDGES), np.float32)
    send = np.zeros((EDGES, TOKENS), np.float32)
    for row in range(ROWS):
        for col in range(COLS):
            grid = row * COLS + col
            place = col // WIN * AREA + row * WIN + col % WIN
            win[place, grid] = 1
            if row + 6 < ROWS and col + 6 < COLS:
                local[place, grid + 6 * COLS + 6] = 1
            elif row + 6 < ROWS:
                edge[place, LAT + DIAG + row * 6 + col - 30] = 1
            elif col + 6 < COLS:
                edge[place, (row - 6) * 30 + col] = 1
            else:
                edge[place, LAT + (row - 6) * 6 + col - 30] = 1
            if row < 6 and col >= 6:
                send[row * 30 + col - 6, grid] = 1
            elif row < 6:
                send[LAT + row * 6 + col, grid] = 1
            elif col < 6:
                send[LAT + DIAG + (row - 6) * 6 + col, grid] = 1
    return win, local, edge, send


WIN_OF_GRID, LOCAL_OF_GRID, AHEAD_EDGE, SEND_OF_GRID = tables()
LOCAL_OF_WIN = LOCAL_OF_GRID @ WIN_OF_GRID.T
SEND_OF_WIN = SEND_OF_GRID @ WIN_OF_GRID.T


EDGE_STARTS = (0, 184, 224)


def sender_table(values):
    rows = np.zeros((EDGES_PADDED, TOKENS), np.float32)
    for start, part in zip(EDGE_STARTS, np.split(values, [LAT, LAT + DIAG])):
        rows[start : start + len(part)] = part
    return table(rows)


def table(values):
    return jnp.asarray(values, BF16)


def edge_tables(values, axis):
    return [table(part) for part in np.split(values, [LAT, LAT + DIAG], axis)]


def mm(a, b):
    return lax.dot_general(a, b, (((1,), (0,)), ((), ())), preferred_element_type=F32)


def mm_nt(a, b):
    return lax.dot_general(a, b, (((1,), (1,)), ((), ())), preferred_element_type=F32)


def mm_tn(a, b):
    return lax.dot_general(a, b, (((0,), (0,)), ((), ())), preferred_element_type=F32)


def call(kernel, outs, scratch, args, hbm=(), after=(), micros=10):
    count, last = len(args), len(args) + len(after)
    spaces = [pltpu.HBM if i in hbm else pltpu.VMEM for i in range(count)]
    spaces += [pl.ANY] * len(after)

    args = [
        pltpu.with_memory_space_constraint(arg, pltpu.HBM) if i in hbm else arg
        for i, arg in enumerate(args)
    ]

    def body(*refs):
        kernel(*refs[:count], *refs[last:])

    return pl.pallas_call(
        body,
        out_shape=[jax.ShapeDtypeStruct(shape, dtype) for shape, dtype in outs],
        in_specs=[pl.BlockSpec(memory_space=space) for space in spaces],
        out_specs=[pl.BlockSpec(memory_space=pltpu.VMEM)] * len(outs),
        scratch_shapes=scratch,
        compiler_params=pltpu.CompilerParams(vmem_limit_bytes=VMEM_LIMIT),
        cost_estimate=pl.CostEstimate(
            flops=int(micros * 1.15e9), transcendentals=0, bytes_accessed=2**20
        ),
    )(*args, *after)


def fetch(*copies):
    handles = [pltpu.make_async_copy(*copy) for copy in copies]
    for handle in handles:
        handle.start()
    return handles


def grid_rows(source, flat):
    for row in range(ROWS):
        flat[row * COLS : (row + 1) * COLS, :] = source[0, row].astype(F32)
    return flat[:TOKENS].astype(BF16)


def standardized(tokens):
    centred = tokens - jnp.mean(tokens, -1, keepdims=True)
    inv_std = lax.rsqrt(jnp.mean(centred * centred, -1, keepdims=True) + 1e-05)
    return centred * inv_std, inv_std


def quarter(width=4 * 64):
    return lax.broadcasted_iota(jnp.int32, (1, width), 1) // 64


def stacked(values):
    parts = [values * jnp.where(quarter() == n, 0.125, 0.0).astype(BF16) for n in range(QUAD)]
    return jnp.concatenate(parts, 0)


def by_head(values):
    return values.reshape(QUAD, AREA, AREA)


def flipped(values):
    return jnp.concatenate([values[n].T for n in range(QUAD)], 0)


def merged(values):
    result = values[:AREA]
    for n in range(1, QUAD):
        result = jnp.where(quarter() == n, values[n * AREA : (n + 1) * AREA], result)
    return result.astype(BF16)


def columns(group, block=0, width=WIDTH):
    start = group * 256 + width * block
    return slice(start, start + 256)


def project(normed, proj_in, group, out, place=0, width=256):
    for block in range(3):
        values = mm(normed[...], proj_in[:, columns(group, block)])
        out[:, columns(place, block, width)] = values.astype(BF16)


def softmax(scores):
    expo = jnp.exp(scores - jnp.max(scores, 1, keepdims=True))
    return expo * (1.0 / jnp.sum(expo, 1, keepdims=True))


def scores_of(key, query, bias):
    return by_head(mm_nt(stacked(key), query)) + bias


def bias_of(bias, group):
    return jnp.stack([bias[QUAD * group + n].T for n in range(QUAD)], 0)


def split_edges(values, outs):
    for start, out in zip(EDGE_STARTS, outs):
        out[...] = values[start : start + out.shape[0]].astype(BF16)


def joined(local_table, edge_tables, local, edges):
    total = mm(local_table[...], local[...])
    for edge_table, edge in zip(edge_tables, edges):
        total = total + mm(edge_table[...], edge[...])
    return total


def cotangent_kernel(
    cotangent_hbm, send_hbm, flat_out, lat, diag, lon, flat, cotangent, send, sems
):
    tokens_in, send_in = fetch(
        (cotangent_hbm, cotangent, sems.at[0]), (send_hbm, send, sems.at[1])
    )
    tokens_in.wait()
    tokens = grid_rows(cotangent, flat)
    flat_out[...] = tokens
    send_in.wait()
    split_edges(mm(send[...], tokens), (lat, diag, lon))


def first_forward_kernel(
    inputs_hbm, send_hbm, proj_in_hbm, proj_out_hbm, gain_hbm, bias_hbm,
    out, lat, diag, lon, attended, standard, inv_std, *rest,
):
    packed, probs = rest[:2], rest[2:4]
    flat, normed, inputs, send, proj_in, proj_out, gain, bias, sems = rest[4:]
    tokens_in, gain_in, weights_in, bias_in, weights_out, send_in = fetch(
        (inputs_hbm, inputs, sems.at[0]),
        (gain_hbm, gain, sems.at[1]),
        (proj_in_hbm.at[0], proj_in, sems.at[2]),
        (bias_hbm.at[0], bias, sems.at[3]),
        (proj_out_hbm.at[0], proj_out, sems.at[4]),
        (send_hbm, send, sems.at[5]),
    )
    tokens_in.wait()
    for row in range(ROWS):
        values = inputs[0, row].astype(F32)
        for window in range(WINDOWS):
            start = window * AREA + row * WIN
            flat[start : start + WIN, :] = values[window * WIN : (window + 1) * WIN]
    tokens = flat[:TOKENS]
    hat, inv = standardized(tokens)
    standard[...] = hat
    inv_std[...] = jnp.broadcast_to(inv, (TOKENS, 128))
    gain_in.wait()
    normed[...] = (hat * gain[0:1, :]).astype(BF16)
    weights_in.wait()
    bias_in.wait()
    project(normed, proj_in, 0, packed[0], 0, 512)
    for group in range(4):
        if group < 3:
            half, place = divmod(group + 1, 2)
            project(normed, proj_in, group + 1, packed[half], place, 512)
        added = bias_of(bias, group)
        half, place = divmod(group, 2)
        for window in range(WINDOWS):
            rows = slice(window * AREA, (window + 1) * AREA)
            query, key, value = (packed[half][rows, columns(place, n, 512)] for n in range(3))
            rounded = softmax(scores_of(key, query, added)).astype(BF16)
            probs[half][window, QUAD * place : QUAD * place + QUAD] = rounded
            attended[rows, columns(group)] = merged(mm(flipped(rounded), value))
    weights_out.wait()
    send_in.wait()
    result = (flat[:TOKENS] + mm(attended[...], proj_out[...])).astype(BF16)
    out[...] = result
    split_edges(mm(send[...], result), (lat, diag, lon))


def score_grad(weights, value, d_att):
    d_probs = by_head(mm_nt(stacked(value), d_att))
    d_scaled = weights * (d_probs - jnp.sum(d_probs * weights, 1, keepdims=True))
    return d_scaled.astype(BF16)


def norm_backward(d_norm, standard, inv_std, gain, grad):
    d_hat = d_norm * gain
    d_x = inv_std * (
        d_hat
        - jnp.mean(d_hat, -1, keepdims=True)
        - standard * jnp.mean(d_hat * standard, -1, keepdims=True)
    )
    return (grad + d_x).astype(BF16)


def write_out_grad(attended, grad, kept, sent):
    core = lax.axis_index("lon") % 2
    for pair in range(PAIRS):
        both = mm_tn(attended[:, pair * 128 : (pair + 1) * 128], grad[...])
        kept[pair] = jnp.where(core == 0, both[:64], both[64:])
        sent[pair] = jnp.where(core == 0, both[64:], both[:64]).astype(BF16)


def second_grad_kernel(
    local, lat, diag, lon, local_table, to_lat, to_diag, to_lon, proj_hbm,
    grad, d_att, proj, sem,
):
    (weights,) = fetch((proj_hbm.at[1], proj, sem))
    tables = (to_lat, to_diag, to_lon)
    grad[...] = joined(local_table, tables, local, (lat, diag, lon)).astype(BF16)
    weights.wait()
    d_att[...] = mm_nt(grad[...], proj[...]).astype(BF16)


def first_grad_kernel(
    local, lat, diag, lon, local_table, to_lat, to_diag, to_lon, attended, grad, kept, sent
):
    tables = (to_lat, to_diag, to_lon)
    grad[...] = joined(local_table, tables, local, (lat, diag, lon)).astype(BF16)
    write_out_grad(attended, grad, kept, sent)


def mask_kernel(
    region, diag_in, lon_in, bias_hbm, allowed, bias_out, diag, lon, bias, sem
):
    (bias_in,) = fetch((bias_hbm.at[1], bias, sem))
    diag[...] = diag_in[...]
    lon[...] = lon_in[...]
    token = lax.broadcasted_iota(jnp.int32, (AREA, 1), 0)
    row_of = (token * 171) >> 11
    col_of = token - 12 * row_of
    pick_row = (row_of == lax.broadcasted_iota(jnp.int32, (AREA, ROWS), 1)).astype(BF16)
    by_row = mm(pick_row, region[...].astype(F32).astype(BF16))
    for window in range(WINDOWS):
        column = lax.broadcasted_iota(jnp.int32, (AREA, COLS), 1)
        picked = jnp.where(column == col_of + 12 * window, by_row, 0.0)
        own = jnp.sum(picked, -1, keepdims=True)
        other = mm_nt(jnp.ones((AREA, COLS), BF16), picked.astype(BF16))
        allowed[window] = jnp.where(own == other, 0.0, -2e9)
    bias_in.wait()
    for head in range(HEADS):
        bias_out[head] = bias[head].T


def second_kernel(
    tokens_in, lat_in, diag_in, lon_in, grad, d_att,
    local_win, to_lat, to_diag, to_lon, send,
    proj_in_hbm, gain, bias, allowed,
    out, lat, diag, lon, attended, gain_grad,
    d_packed, standard, normed, proj_in, sem, *packed,
):
    (weights_in,) = fetch((proj_in_hbm.at[1], proj_in, sem))
    tables = (to_lat, to_diag, to_lon)
    tokens = joined(local_win, tables, tokens_in, (lat_in, diag_in, lon_in))
    hat, inv_std = standardized(tokens)
    standard[...] = hat
    normed[...] = (hat * gain[1:2, :]).astype(BF16)
    weights_in.wait()
    project(normed, proj_in, 0, packed[0])
    for group in range(4):
        if group < 3:
            project(normed, proj_in, group + 1, packed[group + 1])
        added = bias[QUAD * group : QUAD * group + QUAD]
        for window in range(WINDOWS):
            rows = slice(window * AREA, (window + 1) * AREA)
            query, key, value = (packed[group][rows, columns(n)] for n in range(3))
            d_out = d_att[rows, columns(group)]
            weights = softmax(scores_of(key, query, added) + allowed[window])
            rounded = weights.astype(BF16)
            d_scaled = score_grad(weights, value, d_out)
            flat_scaled = d_scaled.reshape(QUAD * AREA, AREA)
            flat_rounded = rounded.reshape(QUAD * AREA, AREA)
            d_packed[rows, columns(group, 1)] = merged(mm(flat_scaled, query))
            d_packed[rows, columns(group, 2)] = merged(mm(flat_rounded, d_out))
            attended[rows, columns(group)] = merged(mm(flipped(rounded), value))
            d_packed[rows, columns(group, 0)] = merged(mm(flipped(d_scaled), key))
    d_norm = mm_nt(d_packed[...], proj_in[...])
    gain_grad[...] = jnp.sum(d_norm * standard[...], 0, keepdims=True)
    result = norm_backward(d_norm, standard[...], inv_std, gain[1:2, :], grad[...].astype(F32))
    out[...] = result
    split_edges(mm(send[...], result), (lat, diag, lon))


def attention_grad(index, d_att, packed, probs, at_in, at_out, out):
    for window in range(WINDOWS):
        rows = slice(window * AREA, (window + 1) * AREA)
        query, key, value = (packed[rows, at] for at in at_in)
        d_out = d_att[rows, at_in[0]]
        rounded = probs[window, pl.ds(QUAD * index, QUAD)]
        d_scaled = score_grad(rounded.astype(F32), value, d_out)
        flat_scaled = d_scaled.reshape(QUAD * AREA, AREA)
        flat_rounded = rounded.reshape(QUAD * AREA, AREA)
        out[rows, at_out[1]] = merged(mm(flat_scaled, query))
        out[rows, at_out[2]] = merged(mm(flat_rounded, d_out))
        out[rows, at_out[0]] = merged(mm(flipped(d_scaled), key))


def first_half_kernel(grad, packed, probs, proj, out, d_att):
    d_att[...] = mm_nt(grad[...], proj[0, 0:512]).astype(BF16)
    for index in range(2):
        at = [columns(index, n, 512) for n in range(3)]
        attention_grad(index, d_att, packed, probs, at, at, out)


def second_half_kernel(
    part_a, grad, packed_in, probs, proj, standard, gain_second, proj_in_hbm,
    d_norm, gains, d_att, packed, proj_in, sem,
):
    (weights,) = fetch((proj_in_hbm.at[0], proj_in, sem))
    for block in range(3):
        packed[:, block * WIDTH : block * WIDTH + 512] = part_a[:, block * 512 : (block + 1) * 512]
    d_att[...] = mm_nt(grad[...], proj[0, 512:1024]).astype(BF16)

    def moving(start):
        return pl.ds(pl.multiple_of(start, 256), 256)

    def step(index, carry):
        at_in = [moving(index * 256 + n * 512) for n in range(3)]
        at_out = [moving(512 + index * 256 + n * WIDTH) for n in range(3)]
        attention_grad(index, d_att, packed_in, probs, at_in, at_out, packed)
        return carry

    lax.fori_loop(0, 2, step, 0)
    weights.wait()
    result = mm_nt(packed[...], proj_in[...])
    d_norm[...] = result
    gain_first = jnp.sum(result * standard[...], 0, keepdims=True)
    gains[...] = jnp.concatenate([gain_first, gain_second[...]], 0)


def input_grad_kernel(d_norm, grad, standard, inv_std, gain, out, done, flat):
    done[...] = inv_std[0:8, :]
    result = norm_backward(
        d_norm[...], standard[...], inv_std[:, 0:1], gain[0:1, :], grad[...].astype(F32)
    )
    flat[:TOKENS] = result.astype(F32)
    for row in range(ROWS):
        starts = [window * AREA + row * WIN for window in range(WINDOWS)]
        out[0, row] = jnp.concatenate([flat[s : s + WIN, :] for s in starts], 0).astype(BF16)


def split_x_kernel(kept, arrived, own, one, two, three, total):
    x = lax.axis_index("dp")
    for n in range(8):
        total[n] = (kept[n] + arrived[n].astype(F32)).reshape(8, 8, WIDTH)
    for n in range(8):
        for step, out in enumerate((own, one, two, three)):
            place = lax.rem(x + step, 4)
            rows = jnp.concatenate([total[n, place], total[n, 4 + place]], 0)
            out[n] = rows.astype(out.dtype)


def pair_of(values):
    high = values.astype(BF16)
    return high, (values - high.astype(F32)).astype(BF16)


def put_gains(out, start, values):
    high, low = pair_of(values)
    rows = jnp.concatenate([high.astype(F32), low.astype(F32), jnp.zeros((4, WIDTH), F32)], 0)
    out[start : start + 8] = rows.astype(BF16)


def taken_gains(part, start):
    rows = part[start : start + 8].astype(F32)
    return rows[0:2] + rows[2:4]


def split_y_kernel(kept, arrived, own, one, two, three):
    y = lax.axis_index("lon") // 4
    for step, out in enumerate((own, one, two, three)):
        place = lax.rem(y + step, 4)
        for n in range(2):
            terms = kept[2 * place + n] + arrived[2 * place + n].astype(F32)
            out[n * 64 : n * 64 + 64] = terms.astype(out.dtype)


def middle_y_kernel(
    kept, a, b, c, gains, gains_arrived, own, own_gains, one, two, three, total
):
    y = lax.axis_index("lon") // 4
    sums = gains[...] + gains_arrived[...]
    own_gains[...] = sums
    terms = kept[...] + a[...].astype(F32) + b[...].astype(F32) + c[...].astype(F32)
    total[...] = terms.reshape(4, 32, WIDTH)
    for step, out in enumerate((own, one, two, three)):
        out[0:32] = total[lax.rem(y + step, 4)].astype(out.dtype)
        if step:
            put_gains(out, 32, sums)


def middle_x_kernel(
    kept, a, b, c, second, gains, d, e, f,
    own, own_second, own_gains, one, two, three, total,
):
    x = lax.axis_index("dp")
    sums, others = gains[...], second[...]
    for part in (d, e, f):
        sums = sums + taken_gains(part, 32)
        others = others + part[0:32].astype(F32)
    own_gains[...] = sums
    own_second[...] = others
    terms = kept[...] + a[...].astype(F32) + b[...].astype(F32) + c[...].astype(F32)
    total[...] = terms.reshape(4, 4, 8, WIDTH)
    for step, out in enumerate((own, one, two, three)):
        place = lax.rem(x + step, 4)
        out[0:32] = jnp.concatenate([total[n, place] for n in range(4)], 0).astype(out.dtype)
        if step:
            put_gains(out, 32, sums)


def split_z_kernel(kept, second, gains, one, two, three, own, own_gains, *rest):
    outs, total = rest[:3], rest[3]
    near, far = lax.rem(lax.axis_index("lon") // 2, 2), lax.axis_index("lat")
    sums, terms = gains[...], kept[...]
    for part in (one, two, three):
        sums = sums + taken_gains(part, 32)
        terms = terms + part[0:32].astype(F32)
    own_gains[...] = sums
    total[0] = terms.reshape(2, 2, 8, WIDTH)
    total[1] = second[...].reshape(2, 2, 8, WIDTH)
    own[...] = jnp.concatenate([total[0, near, far], total[1, near, far]], 0)
    for step, out in enumerate(outs):
        near_at = near if step == 1 else 1 - near
        far_at = far if step == 0 else 1 - far
        rows = jnp.concatenate([total[0, near_at, far_at], total[1, near_at, far_at]], 0)
        out[0:16] = rows.astype(BF16)
        put_gains(out, 16, sums)


def final_kernel(kept, gains, one, two, three, rows, gain_rows):
    terms, sums = kept[...], gains[...]
    for part in (one, two, three):
        terms = terms + part[0:16].astype(F32)
        sums = sums + taken_gains(part, 16)
    rows[0] = terms[0:8]
    rows[1] = terms[8:16]
    place = (lax.axis_index("lon") * 2 + lax.axis_index("lat")) * 4 + lax.axis_index("dp")
    padded = jnp.concatenate([sums, jnp.zeros((6, WIDTH), F32)], 0)
    gain_rows[...] = pltpu.roll(padded, lax.rem(WIDTH - 8 * place, WIDTH), 1)[0:2, 0:8]


def over_lat(value):
    return lax.ppermute(value, "lat", [(0, 1), (1, 0)])


def over_lon(value, step):
    return lax.ppermute(value, "lon", [(i, (i + step) % 16) for i in range(16)])


def over_both(value, step):
    pairs = [(i * 2 + j, (i + step) % 16 * 2 + 1 - j) for i in range(16) for j in range(2)]
    return lax.ppermute(value, ("lon", "lat"), pairs)


def exchanged(lat, diag, lon, step):
    return over_lat(lat), over_both(diag, step), over_lon(lon, step)


def to_core(value):
    return lax.ppermute(value, "lon", [(i, i ^ 1) for i in range(16)])


def along_x(value, step):
    return lax.ppermute(value, "dp", [(i, (i + step) % 4) for i in range(4)])


def along_y(value, step):
    return lax.ppermute(value, "lon", [(i, (i + 4 * step) % 16) for i in range(16)])


def along_z(value, step):
    near, far = step % 2, step // 2
    pairs = [
        (i * 2 + j, (i ^ (2 * near)) * 2 + (j ^ far)) for i in range(16) for j in range(2)
    ]
    return lax.ppermute(value, ("lon", "lat"), pairs)


EDGE_OUTS = [((LAT, WIDTH), BF16), ((DIAG, WIDTH), BF16), ((LON, WIDTH), BF16)]
HALF_OUTS = [((PAIRS, 64, WIDTH), F32), ((PAIRS, 64, WIDTH), BF16)]
FLAT_OUT = ((TOKENS, WIDTH), BF16)
X_OUTS = [((8, 16, WIDTH), F32)] + [((8, 16, WIDTH), BF16)] * 3
GAINS = ((2, WIDTH), F32)
Y_OUTS = [((128, WIDTH), F32)] + [((128, WIDTH), BF16)] * 3
OWN = ((32, WIDTH), F32)
MIDDLE_OUTS = [((40, WIDTH), BF16)] * 3
Z_OUTS = [((16, WIDTH), F32), GAINS] + [((24, WIDTH), BF16)] * 3


def split_x(kept, sent):
    return call(
        split_x_kernel, X_OUTS, [pltpu.VMEM((8, 8, 8, WIDTH), F32)], (kept, to_core(sent)), micros=1
    )


def per_device(inputs, cotangent, qkv_weight, out_weight, norm_gain, position_bias, region_ids):
    flat = pltpu.VMEM((TOKENS + 8, WIDTH), F32)
    square = pltpu.VMEM((TOKENS, WIDTH), F32)
    tokens = pltpu.VMEM((TOKENS, WIDTH), BF16)
    grid = pltpu.VMEM((1, ROWS, COLS, WIDTH), BF16)
    sender = pltpu.VMEM((EDGES_PADDED, TOKENS), BF16)
    proj_in = pltpu.VMEM((WIDTH, 3 * WIDTH), BF16)
    proj_out = pltpu.VMEM((WIDTH, WIDTH), BF16)
    bias = pltpu.VMEM((HEADS, AREA, AREA), F32)
    wide = pltpu.VMEM((TOKENS, 3 * WIDTH), BF16)
    dma = pltpu.SemaphoreType.DMA
    cot, *cot_edges = call(
        cotangent_kernel,
        [FLAT_OUT] + EDGE_OUTS,
        [flat, grid, sender, dma((2,))],
        (cotangent, sender_table(SEND_OF_GRID)),
        hbm=(0, 1),
        micros=2,
    )
    cot_edges = exchanged(*cot_edges, -1)
    first_out, lat, diag, lon, attended, standard, inv_std, *saved = call(
        first_forward_kernel,
        [FLAT_OUT] + EDGE_OUTS
        + [FLAT_OUT, ((TOKENS, WIDTH), F32), ((TOKENS, 128), F32)]
        + [((TOKENS, 3 * 512), BF16)] * 2
        + [((WINDOWS, 2 * QUAD, AREA, AREA), BF16)] * 2,
        [
            flat, tokens, grid, sender, proj_in, proj_out, pltpu.VMEM((2, WIDTH), F32), bias,
            dma((6,)),
        ],
        (
            inputs, sender_table(SEND_OF_WIN), qkv_weight, out_weight, norm_gain,
            position_bias,
        ),
        hbm=range(6),
        after=(cot,),
        micros=12,
    )
    allowed, bias_second, diag, lon = call(
        mask_kernel,
        [((WINDOWS, AREA, AREA), F32), ((HEADS, AREA, AREA), F32)] + EDGE_OUTS[1:],
        [bias, dma],
        (region_ids, diag, lon, position_bias),
        hbm=(3,),
        after=cot_edges,
        micros=2,
    )
    edges = exchanged(lat, diag, lon, -1)
    grad_second, d_att = call(
        second_grad_kernel,
        [FLAT_OUT, FLAT_OUT],
        [proj_out, dma],
        (cot, *cot_edges, table(LOCAL_OF_GRID), *edge_tables(AHEAD_EDGE, 1), out_weight),
        hbm=(8,),
        after=(allowed,),
        micros=3,
    )
    back, lat, diag, lon, attended_second, gain_second = call(
        second_kernel,
        [FLAT_OUT] + EDGE_OUTS + [FLAT_OUT, ((1, WIDTH), F32)],
        [wide, square, tokens, proj_in, dma] + [pltpu.VMEM((TOKENS, 768), BF16)] * 4,
        (
            first_out, *edges, grad_second, d_att, table(LOCAL_OF_WIN),
            *edge_tables(AHEAD_EDGE, 1), sender_table(AHEAD_EDGE.T), qkv_weight, norm_gain,
            bias_second, allowed,
        ),
        hbm=(11,),
        micros=19,
    )
    edges = exchanged(lat, diag, lon, 1)
    halves = call(write_out_grad, HALF_OUTS, [], (attended_second, grad_second), micros=2)
    own_second, *outs_second = split_x(*halves)
    shares_second = [along_x(out, step + 1) for step, out in enumerate(outs_second)]
    grad, *halves = call(
        first_grad_kernel,
        [FLAT_OUT] + HALF_OUTS,
        [],
        (back, *edges, table(LOCAL_OF_WIN.T), *edge_tables(SEND_OF_WIN.T, 1), attended),
        after=(*outs_second, shares_second[0], shares_second[2]),
        micros=3,
    )

    half = pltpu.VMEM((TOKENS, 512), BF16)
    (part_a,) = call(
        first_half_kernel,
        [((TOKENS, 3 * 512), BF16)],
        [half],
        (grad, saved[0], saved[2], out_weight),
        micros=4,
    )
    own_first, *outs_first = call(
        split_y_kernel, Y_OUTS, [], (halves[0], to_core(halves[1])), micros=1
    )
    shares_first = [along_y(out, step + 1) for step, out in enumerate(outs_first)]
    d_norm, gains = call(
        second_half_kernel,
        [((TOKENS, WIDTH), F32), GAINS],
        [half, wide, proj_in, dma],
        (part_a, grad, saved[1], saved[3], out_weight, standard, gain_second, qkv_weight),
        hbm=(7,),
        after=(*outs_first, shares_second[1]),
        micros=8,
    )
    own_second, own_gains, *outs = call(
        middle_y_kernel,
        [OWN, GAINS] + MIDDLE_OUTS,
        [pltpu.VMEM((4, 32, WIDTH), F32)],
        (own_second, *shares_second, gains, to_core(gains)),
        after=(shares_first[0],),
        micros=0.05,
    )
    shares = [along_y(out, step + 1) for step, out in enumerate(outs)]
    own_first, own_second, own_gains, *outs = call(
        middle_x_kernel,
        [OWN, OWN, GAINS] + MIDDLE_OUTS,
        [pltpu.VMEM((4, 4, 8, WIDTH), F32)],
        (own_first, *shares_first, own_second, own_gains, *shares),
        micros=0.05,
    )
    shares = [along_x(out, step + 1) for step, out in enumerate(outs)]
    own, own_gains, *outs = call(
        split_z_kernel,
        Z_OUTS,
        [pltpu.VMEM((2, 2, 2, 8, WIDTH), F32)],
        (own_first, own_second, own_gains, *shares),
        micros=0.05,
    )
    result, done = call(
        input_grad_kernel,
        [((1, ROWS, COLS, WIDTH), BF16), ((8, 128), F32)],
        [flat],
        (d_norm, grad, standard, inv_std, norm_gain),
        after=outs,
        micros=1,
    )
    shares = [along_z(out, step + 1) for step, out in enumerate(outs)]
    rows, gain_rows = call(
        final_kernel, [((2, 8, WIDTH), F32), ((2, 8), F32)], [], (own, own_gains, *shares),
        after=(done,), micros=1,
    )
    return result, rows, gain_rows


def solution(mesh):
    in_specs = (
        P("dp", "lat", "lon", None),
        P("dp", "lat", "lon", None),
        P(),
        P(),
        P(),
        P(),
        P("lat", "lon"),
    )
    out_specs = (
        P("dp", "lat", "lon", None),
        P(None, ("lon", "lat", "dp"), None),
        P(None, ("lon", "lat", "dp")),
    )
    return jax.shard_map(
        per_device, mesh=mesh, in_specs=in_specs, out_specs=out_specs, check_vma=False
    )
```

```python
import functools

import numpy as np

import jax
import jax.numpy as jnp
from jax import lax
from jax.experimental import pallas as pl
from jax.experimental.pallas import tpu as pltpu
from jax.sharding import PartitionSpec as P

WIN = 12
ROWS = 12
COLS = 36
TOKENS = 432
AREA = 144
WINDOWS = 3
WIDTH = 1024
HEADS = 16
PAIRS = 8
QUAD = 4
LAT, DIAG, LON, EDGES = 180, 36, 36, 252
EDGES_PADDED = 272
F32 = jnp.float32
BF16 = jnp.bfloat16
VMEM_LIMIT = 26 * 2**20


def tables():
    win = np.zeros((TOKENS, TOKENS), np.float32)
    local = np.zeros((TOKENS, TOKENS), np.float32)
    edge = np.zeros((TOKENS, EDGES), np.float32)
    send = np.zeros((EDGES, TOKENS), np.float32)
    for row in range(ROWS):
        for col in range(COLS):
            grid = row * COLS + col
            place = col // WIN * AREA + row * WIN + col % WIN
            win[place, grid] = 1
            if row + 6 < ROWS and col + 6 < COLS:
                local[place, grid + 6 * COLS + 6] = 1
            elif row + 6 < ROWS:
                edge[place, LAT + DIAG + row * 6 + col - 30] = 1
            elif col + 6 < COLS:
                edge[place, (row - 6) * 30 + col] = 1
            else:
                edge[place, LAT + (row - 6) * 6 + col - 30] = 1
            if row < 6 and col >= 6:
                send[row * 30 + col - 6, grid] = 1
            elif row < 6:
                send[LAT + row * 6 + col, grid] = 1
            elif col < 6:
                send[LAT + DIAG + (row - 6) * 6 + col, grid] = 1
    return win, local, edge, send


WIN_OF_GRID, LOCAL_OF_GRID, AHEAD_EDGE, SEND_OF_GRID = tables()
LOCAL_OF_WIN = LOCAL_OF_GRID @ WIN_OF_GRID.T
SEND_OF_WIN = SEND_OF_GRID @ WIN_OF_GRID.T


EDGE_STARTS = (0, 184, 224)


def sender_table(values):
    rows = np.zeros((EDGES_PADDED, TOKENS), np.float32)
    for start, part in zip(EDGE_STARTS, np.split(values, [LAT, LAT + DIAG])):
        rows[start : start + len(part)] = part
    return table(rows)


def table(values):
    return jnp.asarray(values, BF16)


def edge_tables(values, axis):
    return [table(part) for part in np.split(values, [LAT, LAT + DIAG], axis)]


def mm(a, b):
    return lax.dot_general(a, b, (((1,), (0,)), ((), ())), preferred_element_type=F32)


def mm_nt(a, b):
    return lax.dot_general(a, b, (((1,), (1,)), ((), ())), preferred_element_type=F32)


def mm_tn(a, b):
    return lax.dot_general(a, b, (((0,), (0,)), ((), ())), preferred_element_type=F32)


def call(kernel, outs, scratch, args, hbm=(), after=(), micros=10):
    count, last = len(args), len(args) + len(after)
    spaces = [pltpu.HBM if i in hbm else pltpu.VMEM for i in range(count)]
    spaces += [pl.ANY] * len(after)

    args = [
        pltpu.with_memory_space_constraint(arg, pltpu.HBM) if i in hbm else arg
        for i, arg in enumerate(args)
    ]

    def body(*refs):
        kernel(*refs[:count], *refs[last:])

    return pl.pallas_call(
        body,
        out_shape=[jax.ShapeDtypeStruct(shape, dtype) for shape, dtype in outs],
        in_specs=[pl.BlockSpec(memory_space=space) for space in spaces],
        out_specs=[pl.BlockSpec(memory_space=pltpu.VMEM)] * len(outs),
        scratch_shapes=scratch,
        compiler_params=pltpu.CompilerParams(vmem_limit_bytes=VMEM_LIMIT),
        cost_estimate=pl.CostEstimate(
            flops=int(micros * 1.15e9), transcendentals=0, bytes_accessed=2**20
        ),
    )(*args, *after)


def fetch(*copies):
    handles = [pltpu.make_async_copy(*copy) for copy in copies]
    for handle in handles:
        handle.start()
    return handles


def grid_rows(source, flat):
    for row in range(ROWS):
        flat[row * COLS : (row + 1) * COLS, :] = source[0, row].astype(F32)
    return flat[:TOKENS].astype(BF16)


def standardized(tokens):
    centred = tokens - jnp.mean(tokens, -1, keepdims=True)
    inv_std = lax.rsqrt(jnp.mean(centred * centred, -1, keepdims=True) + 1e-05)
    return centred * inv_std, inv_std


def quarter(width=4 * 64):
    return lax.broadcasted_iota(jnp.int32, (1, width), 1) // 64


def stacked(values):
    parts = [values * jnp.where(quarter() == n, 0.125, 0.0).astype(BF16) for n in range(QUAD)]
    return jnp.concatenate(parts, 0)


def by_head(values):
    return values.reshape(QUAD, AREA, AREA)


def flipped(values):
    return jnp.concatenate([values[n].T for n in range(QUAD)], 0)


def merged(values):
    result = values[:AREA]
    for n in range(1, QUAD):
        result = jnp.where(quarter() == n, values[n * AREA : (n + 1) * AREA], result)
    return result.astype(BF16)


def columns(group, block=0, width=WIDTH):
    start = group * 256 + width * block
    return slice(start, start + 256)


def project(normed, proj_in, group, out, place=0, width=256):
    for block in range(3):
        values = mm(normed[...], proj_in[:, columns(group, block)])
        out[:, columns(place, block, width)] = values.astype(BF16)


def softmax(scores):
    expo = jnp.exp(scores - jnp.max(scores, 1, keepdims=True))
    return expo * (1.0 / jnp.sum(expo, 1, keepdims=True))


def scores_of(key, query, bias):
    return by_head(mm_nt(stacked(key), query)) + bias


def bias_of(bias, group):
    return jnp.stack([bias[QUAD * group + n].T for n in range(QUAD)], 0)


def split_edges(values, outs):
    for start, out in zip(EDGE_STARTS, outs):
        out[...] = values[start : start + out.shape[0]].astype(BF16)


def joined(local_table, edge_tables, local, edges):
    total = mm(local_table[...], local[...])
    for edge_table, edge in zip(edge_tables, edges):
        total = total + mm(edge_table[...], edge[...])
    return total


def cotangent_kernel(
    cotangent_hbm, send_hbm, flat_out, lat, diag, lon, flat, cotangent, send, sems
):
    tokens_in, send_in = fetch(
        (cotangent_hbm, cotangent, sems.at[0]), (send_hbm, send, sems.at[1])
    )
    tokens_in.wait()
    tokens = grid_rows(cotangent, flat)
    flat_out[...] = tokens
    send_in.wait()
    split_edges(mm(send[...], tokens), (lat, diag, lon))


def first_forward_kernel(
    inputs_hbm, send_hbm, proj_in_hbm, proj_out_hbm, gain_hbm, bias_hbm,
    out, lat, diag, lon, attended, standard, inv_std, *rest,
):
    packed, probs = rest[:2], rest[2:4]
    flat, normed, inputs, send, proj_in, proj_out, gain, bias, sems = rest[4:]
    tokens_in, gain_in, weights_in, bias_in, weights_out, send_in = fetch(
        (inputs_hbm, inputs, sems.at[0]),
        (gain_hbm, gain, sems.at[1]),
        (proj_in_hbm.at[0], proj_in, sems.at[2]),
        (bias_hbm.at[0], bias, sems.at[3]),
        (proj_out_hbm.at[0], proj_out, sems.at[4]),
        (send_hbm, send, sems.at[5]),
    )
    tokens_in.wait()
    for row in range(ROWS):
        values = inputs[0, row].astype(F32)
        for window in range(WINDOWS):
            start = window * AREA + row * WIN
            flat[start : start + WIN, :] = values[window * WIN : (window + 1) * WIN]
    tokens = flat[:TOKENS]
    hat, inv = standardized(tokens)
    standard[...] = hat
    inv_std[...] = jnp.broadcast_to(inv, (TOKENS, 128))
    gain_in.wait()
    normed[...] = (hat * gain[0:1, :]).astype(BF16)
    weights_in.wait()
    bias_in.wait()
    project(normed, proj_in, 0, packed[0], 0, 512)
    for group in range(4):
        if group < 3:
            half, place = divmod(group + 1, 2)
            project(normed, proj_in, group + 1, packed[half], place, 512)
        added = bias_of(bias, group)
        half, place = divmod(group, 2)
        for window in range(WINDOWS):
            rows = slice(window * AREA, (window + 1) * AREA)
            query, key, value = (packed[half][rows, columns(place, n, 512)] for n in range(3))
            rounded = softmax(scores_of(key, query, added)).astype(BF16)
            probs[half][window, QUAD * place : QUAD * place + QUAD] = rounded
            attended[rows, columns(group)] = merged(mm(flipped(rounded), value))
    weights_out.wait()
    send_in.wait()
    result = (flat[:TOKENS] + mm(attended[...], proj_out[...])).astype(BF16)
    out[...] = result
    split_edges(mm(send[...], result), (lat, diag, lon))


def score_grad(weights, value, d_att):
    d_probs = by_head(mm_nt(stacked(value), d_att))
    d_scaled = weights * (d_probs - jnp.sum(d_probs * weights, 1, keepdims=True))
    return d_scaled.astype(BF16)


def norm_backward(d_norm, standard, inv_std, gain, grad):
    d_hat = d_norm * gain
    d_x = inv_std * (
        d_hat
        - jnp.mean(d_hat, -1, keepdims=True)
        - standard * jnp.mean(d_hat * standard, -1, keepdims=True)
    )
    return (grad + d_x).astype(BF16)


def write_out_grad(attended, grad, kept, sent):
    core = lax.axis_index("lon") % 2
    for pair in range(PAIRS):
        both = mm_tn(attended[:, pair * 128 : (pair + 1) * 128], grad[...])
        kept[pair] = jnp.where(core == 0, both[:64], both[64:])
        sent[pair] = jnp.where(core == 0, both[64:], both[:64]).astype(BF16)


def second_grad_kernel(
    local, lat, diag, lon, local_table, to_lat, to_diag, to_lon, proj_hbm,
    grad, d_att, proj, sem,
):
    (weights,) = fetch((proj_hbm.at[1], proj, sem))
    tables = (to_lat, to_diag, to_lon)
    grad[...] = joined(local_table, tables, local, (lat, diag, lon)).astype(BF16)
    weights.wait()
    d_att[...] = mm_nt(grad[...], proj[...]).astype(BF16)


def first_grad_kernel(
    local, lat, diag, lon, local_table, to_lat, to_diag, to_lon, attended, grad, kept, sent
):
    tables = (to_lat, to_diag, to_lon)
    grad[...] = joined(local_table, tables, local, (lat, diag, lon)).astype(BF16)
    write_out_grad(attended, grad, kept, sent)


def mask_kernel(
    region, diag_in, lon_in, bias_hbm, allowed, bias_out, diag, lon, bias, sem
):
    (bias_in,) = fetch((bias_hbm.at[1], bias, sem))
    diag[...] = diag_in[...]
    lon[...] = lon_in[...]
    token = lax.broadcasted_iota(jnp.int32, (AREA, 1), 0)
    row_of = (token * 171) >> 11
    col_of = token - 12 * row_of
    pick_row = (row_of == lax.broadcasted_iota(jnp.int32, (AREA, ROWS), 1)).astype(BF16)
    by_row = mm(pick_row, region[...].astype(F32).astype(BF16))
    for window in range(WINDOWS):
        column = lax.broadcasted_iota(jnp.int32, (AREA, COLS), 1)
        picked = jnp.where(column == col_of + 12 * window, by_row, 0.0)
        own = jnp.sum(picked, -1, keepdims=True)
        other = mm_nt(jnp.ones((AREA, COLS), BF16), picked.astype(BF16))
        allowed[window] = jnp.where(own == other, 0.0, -2e9)
    bias_in.wait()
    for head in range(HEADS):
        bias_out[head] = bias[head].T


def second_kernel(
    tokens_in, lat_in, diag_in, lon_in, grad, d_att,
    local_win, to_lat, to_diag, to_lon, send,
    proj_in_hbm, gain, bias, allowed,
    out, lat, diag, lon, kept, sent, gain_grad,
    attended, d_packed, standard, normed, proj_in, sem, *packed,
):
    (weights_in,) = fetch((proj_in_hbm.at[1], proj_in, sem))
    tables = (to_lat, to_diag, to_lon)
    tokens = joined(local_win, tables, tokens_in, (lat_in, diag_in, lon_in))
    hat, inv_std = standardized(tokens)
    standard[...] = hat
    normed[...] = (hat * gain[1:2, :]).astype(BF16)
    weights_in.wait()
    project(normed, proj_in, 0, packed[0])
    for group in range(4):
        if group < 3:
            project(normed, proj_in, group + 1, packed[group + 1])
        added = bias[QUAD * group : QUAD * group + QUAD]
        for window in range(WINDOWS):
            rows = slice(window * AREA, (window + 1) * AREA)
            query, key, value = (packed[group][rows, columns(n)] for n in range(3))
            d_out = d_att[rows, columns(group)]
            weights = softmax(scores_of(key, query, added) + allowed[window])
            rounded = weights.astype(BF16)
            d_scaled = score_grad(weights, value, d_out)
            flat_scaled = d_scaled.reshape(QUAD * AREA, AREA)
            flat_rounded = rounded.reshape(QUAD * AREA, AREA)
            d_packed[rows, columns(group, 1)] = merged(mm(flat_scaled, query))
            d_packed[rows, columns(group, 2)] = merged(mm(flat_rounded, d_out))
            attended[rows, columns(group)] = merged(mm(flipped(rounded), value))
            d_packed[rows, columns(group, 0)] = merged(mm(flipped(d_scaled), key))
    write_out_grad(attended, grad, kept, sent)
    d_norm = mm_nt(d_packed[...], proj_in[...])
    gain_grad[...] = jnp.sum(d_norm * standard[...], 0, keepdims=True)
    result = norm_backward(d_norm, standard[...], inv_std, gain[1:2, :], grad[...].astype(F32))
    out[...] = result
    split_edges(mm(send[...], result), (lat, diag, lon))


def attention_grad(index, d_att, packed, probs, at_in, at_out, out):
    for window in range(WINDOWS):
        rows = slice(window * AREA, (window + 1) * AREA)
        query, key, value = (packed[rows, at] for at in at_in)
        d_out = d_att[rows, at_in[0]]
        rounded = probs[window, pl.ds(QUAD * index, QUAD)]
        d_scaled = score_grad(rounded.astype(F32), value, d_out)
        flat_scaled = d_scaled.reshape(QUAD * AREA, AREA)
        flat_rounded = rounded.reshape(QUAD * AREA, AREA)
        out[rows, at_out[1]] = merged(mm(flat_scaled, query))
        out[rows, at_out[2]] = merged(mm(flat_rounded, d_out))
        out[rows, at_out[0]] = merged(mm(flipped(d_scaled), key))


def first_half_kernel(grad, packed, probs, proj, out, d_att):
    d_att[...] = mm_nt(grad[...], proj[0, 0:512]).astype(BF16)
    for index in range(2):
        at = [columns(index, n, 512) for n in range(3)]
        attention_grad(index, d_att, packed, probs, at, at, out)


def second_half_kernel(
    part_a, grad, packed_in, probs, proj, standard, gain_second, proj_in_hbm,
    d_norm, gains, d_att, packed, proj_in, sem,
):
    (weights,) = fetch((proj_in_hbm.at[0], proj_in, sem))
    for block in range(3):
        packed[:, block * WIDTH : block * WIDTH + 512] = part_a[:, block * 512 : (block + 1) * 512]
    d_att[...] = mm_nt(grad[...], proj[0, 512:1024]).astype(BF16)

    def moving(start):
        return pl.ds(pl.multiple_of(start, 256), 256)

    def step(index, carry):
        at_in = [moving(index * 256 + n * 512) for n in range(3)]
        at_out = [moving(512 + index * 256 + n * WIDTH) for n in range(3)]
        attention_grad(index, d_att, packed_in, probs, at_in, at_out, packed)
        return carry

    lax.fori_loop(0, 2, step, 0)
    weights.wait()
    result = mm_nt(packed[...], proj_in[...])
    d_norm[...] = result
    gain_first = jnp.sum(result * standard[...], 0, keepdims=True)
    gains[...] = jnp.concatenate([gain_first, gain_second[...]], 0)


def input_grad_kernel(d_norm, grad, standard, inv_std, gain, out, done, flat):
    done[...] = inv_std[0:8, :]
    result = norm_backward(
        d_norm[...], standard[...], inv_std[:, 0:1], gain[0:1, :], grad[...].astype(F32)
    )
    flat[:TOKENS] = result.astype(F32)
    for row in range(ROWS):
        starts = [window * AREA + row * WIN for window in range(WINDOWS)]
        out[0, row] = jnp.concatenate([flat[s : s + WIN, :] for s in starts], 0).astype(BF16)


def split_x_kernel(kept, arrived, own, one, two, three, total):
    x = lax.axis_index("dp")
    for n in range(8):
        total[n] = (kept[n] + arrived[n].astype(F32)).reshape(8, 8, WIDTH)
    for n in range(8):
        for step, out in enumerate((own, one, two, three)):
            place = lax.rem(x + step, 4)
            rows = jnp.concatenate([total[n, place], total[n, 4 + place]], 0)
            out[n] = rows.astype(out.dtype)


def pair_of(values):
    high = values.astype(BF16)
    return high, (values - high.astype(F32)).astype(BF16)


def put_gains(out, start, values):
    high, low = pair_of(values)
    rows = jnp.concatenate([high.astype(F32), low.astype(F32), jnp.zeros((4, WIDTH), F32)], 0)
    out[start : start + 8] = rows.astype(BF16)


def taken_gains(part, start):
    rows = part[start : start + 8].astype(F32)
    return rows[0:2] + rows[2:4]


def split_y_kernel(kept, arrived, own, one, two, three):
    y = lax.axis_index("lon") // 4
    for step, out in enumerate((own, one, two, three)):
        place = lax.rem(y + step, 4)
        for n in range(2):
            terms = kept[2 * place + n] + arrived[2 * place + n].astype(F32)
            out[n * 64 : n * 64 + 64] = terms.astype(out.dtype)


def middle_y_kernel(
    kept, a, b, c, gains, gains_arrived, own, own_gains, one, two, three, total
):
    y = lax.axis_index("lon") // 4
    sums = gains[...] + gains_arrived[...]
    own_gains[...] = sums
    terms = kept[...] + a[...].astype(F32) + b[...].astype(F32) + c[...].astype(F32)
    total[...] = terms.reshape(4, 32, WIDTH)
    for step, out in enumerate((own, one, two, three)):
        out[0:32] = total[lax.rem(y + step, 4)].astype(out.dtype)
        if step:
            put_gains(out, 32, sums)


def middle_x_kernel(
    kept, a, b, c, second, gains, d, e, f,
    own, own_second, own_gains, one, two, three, total,
):
    x = lax.axis_index("dp")
    sums, others = gains[...], second[...]
    for part in (d, e, f):
        sums = sums + taken_gains(part, 32)
        others = others + part[0:32].astype(F32)
    own_gains[...] = sums
    own_second[...] = others
    terms = kept[...] + a[...].astype(F32) + b[...].astype(F32) + c[...].astype(F32)
    total[...] = terms.reshape(4, 4, 8, WIDTH)
    for step, out in enumerate((own, one, two, three)):
        place = lax.rem(x + step, 4)
        out[0:32] = jnp.concatenate([total[n, place] for n in range(4)], 0).astype(out.dtype)
        if step:
            put_gains(out, 32, sums)


def split_z_kernel(kept, second, gains, one, two, three, own, own_gains, *rest):
    outs, total = rest[:3], rest[3]
    near, far = lax.rem(lax.axis_index("lon") // 2, 2), lax.axis_index("lat")
    sums, terms = gains[...], kept[...]
    for part in (one, two, three):
        sums = sums + taken_gains(part, 32)
        terms = terms + part[0:32].astype(F32)
    own_gains[...] = sums
    total[0] = terms.reshape(2, 2, 8, WIDTH)
    total[1] = second[...].reshape(2, 2, 8, WIDTH)
    own[...] = jnp.concatenate([total[0, near, far], total[1, near, far]], 0)
    for step, out in enumerate(outs):
        near_at = near if step == 1 else 1 - near
        far_at = far if step == 0 else 1 - far
        rows = jnp.concatenate([total[0, near_at, far_at], total[1, near_at, far_at]], 0)
        out[0:16] = rows.astype(BF16)
        put_gains(out, 16, sums)


def final_kernel(kept, gains, one, two, three, rows, gain_rows):
    terms, sums = kept[...], gains[...]
    for part in (one, two, three):
        terms = terms + part[0:16].astype(F32)
        sums = sums + taken_gains(part, 16)
    rows[0] = terms[0:8]
    rows[1] = terms[8:16]
    place = (lax.axis_index("lon") * 2 + lax.axis_index("lat")) * 4 + lax.axis_index("dp")
    padded = jnp.concatenate([sums, jnp.zeros((6, WIDTH), F32)], 0)
    gain_rows[...] = pltpu.roll(padded, lax.rem(WIDTH - 8 * place, WIDTH), 1)[0:2, 0:8]


def over_lat(value):
    return lax.ppermute(value, "lat", [(0, 1), (1, 0)])


def over_lon(value, step):
    return lax.ppermute(value, "lon", [(i, (i + step) % 16) for i in range(16)])


def over_both(value, step):
    pairs = [(i * 2 + j, (i + step) % 16 * 2 + 1 - j) for i in range(16) for j in range(2)]
    return lax.ppermute(value, ("lon", "lat"), pairs)


def exchanged(lat, diag, lon, step):
    return over_lat(lat), over_both(diag, step), over_lon(lon, step)


def to_core(value):
    return lax.ppermute(value, "lon", [(i, i ^ 1) for i in range(16)])


def along_x(value, step):
    return lax.ppermute(value, "dp", [(i, (i + step) % 4) for i in range(4)])


def along_y(value, step):
    return lax.ppermute(value, "lon", [(i, (i + 4 * step) % 16) for i in range(16)])


def along_z(value, step):
    near, far = step % 2, step // 2
    pairs = [
        (i * 2 + j, (i ^ (2 * near)) * 2 + (j ^ far)) for i in range(16) for j in range(2)
    ]
    return lax.ppermute(value, ("lon", "lat"), pairs)


EDGE_OUTS = [((LAT, WIDTH), BF16), ((DIAG, WIDTH), BF16), ((LON, WIDTH), BF16)]
HALF_OUTS = [((PAIRS, 64, WIDTH), F32), ((PAIRS, 64, WIDTH), BF16)]
FLAT_OUT = ((TOKENS, WIDTH), BF16)
X_OUTS = [((8, 16, WIDTH), F32)] + [((8, 16, WIDTH), BF16)] * 3
GAINS = ((2, WIDTH), F32)
Y_OUTS = [((128, WIDTH), F32)] + [((128, WIDTH), BF16)] * 3
OWN = ((32, WIDTH), F32)
MIDDLE_OUTS = [((40, WIDTH), BF16)] * 3
Z_OUTS = [((16, WIDTH), F32), GAINS] + [((24, WIDTH), BF16)] * 3


def split_x(kept, sent):
    return call(
        split_x_kernel, X_OUTS, [pltpu.VMEM((8, 8, 8, WIDTH), F32)], (kept, to_core(sent)), micros=1
    )


def per_device(inputs, cotangent, qkv_weight, out_weight, norm_gain, position_bias, region_ids):
    flat = pltpu.VMEM((TOKENS + 8, WIDTH), F32)
    square = pltpu.VMEM((TOKENS, WIDTH), F32)
    tokens = pltpu.VMEM((TOKENS, WIDTH), BF16)
    grid = pltpu.VMEM((1, ROWS, COLS, WIDTH), BF16)
    sender = pltpu.VMEM((EDGES_PADDED, TOKENS), BF16)
    proj_in = pltpu.VMEM((WIDTH, 3 * WIDTH), BF16)
    proj_out = pltpu.VMEM((WIDTH, WIDTH), BF16)
    bias = pltpu.VMEM((HEADS, AREA, AREA), F32)
    wide = pltpu.VMEM((TOKENS, 3 * WIDTH), BF16)
    dma = pltpu.SemaphoreType.DMA
    cot, *cot_edges = call(
        cotangent_kernel,
        [FLAT_OUT] + EDGE_OUTS,
        [flat, grid, sender, dma((2,))],
        (cotangent, sender_table(SEND_OF_GRID)),
        hbm=(0, 1),
        micros=2,
    )
    cot_edges = exchanged(*cot_edges, -1)
    first_out, lat, diag, lon, attended, standard, inv_std, *saved = call(
        first_forward_kernel,
        [FLAT_OUT] + EDGE_OUTS
        + [FLAT_OUT, ((TOKENS, WIDTH), F32), ((TOKENS, 128), F32)]
        + [((TOKENS, 3 * 512), BF16)] * 2
        + [((WINDOWS, 2 * QUAD, AREA, AREA), BF16)] * 2,
        [
            flat, tokens, grid, sender, proj_in, proj_out, pltpu.VMEM((2, WIDTH), F32), bias,
            dma((6,)),
        ],
        (
            inputs, sender_table(SEND_OF_WIN), qkv_weight, out_weight, norm_gain,
            position_bias,
        ),
        hbm=range(6),
        after=(cot,),
        micros=12,
    )
    allowed, bias_second, diag, lon = call(
        mask_kernel,
        [((WINDOWS, AREA, AREA), F32), ((HEADS, AREA, AREA), F32)] + EDGE_OUTS[1:],
        [bias, dma],
        (region_ids, diag, lon, position_bias),
        hbm=(3,),
        after=cot_edges,
        micros=2,
    )
    edges = exchanged(lat, diag, lon, -1)
    grad_second, d_att = call(
        second_grad_kernel,
        [FLAT_OUT, FLAT_OUT],
        [proj_out, dma],
        (cot, *cot_edges, table(LOCAL_OF_GRID), *edge_tables(AHEAD_EDGE, 1), out_weight),
        hbm=(8,),
        after=(allowed,),
        micros=3,
    )
    back, lat, diag, lon, *halves, gain_second = call(
        second_kernel,
        [FLAT_OUT] + EDGE_OUTS + HALF_OUTS + [((1, WIDTH), F32)],
        [tokens, wide, square, tokens, proj_in, dma] + [pltpu.VMEM((TOKENS, 768), BF16)] * 4,
        (
            first_out, *edges, grad_second, d_att, table(LOCAL_OF_WIN),
            *edge_tables(AHEAD_EDGE, 1), sender_table(AHEAD_EDGE.T), qkv_weight, norm_gain,
            bias_second, allowed,
        ),
        hbm=(11,),
        micros=19,
    )
    edges = exchanged(lat, diag, lon, 1)
    own_second, *outs_second = split_x(*halves)
    shares_second = [along_x(out, step + 1) for step, out in enumerate(outs_second)]
    grad, *halves = call(
        first_grad_kernel,
        [FLAT_OUT] + HALF_OUTS,
        [],
        (back, *edges, table(LOCAL_OF_WIN.T), *edge_tables(SEND_OF_WIN.T, 1), attended),
        after=(*outs_second, shares_second[0], shares_second[2]),
        micros=3,
    )

    half = pltpu.VMEM((TOKENS, 512), BF16)
    (part_a,) = call(
        first_half_kernel,
        [((TOKENS, 3 * 512), BF16)],
        [half],
        (grad, saved[0], saved[2], out_weight),
        micros=4,
    )
    own_first, *outs_first = call(
        split_y_kernel, Y_OUTS, [], (halves[0], to_core(halves[1])), micros=1
    )
    shares_first = [along_y(out, step + 1) for step, out in enumerate(outs_first)]
    d_norm, gains = call(
        second_half_kernel,
        [((TOKENS, WIDTH), F32), GAINS],
        [half, wide, proj_in, dma],
        (part_a, grad, saved[1], saved[3], out_weight, standard, gain_second, qkv_weight),
        hbm=(7,),
        after=(*outs_first, shares_second[1]),
        micros=8,
    )
    own_second, own_gains, *outs = call(
        middle_y_kernel,
        [OWN, GAINS] + MIDDLE_OUTS,
        [pltpu.VMEM((4, 32, WIDTH), F32)],
        (own_second, *shares_second, gains, to_core(gains)),
        after=(shares_first[0],),
        micros=0.05,
    )
    shares = [along_y(out, step + 1) for step, out in enumerate(outs)]
    own_first, own_second, own_gains, *outs = call(
        middle_x_kernel,
        [OWN, OWN, GAINS] + MIDDLE_OUTS,
        [pltpu.VMEM((4, 4, 8, WIDTH), F32)],
        (own_first, *shares_first, own_second, own_gains, *shares),
        micros=0.05,
    )
    shares = [along_x(out, step + 1) for step, out in enumerate(outs)]
    own, own_gains, *outs = call(
        split_z_kernel,
        Z_OUTS,
        [pltpu.VMEM((2, 2, 2, 8, WIDTH), F32)],
        (own_first, own_second, own_gains, *shares),
        micros=0.05,
    )
    result, done = call(
        input_grad_kernel,
        [((1, ROWS, COLS, WIDTH), BF16), ((8, 128), F32)],
        [flat],
        (d_norm, grad, standard, inv_std, norm_gain),
        after=outs,
        micros=1,
    )
    shares = [along_z(out, step + 1) for step, out in enumerate(outs)]
    rows, gain_rows = call(
        final_kernel, [((2, 8, WIDTH), F32), ((2, 8), F32)], [], (own, own_gains, *shares),
        after=(done,), micros=1,
    )
    return result, rows, gain_rows


def solution(mesh):
    in_specs = (
        P("dp", "lat", "lon", None),
        P("dp", "lat", "lon", None),
        P(),
        P(),
        P(),
        P(),
        P("lat", "lon"),
    )
    out_specs = (
        P("dp", "lat", "lon", None),
        P(None, ("lon", "lat", "dp"), None),
        P(None, ("lon", "lat", "dp")),
    )
    return jax.shard_map(
        per_device, mesh=mesh, in_specs=in_specs, out_specs=out_specs, check_vma=False
    )
```
